256 devices in a mesh: cube: 64 (over x, z, core), blk: 4 (over y).
Axes of the slice: x: 4, y: 4, z: 8, core: 2. Of those that a mesh axis runs over, the one named last changes fastest.
Arguments:
- front_entries: float32 [8192, 8192], P('cube', 'blk'), may hold values from -6 to 6
- child_blocks: float32 [8192, 4096], P('cube', 'blk'), may hold values from -6 to 6
- child_map: int32 [2, 4096], replicated, may hold values from 0 to 8191, as said below
- pivot_inverse: float32 [2, 256, 256], replicated
- rhs_index: int32 [65536], P('cube'), may hold values from 0 to 8191, as said below
- rhs_values: float32 [64, 65536], P('blk', 'cube'), may hold values from -6 to 6
Outputs:
- front: float32 [8192, 8192], P('cube', 'blk')
- solved: float32 [64, 8192], P('blk', 'cube')
The draws below stay inside these ranges and needn't reach their ends.
Inputs may be any that keep to these rules, and one draw needn't show every extreme that they name: Each row of child_map increases. For block m of 128 contribution indices (m * 128 to m * 128 + 127), the first 64 map into front indices 2 m * 128 to 2 m * 128 + 127 and the last 64 into the next 128 front indices. Among one device's 1024 entries (an aligned block of rhs_index) at most 32 name rows of one block of 128 front rows; in every draw one such block of rows is named exactly 32 times by every device. Rows may repeat; repeated entries add.
All inputs are finite; a program needn't handle non-finite values.
Results may differ from the reference program's by a relative error of at most 0.0001.
Values sent between devices are 32-bit elements; how exact they have to be, the bound alone decides.
No kernel may reach another device: no remote copies, remote signals or barrier semaphores. Data moves between devices by JAX's collectives and lax.ppermute only.
A program may use at most 64 MiB of HBM per device.

```python
import math
import jax
import jax.numpy as jnp
from jax import lax

FRONT_ORDER = 8192
PANEL_WIDTH = 256
PANELS = 2
EXCITES = 64
ENTRIES = 1024
ROWS_DEV = 128
CHILD_ORDER = 4096
N_CUBE = 64


def draw_pivot_inverse(key, part):
    key = jax.random.fold_in(key, 5)
    shape = (PANELS, PANEL_WIDTH, PANEL_WIDTH)
    spread_terms = jax.random.normal(key, shape, jnp.float32)
    identity = jnp.eye(PANEL_WIDTH, dtype=jnp.float32)
    return (2.0 * identity + spread_terms / math.sqrt(PANEL_WIDTH)) / 64.0


def draw_child_map(key, part):
    key = jax.random.fold_in(key, 7)
    rows_dev = FRONT_ORDER // N_CUBE
    half_rows = rows_dev // 2
    pairs = N_CUBE // 2
    positions = jnp.arange(rows_dev, dtype=jnp.int32)

    def choose(child, pair_index, side):
        sub_key = jax.random.fold_in(jax.random.fold_in(jax.random.fold_in(key, child), pair_index), side)
        scores = jax.random.permutation(sub_key, rows_dev).astype(jnp.int32)
        forced = (pair_index == 0) & (side == 0) & (positions == 0) | (pair_index == pairs - 1) & (side == 1) & (positions == rows_dev - 1)
        scores = jnp.where(forced, -1, scores)
        chosen = jnp.sort(jnp.argsort(scores, stable=True)[:half_rows].astype(jnp.int32))
        return (pair_index * 2 * rows_dev + side * rows_dev + chosen).astype(jnp.int32)
    children = jnp.arange(2, dtype=jnp.int32)
    pair_ids = jnp.arange(pairs, dtype=jnp.int32)
    sides = jnp.arange(2, dtype=jnp.int32)
    picked = jax.vmap(lambda child: jax.vmap(lambda pair_index: jax.vmap(lambda side: choose(child, pair_index, side))(sides))(pair_ids))(children)
    return picked.reshape(2, CHILD_ORDER)


def draw_rhs_index(key, part):
    key = jax.random.fold_in(key, 11)
    rows_dev = FRONT_ORDER // N_CUBE
    capacity = 2 * ENTRIES // N_CUBE
    slot_total = N_CUBE * capacity
    busiest = jax.random.randint(jax.random.fold_in(key, 1), (), 0, N_CUBE)
    slot_holder = jnp.arange(slot_total, dtype=jnp.int32) // capacity

    def one_device(device):
        dev_key = jax.random.fold_in(jax.random.fold_in(key, 2), device)
        scores = jax.random.permutation(jax.random.fold_in(dev_key, 1), slot_total).astype(jnp.int32)
        scores = jnp.where(slot_holder == busiest, scores - slot_total, scores)
        chosen = jnp.argsort(scores, stable=True)[:ENTRIES].astype(jnp.int32)
        chosen = chosen[jax.random.permutation(jax.random.fold_in(dev_key, 2), ENTRIES)]
        offsets = jax.random.randint(jax.random.fold_in(dev_key, 3), (ENTRIES,), 0, rows_dev)
        return (chosen // capacity * rows_dev + offsets).astype(jnp.int32)
    return jax.vmap(one_device)(jnp.arange(N_CUBE, dtype=jnp.int32)).reshape(-1)


def steps_of(key, shape, shards, least, largest):
    def one(axis_at, shards_of):
        draws = jax.random.uniform(jax.random.fold_in(jax.random.fold_in(key, 6), axis_at), (shards_of,), jnp.float32, least / len(shards), largest / len(shards))
        return jnp.repeat(jnp.exp(draws), shape[axis_at] // shards_of).reshape((-1,) + (1,) * (len(shape) - axis_at - 1))

    gain = one(*shards[0])
    for cut in shards[1:]:
        gain = gain * one(*cut)
    return gain


def centred(own_key, extent, deviation, limit, shards=(), kind=jnp.bfloat16):
    level = steps_of(own_key, extent, shards, -0.22, 0.18) if shards else 1.0
    values = jax.random.normal(own_key, extent, jnp.float32) * deviation * level
    return jnp.minimum(jnp.maximum(values, -limit), limit).astype(kind)


def setup_inputs(seed: int = 0) -> dict:
    key_list = jax.random.split(jax.random.key(seed), 7)
    return {
        "front_entries": centred(key_list[0], (FRONT_ORDER, FRONT_ORDER), 1.0, 6.0, ((0, 64), (1, 4)), jnp.float32),
        "child_blocks": centred(key_list[1], (FRONT_ORDER, CHILD_ORDER), 1.0, 6.0, ((0, 64), (1, 4)), jnp.float32),
        "child_map": draw_child_map(jax.random.fold_in(key_list[6], 71), 0),
        "pivot_inverse": draw_pivot_inverse(jax.random.fold_in(key_list[6], 71), 0),
        "rhs_index": draw_rhs_index(jax.random.fold_in(key_list[6], 71), 0),
        "rhs_values": centred(key_list[5], (EXCITES, N_CUBE * ENTRIES), 1.0, 6.0, ((0, 4), (1, 64)), jnp.float32),
    }


def exact_dot(left, right):
    return jnp.dot(left, right, precision=lax.Precision.HIGHEST, preferred_element_type=jnp.float32)


def reference(front_entries, child_blocks, child_map, pivot_inverse, rhs_index, rhs_values):
    stacked = child_blocks.reshape(N_CUBE // 2, 2, ROWS_DEV, CHILD_ORDER)
    matrix = front_entries
    for child in range(2):
        contrib = stacked[:, child].reshape(CHILD_ORDER, CHILD_ORDER)
        targets = child_map[child]
        matrix = matrix.at[targets[:, None], targets[None, :]].add(contrib)
    forcing = jnp.zeros((EXCITES, FRONT_ORDER), jnp.float32).at[:, rhs_index].add(rhs_values)
    for which_panel in range(PANELS):
        start_col = which_panel * PANEL_WIDTH
        end_col = start_col + PANEL_WIDTH
        weights = pivot_inverse[which_panel]
        multipliers = exact_dot(matrix[end_col:, start_col:end_col], weights)
        trailing = matrix[end_col:, end_col:] - exact_dot(multipliers, matrix[start_col:end_col, end_col:])
        matrix = matrix.at[end_col:, end_col:].set(trailing)
        matrix = matrix.at[end_col:, start_col:end_col].set(multipliers)
        upper_rhs = forcing[:, start_col:end_col]
        reduced = forcing[:, end_col:] - exact_dot(upper_rhs, multipliers.T)
        forcing = forcing.at[:, end_col:].set(reduced)
        forcing = forcing.at[:, start_col:end_col].set(exact_dot(upper_rhs, weights.T))
    return matrix, forcing
```

```python
import jax
import jax.numpy as jnp
from jax import lax
from jax.sharding import PartitionSpec as P

NX, NZ, NC, NY = 4, 8, 2, 4
ROWS = 128
WIDTH = 256
CHUNKS = ((0, 512), (512, 2048))
HIGH = lax.Precision.HIGHEST


def dot(left, right):
    return jnp.dot(left, right, precision=HIGH, preferred_element_type=jnp.float32)


def cube_send(value, target):
    pairs = []
    for x in range(NX):
        for z in range(NZ):
            for c in range(NC):
                to = target(x, z, c)
                if to is not None:
                    tx, tz, tc = to
                    pairs.append(
                        ((x * NZ + z) * NC + c, ((tx % NX) * NZ + tz % NZ) * NC + tc % NC)
                    )
    return lax.ppermute(value, "cube", pairs)


def swap_core(value):
    return cube_send(value, lambda x, z, c: (x, z, 1 - c))


def place():
    rank = lax.axis_index("cube")
    return rank, rank // (NZ * NC), rank // NC % NZ, rank % NC


def spread_columns(rows, targets, col_base, block):
    count = rows.shape[0]
    blocks = targets.shape[0] // block
    local = (targets - col_base).reshape(blocks, block) - 2 * block * jnp.arange(
        blocks, dtype=jnp.int32
    )[:, None]
    table = (local[:, :, None] == jnp.arange(2 * block, dtype=jnp.int32)[None, None, :]).astype(
        jnp.float32
    )
    shaped = rows.reshape(count, blocks, block)
    placed = jnp.einsum(
        "rbt,btu->rbu", shaped, table, precision=HIGH, preferred_element_type=jnp.float32
    )
    return placed.reshape(count, blocks * 2 * block)


def assemble(front_entries, child_blocks, child_map):
    rows_dev, front_cols = front_entries.shape
    child_cols = child_blocks.shape[1]
    half_rows = rows_dev // 2
    cube_rank = lax.axis_index("cube")
    blk_rank = lax.axis_index("blk")
    parity = cube_rank % 2
    lower_half = child_blocks[:half_rows]
    upper_half = child_blocks[half_rows:]
    kept_rows = jnp.where(parity == 0, lower_half, upper_half)
    sent_rows = jnp.where(parity == 0, upper_half, lower_half)
    arrived = swap_core(sent_rows)
    child_start = cube_rank // 2 * rows_dev + parity * half_rows
    col_first = blk_rank * child_cols
    own_rows = lax.dynamic_slice(child_map, (parity, child_start), (1, half_rows))[0]
    other_rows = lax.dynamic_slice(child_map, (1 - parity, child_start), (1, half_rows))[0]
    own_cols = lax.dynamic_slice(child_map, (parity, col_first), (1, child_cols))[0]
    other_cols = lax.dynamic_slice(child_map, (1 - parity, col_first), (1, child_cols))[0]
    row_base = cube_rank * rows_dev
    col_base = blk_rank * front_cols
    placed = jnp.concatenate(
        [
            spread_columns(kept_rows, own_cols, col_base, rows_dev),
            spread_columns(arrived, other_cols, col_base, rows_dev),
        ],
        axis=0,
    )
    targets = jnp.concatenate([own_rows, other_rows]) - row_base
    row_table = (jnp.arange(rows_dev, dtype=jnp.int32)[:, None] == targets[None, :]).astype(
        jnp.float32
    )
    return front_entries + dot(row_table, placed)


def reduce_forcing(rhs_index, rhs_values):
    _, x, z, c = place()
    excites = rhs_values.shape[0]
    dense = jnp.zeros((excites, ROWS * NX * NZ * NC), jnp.float32).at[:, rhs_index].add(rhs_values)
    blocks = dense.reshape(excites, NX, NZ, NC, ROWS).transpose(3, 1, 2, 0, 4)
    pivots = dense[:, : 2 * WIDTH].reshape(excites, 2, NC, NX, 32).transpose(2, 3, 0, 1, 4)
    pivots = jnp.pad(pivots.reshape(NC, NX, 1, excites, 64), ((0, 0),) * 4 + ((0, 64),))
    full = jnp.concatenate([blocks, pivots], axis=2)
    kept = lax.dynamic_index_in_dim(full, c, 0, keepdims=False)
    sent = lax.dynamic_index_in_dim(full, 1 - c, 0, keepdims=False)
    full = kept + swap_core(sent)
    total = lax.dynamic_index_in_dim(full, x, 0, keepdims=False)
    for d in range(1, NX):
        piece = lax.dynamic_index_in_dim(full, (x + d) % NX, 0, keepdims=False)
        total = total + cube_send(piece, lambda i, j, k: (i + d, j, k))
    extra = total[NZ]

    def piece_for(at):
        return jnp.stack([lax.dynamic_index_in_dim(total, at, 0, keepdims=False), extra])

    last = piece_for(z)
    for d in range(1, NZ):
        last = last + cube_send(piece_for((z + d) % NZ), lambda i, j, k: (i, j + d, k))
    return last[0], last[1][:, :64]


def scatter_rows(block):
    _, x, z, c = place()
    quarter = jnp.where(x == 0, block[:32], 0.0)
    for d in range(1, NX):
        quarter = quarter + cube_send(
            block[32 * d : 32 * d + 32],
            lambda i, j, k: (d, j, k) if i == 0 and j < 2 else None,
        )
    share = jnp.where(z < 2, quarter[:8], 0.0)
    for d in range(1, NZ // 2):
        share = share + cube_send(
            quarter[8 * d : 8 * d + 8],
            lambda i, j, k: (i, (-d if j == 0 else 1 + d), k) if j < 2 else None,
        )
    return share


def gather_z(share):
    parts = [share]
    for d in range(1, NZ):
        parts.append(cube_send(share, lambda i, j, k: (i, j + d, k)))
    return jnp.concatenate(parts, axis=0)


def gather_x(block):
    parts = [block]
    for d in range(1, NX):
        parts.append(cube_send(block, lambda i, j, k: (i + d, j, k)))
    own = jnp.concatenate(parts, axis=0)
    return jnp.concatenate([own, swap_core(own)], axis=0)


def gathered_ids():
    _, x, z, c = place()
    at = jnp.arange(2 * WIDTH, dtype=jnp.int32)
    core = (c + at // WIDTH) % NC
    sx = (x - at // 64 % NX) % NX
    sz = (z - at // 8 % NZ) % NZ
    lower = (sz == 0) | (sz > 4)
    pos = jnp.where(lower, (NZ - sz) % NZ, sz - 1)
    holder = jnp.where(lower, 0, 1)
    return (holder * NC + core) * ROWS + sx * 32 + pos * 8 + at % 8


def group_order(z):
    at = jnp.arange(64, dtype=jnp.int32)
    sz = (z - at // 8) % NZ
    lower = (sz == 0) | (sz > 4)
    pos = jnp.where(lower, (NZ - sz) % NZ, sz - 1)
    return jnp.where(lower, 0, 1) * 32 + pos * 8 + at % 8


def one_hot_to(ids, size):
    return (jnp.arange(size, dtype=jnp.int32)[:, None] == ids[None, :]).astype(jnp.float32)


def from_first(value):
    got = [lax.ppermute(value, "blk", [(i, (i + d) % NY) for i in range(NY)]) for d in range(1, NY)]
    rank = lax.axis_index("blk")
    out = value
    for d in range(1, NY):
        out = jnp.where(rank == d, got[d - 1], out)
    return out


def shards(front_entries, child_blocks, child_map, pivot_inverse, rhs_index, rhs_values):
    rank, x, z, c = place()
    blk = lax.axis_index("blk")
    first, second = pivot_inverse[0], pivot_inverse[1]
    holder_one, holder_two = rank < 2, (rank >= 2) & (rank < 4)
    matrix = assemble(front_entries, child_blocks, child_map)
    shares = [scatter_rows(matrix[:, lo:hi]) for lo, hi in CHUNKS]
    forcing, pivots = reduce_forcing(rhs_index, rhs_values)
    ids = gathered_ids()
    table = one_hot_to(ids, 2 * WIDTH)

    head = gather_x(gather_z(shares[0]))
    left, right = matrix[:, :WIDTH], matrix[:, WIDTH : 2 * WIDTH]
    l1 = dot(left, first)
    turned = dot(dot(l1, table[:WIDTH]), head[:, WIDTH : 2 * WIDTH])
    reduced = right - turned
    l2 = dot(reduced, second)
    start = rank % 2 * ROWS
    pick_one = lax.dynamic_slice(first, (start, 0), (ROWS, WIDTH))
    pick_two = lax.dynamic_slice(second, (start, 0), (ROWS, WIDTH))
    lead = jnp.where(holder_two, pick_two, l2)
    back = dot(dot(dot(lead, table[WIDTH:]), head[:, :WIDTH]), first)
    panel = jnp.concatenate(
        [
            jnp.where(holder_one, left, l1),
            jnp.where(holder_one, right, jnp.where(holder_two, reduced, l2)),
        ],
        axis=1,
    )
    factors = jnp.where(
        holder_two,
        jnp.concatenate([l1, back], axis=1),
        jnp.concatenate([l1 - back, l2], axis=1),
    )
    factors = from_first(factors)
    zeros = jnp.zeros((ROWS, WIDTH), jnp.float32)
    front_left = jnp.where(
        holder_one,
        0.0,
        jnp.where(holder_two, jnp.concatenate([factors[:, :WIDTH], zeros], axis=1), factors),
    )
    forcing_left = jnp.where(
        holder_one,
        jnp.concatenate([-pick_one, zeros], axis=1),
        jnp.where(
            holder_two, jnp.concatenate([factors[:, WIDTH:], -pick_two], axis=1), factors
        ),
    )
    turned_left = dot(jnp.concatenate([front_left, forcing_left], axis=0), table)

    block = gather_z(shares[1])
    piece = dot(pivots, one_hot_to(group_order(z), 64)).T
    piece = jnp.pad(piece, ((0, 0), (0, 128 - piece.shape[1])))
    tail = gather_x(jnp.concatenate([block, piece], axis=1))
    width = CHUNKS[1][1] - CHUNKS[1][0]
    body = matrix[:, 512:] - dot(turned_left[:ROWS], tail[:, :width])
    head_out = matrix[:, :512] - dot(turned_left[:ROWS], head)
    head_out = jnp.where(blk == 0, panel, head_out)
    front = jnp.concatenate([head_out, body], axis=1)
    excites = forcing.shape[0]
    change = dot(turned_left[ROWS:], tail[:, width : width + excites]).T
    solved = jnp.where(rank < 4, 0.0, forcing) - change
    return front, solved


def solution(mesh):
    in_specs = (P("cube", "blk"), P("cube", "blk"), P(), P(), P("cube"), P("blk", "cube"))
    out_specs = (P("cube", "blk"), P("blk", "cube"))
    return jax.shard_map(shards, mesh=mesh, in_specs=in_specs, out_specs=out_specs, check_vma=False)
```

```python
import jax
import jax.numpy as jnp
from jax import lax
from jax.sharding import PartitionSpec as P

NX, NZ, NC, NY = 4, 8, 2, 4
ROWS = 128
WIDTH = 256
CHUNKS = ((0, 512), (512, 2048))
HIGH = lax.Precision.HIGHEST


def dot(left, right):
    return jnp.dot(left, right, precision=HIGH, preferred_element_type=jnp.float32)


def cube_send(value, target):
    pairs = []
    for x in range(NX):
        for z in range(NZ):
            for c in range(NC):
                to = target(x, z, c)
                if to is not None:
                    tx, tz, tc = to
                    pairs.append(
                        ((x * NZ + z) * NC + c, ((tx % NX) * NZ + tz % NZ) * NC + tc % NC)
                    )
    return lax.ppermute(value, "cube", pairs)


def swap_core(value):
    return cube_send(value, lambda x, z, c: (x, z, 1 - c))


def place():
    rank = lax.axis_index("cube")
    return rank, rank // (NZ * NC), rank // NC % NZ, rank % NC


def spread_columns(rows, targets, col_base, block):
    count = rows.shape[0]
    blocks = targets.shape[0] // block
    local = (targets - col_base).reshape(blocks, block) - 2 * block * jnp.arange(
        blocks, dtype=jnp.int32
    )[:, None]
    table = (local[:, :, None] == jnp.arange(2 * block, dtype=jnp.int32)[None, None, :]).astype(
        jnp.float32
    )
    shaped = rows.reshape(count, blocks, block)
    placed = jnp.einsum(
        "rbt,btu->rbu", shaped, table, precision=HIGH, preferred_element_type=jnp.float32
    )
    return placed.reshape(count, blocks * 2 * block)


def assemble(front_entries, child_blocks, child_map):
    rows_dev, front_cols = front_entries.shape
    child_cols = child_blocks.shape[1]
    half_rows = rows_dev // 2
    cube_rank = lax.axis_index("cube")
    blk_rank = lax.axis_index("blk")
    parity = cube_rank % 2
    lower_half = child_blocks[:half_rows]
    upper_half = child_blocks[half_rows:]
    kept_rows = jnp.where(parity == 0, lower_half, upper_half)
    sent_rows = jnp.where(parity == 0, upper_half, lower_half)
    arrived = swap_core(sent_rows)
    child_start = cube_rank // 2 * rows_dev + parity * half_rows
    col_first = blk_rank * child_cols
    own_rows = lax.dynamic_slice(child_map, (parity, child_start), (1, half_rows))[0]
    other_rows = lax.dynamic_slice(child_map, (1 - parity, child_start), (1, half_rows))[0]
    own_cols = lax.dynamic_slice(child_map, (parity, col_first), (1, child_cols))[0]
    other_cols = lax.dynamic_slice(child_map, (1 - parity, col_first), (1, child_cols))[0]
    row_base = cube_rank * rows_dev
    col_base = blk_rank * front_cols
    placed = jnp.concatenate(
        [
            spread_columns(kept_rows, own_cols, col_base, rows_dev),
            spread_columns(arrived, other_cols, col_base, rows_dev),
        ],
        axis=0,
    )
    targets = jnp.concatenate([own_rows, other_rows]) - row_base
    row_table = (jnp.arange(rows_dev, dtype=jnp.int32)[:, None] == targets[None, :]).astype(
        jnp.float32
    )
    return front_entries + dot(row_table, placed)


def sign(core):
    return 1 - 2 * core


def take(array, at):
    return lax.dynamic_index_in_dim(array, at, 0, keepdims=False)


def reduce_forcing(rhs_index, rhs_values):
    _, x, z, c = place()
    s = sign(c)
    excites = rhs_values.shape[0]
    dense = jnp.zeros((excites, ROWS * NX * NZ * NC), jnp.float32).at[:, rhs_index].add(rhs_values)
    blocks = dense.reshape(excites, NX, NZ * NC, ROWS).transpose(1, 2, 0, 3)
    pivots = dense[:, : 2 * WIDTH].reshape(excites, 2, NC, NX, 32).transpose(3, 0, 2, 1, 4)
    full = jnp.concatenate([blocks, pivots.reshape(NX, 1, excites, ROWS)], axis=1)

    def half(at, core):
        block = take(full, at % NX)
        pairs = block[: NZ * NC].reshape(NZ, NC, excites, ROWS)
        return jnp.concatenate([jnp.where(core == 0, pairs[:, 0], pairs[:, 1]), block[NZ * NC :]])

    def parts(sgn, core):
        return jnp.concatenate(
            [take(full, (x + sgn + NX) % NX), half(x + 2, core), half(x, core)]
        )

    summed = parts(s, c) + swap_core(parts(-s, 1 - c))
    count = NZ * NC + 1
    lone = jnp.where((jnp.arange(NZ + 1) < NZ)[:, None, None] | (c == 0), 1.0, 0.0)
    side = cube_send(summed[:count], lambda i, j, k: (i + sign(k), j, k))
    across = cube_send(summed[count : count + NZ + 1] * lone, lambda i, j, k: (i + 2, j, k))
    own = summed[count + NZ + 1 :] * lone + across
    is_c = (jnp.arange(NC) == c)[None, :, None, None]
    pairs = side[: NZ * NC].reshape(NZ, NC, excites, ROWS) + jnp.where(is_c, own[:NZ, None], 0.0)
    pivot = side[NZ * NC :] + own[NZ:]

    def rows(sgn, core):
        near = [take(pairs, (z + n * sgn + NZ) % NZ) for n in (1, 2, 3)]
        far = [take(take(pairs, at % NZ), core)[None] for at in (z + 4, z)]
        return jnp.concatenate(near + far + [pivot])

    summed = rows(s, c) + swap_core(rows(-s, 1 - c))
    first = jnp.where(c == 0, summed[8:9], 0.0)
    got = [
        cube_send(
            jnp.concatenate([summed[2 * n - 2 : 2 * n], summed[8:9]]),
            lambda i, j, k: (i, j + n * sign(k), k),
        )
        for n in (1, 2, 3)
    ]
    far = cube_send(jnp.concatenate([summed[6:7], first]), lambda i, j, k: (i, j + 4, k))
    near = got[0] + got[1] + got[2]
    mine = take(near[:2], c) + far[0] + summed[7]
    partial = near[2] + far[1] + first[0]
    back = swap_core(jnp.stack([take(near[:2], 1 - c), partial]))
    return mine + back[0], partial + back[1]


def at_core(core, value):
    zero = jnp.zeros_like(value)
    return jnp.concatenate([jnp.where(core == 0, value, zero), jnp.where(core == 0, zero, value)])


def scatter_rows(block):
    _, x, z, c = place()
    low = c == 0
    got = swap_core(jnp.where(low, block[96:], block[32:64]))
    message = jnp.concatenate([jnp.where(low, block[32:64], block[96:]), got])
    side = cube_send(
        message, lambda i, j, k: (sign(k), j, k) if i == 0 and j < 2 else None
    )
    far = cube_send(block[64:96], lambda i, j, k: (2, j, k) if i == 0 and j < 2 else None)
    side = jnp.where(low, side, jnp.concatenate([side[32:], side[:32]]))
    mine = side + at_core(c, jnp.where(x == 0, block[:32], far))
    whole = mine + swap_core(mine)

    def piece(p):
        return jnp.concatenate([whole[8 * p : 8 * p + 8], whole[32 + 8 * p : 40 + 8 * p]])

    near = cube_send(
        jnp.where(low, piece(1), piece(2)),
        lambda i, j, k: (i, (-1 - k if j == 0 else 2 + k), k) if j < 2 else None,
    )
    far = cube_send(
        jnp.where(low, whole[24:32], whole[56:]),
        lambda i, j, k: (i, (-3 if j == 0 else 4), k) if j < 2 else None,
    )
    share = near + at_core(c, far) + jnp.where((z < 2) & low, piece(0), 0.0)
    return share + swap_core(share)


def gather_z(share):
    low = lax.axis_index("cube") % NC == 0
    own = jnp.where(low, share[:8], share[8:])
    parts = [own]
    for n in (1, 2, 3):
        parts.append(cube_send(share, lambda i, j, k: (i, j + n * sign(k), k)))
    parts.append(cube_send(own, lambda i, j, k: (i, j + 4, k)))
    return parts


def gather_x(mine, theirs):
    block = jnp.concatenate([mine, theirs])
    side = cube_send(block, lambda i, j, k: (i + sign(k), j, k))
    far = cube_send(mine, lambda i, j, k: (i + 2, j, k))
    return jnp.concatenate([block, side, far, swap_core(side), swap_core(far)])


def ids_8(x, z, c):
    x, z = x % NX, z % NZ
    lower = (z == 0) | (z > 4)
    pos = jnp.where(lower, (NZ - z) % NZ, z - 1)
    base = (jnp.where(lower, 0, NC) + c) * ROWS + x * 32 + pos * 8
    return base + jnp.arange(8, dtype=jnp.int32)


def ids_16(x, z):
    return jnp.concatenate([ids_8(x, z, 0), ids_8(x, z, 1)])


def ids_64(x, z, c):
    s = sign(c)
    parts = [ids_16(x, z - n * s + NZ) for n in (1, 2, 3)]
    return jnp.concatenate([ids_8(x, z, c)] + parts + [ids_8(x, z + 4, c)])


def ids_128(x, z, c):
    return jnp.concatenate([ids_64(x, z, c), ids_64(x, z, 1 - c)])


def gathered_ids():
    _, x, z, c = place()
    s = sign(c)
    return jnp.concatenate(
        [
            ids_128(x, z, c),
            ids_128(x - s + NX, z, c),
            ids_64(x + 2, z, c),
            ids_128(x + s + NX, z, 1 - c),
            ids_64(x + 2, z, 1 - c),
        ]
    )


def group_order():
    _, x, z, c = place()
    ids = ids_128(x, z, c)
    return ids // ROWS % NC * 64 + ids // WIDTH * 32 + ids % 32


def one_hot_to(ids, size):
    return (jnp.arange(size, dtype=jnp.int32)[:, None] == ids[None, :]).astype(jnp.float32)


def from_first(value):
    got = [lax.ppermute(value, "blk", [(i, (i + d) % NY) for i in range(NY)]) for d in range(1, NY)]
    rank = lax.axis_index("blk")
    out = value
    for d in range(1, NY):
        out = jnp.where(rank == d, got[d - 1], out)
    return out


def shards(front_entries, child_blocks, child_map, pivot_inverse, rhs_index, rhs_values):
    rank, x, z, c = place()
    blk = lax.axis_index("blk")
    first, second = pivot_inverse[0], pivot_inverse[1]
    holder_one, holder_two = rank < 2, (rank >= 2) & (rank < 4)
    matrix = assemble(front_entries, child_blocks, child_map)
    share = scatter_rows(matrix)
    rhs_values, matrix = lax.optimization_barrier((rhs_values, matrix))
    forcing, pivots = reduce_forcing(rhs_index, rhs_values)
    parts = gather_z(share)
    ids = gathered_ids()
    table = one_hot_to(ids, 2 * WIDTH)

    cut = CHUNKS[0][1]
    mine = jnp.concatenate([part[:, :cut] for part in parts])
    head = gather_x(mine, swap_core(mine))
    left, right = matrix[:, :WIDTH], matrix[:, WIDTH : 2 * WIDTH]
    l1 = dot(left, first)
    turned = dot(dot(l1, table[:WIDTH]), head[:, WIDTH : 2 * WIDTH])
    reduced = right - turned
    l2 = dot(reduced, second)
    start = rank % 2 * ROWS
    pick_one = lax.dynamic_slice(first, (start, 0), (ROWS, WIDTH))
    pick_two = lax.dynamic_slice(second, (start, 0), (ROWS, WIDTH))
    lead = jnp.where(holder_two, pick_two, l2)
    back = dot(dot(dot(lead, table[WIDTH:]), head[:, :WIDTH]), first)
    panel = jnp.concatenate(
        [
            jnp.where(holder_one, left, l1),
            jnp.where(holder_one, right, jnp.where(holder_two, reduced, l2)),
        ],
        axis=1,
    )
    factors = jnp.where(
        holder_two,
        jnp.concatenate([l1, back], axis=1),
        jnp.concatenate([l1 - back, l2], axis=1),
    )
    factors = from_first(factors)
    zeros = jnp.zeros((ROWS, WIDTH), jnp.float32)
    front_left = jnp.where(
        holder_one,
        0.0,
        jnp.where(holder_two, jnp.concatenate([factors[:, :WIDTH], zeros], axis=1), factors),
    )
    forcing_left = jnp.where(
        holder_one,
        jnp.concatenate([-pick_one, zeros], axis=1),
        jnp.where(
            holder_two, jnp.concatenate([factors[:, WIDTH:], -pick_two], axis=1), factors
        ),
    )
    turned_left = dot(jnp.concatenate([front_left, forcing_left], axis=0), table)

    mine = jnp.concatenate([part[:, cut:] for part in parts])
    theirs = swap_core(mine)
    piece = dot(one_hot_to(group_order(), ROWS).T, pivots.T)
    piece = jnp.pad(piece, ((0, 0), (0, 128 - piece.shape[1])))
    tail = gather_x(
        jnp.concatenate([mine, piece[:64]], axis=1),
        jnp.concatenate([theirs, piece[64:]], axis=1),
    )
    width = CHUNKS[1][1] - CHUNKS[1][0]
    body = matrix[:, 512:] - dot(turned_left[:ROWS], tail[:, :width])
    head_out = matrix[:, :512] - dot(turned_left[:ROWS], head)
    head_out = jnp.where(blk == 0, panel, head_out)
    front = jnp.concatenate([head_out, body], axis=1)
    excites = forcing.shape[0]
    change = dot(turned_left[ROWS:], tail[:, width : width + excites]).T
    solved = jnp.where(rank < 4, 0.0, forcing) - change
    return front, solved


def solution(mesh):
    in_specs = (P("cube", "blk"), P("cube", "blk"), P(), P(), P("cube"), P("blk", "cube"))
    out_specs = (P("cube", "blk"), P("blk", "cube"))
    return jax.shard_map(shards, mesh=mesh, in_specs=in_specs, out_specs=out_specs, check_vma=False)
```

```python
import jax
import jax.numpy as jnp
from jax import lax
from jax.experimental import pallas as pl
from jax.experimental.pallas import tpu as pltpu
from jax.sharding import PartitionSpec as P

NX, NZ, NC, NY = 4, 8, 2, 4
ROWS = 128
WIDTH = 256
CHUNKS = ((0, 512), (512, 2048))
HIGH = lax.Precision.HIGHEST


def dot(left, right):
    return jnp.dot(left, right, precision=HIGH, preferred_element_type=jnp.float32)


def after(value, *others):
    return lax.optimization_barrier((value, others))[0]


def cube_send(value, target):
    pairs = []
    for x in range(NX):
        for z in range(NZ):
            for c in range(NC):
                to = target(x, z, c)
                if to is not None:
                    tx, tz, tc = to
                    pairs.append(
                        ((x * NZ + z) * NC + c, ((tx % NX) * NZ + tz % NZ) * NC + tc % NC)
                    )
    return lax.ppermute(value, "cube", pairs)


def swap_core(value):
    return cube_send(value, lambda x, z, c: (x, z, 1 - c))


def place():
    rank = lax.axis_index("cube")
    return rank, rank >> 4, rank >> 1 & 7, rank & 1


def spread_columns(rows, targets, col_base, block):
    count = rows.shape[0]
    blocks = targets.shape[0] // block
    local = (targets - col_base).reshape(blocks, block) - 2 * block * jnp.arange(
        blocks, dtype=jnp.int32
    )[:, None]
    table = (local[:, :, None] == jnp.arange(2 * block, dtype=jnp.int32)[None, None, :]).astype(
        jnp.float32
    )
    shaped = rows.reshape(count, blocks, block)
    placed = jnp.einsum(
        "rbt,btu->rbu", shaped, table, precision=HIGH, preferred_element_type=jnp.float32
    )
    return placed.reshape(count, blocks * 2 * block)


def assemble(front_entries, child_blocks, child_map):
    rows_dev, front_cols = front_entries.shape
    child_cols = child_blocks.shape[1]
    half_rows = rows_dev // 2
    cube_rank = lax.axis_index("cube")
    blk_rank = lax.axis_index("blk")
    parity = cube_rank % 2
    lower_half = child_blocks[:half_rows]
    upper_half = child_blocks[half_rows:]
    kept_rows = jnp.where(parity == 0, lower_half, upper_half)
    sent_rows = jnp.where(parity == 0, upper_half, lower_half)
    arrived = swap_core(sent_rows)
    child_start = cube_rank // 2 * rows_dev + parity * half_rows
    col_first = blk_rank * child_cols
    own_rows = lax.dynamic_slice(child_map, (parity, child_start), (1, half_rows))[0]
    other_rows = lax.dynamic_slice(child_map, (1 - parity, child_start), (1, half_rows))[0]
    own_cols = lax.dynamic_slice(child_map, (parity, col_first), (1, child_cols))[0]
    other_cols = lax.dynamic_slice(child_map, (1 - parity, col_first), (1, child_cols))[0]
    row_base = cube_rank * rows_dev
    col_base = blk_rank * front_cols
    placed = jnp.concatenate(
        [
            spread_columns(kept_rows, own_cols, col_base, rows_dev),
            spread_columns(arrived, other_cols, col_base, rows_dev),
        ],
        axis=0,
    )
    targets = jnp.concatenate([own_rows, other_rows]) - row_base
    row_table = (jnp.arange(rows_dev, dtype=jnp.int32)[:, None] == targets[None, :]).astype(
        jnp.float32
    )
    return front_entries + dot(row_table, placed)


def sign(core):
    return 1 - 2 * core


def take(array, at):
    return lax.dynamic_index_in_dim(array, at, 0, keepdims=False)


def dense_kernel(index_ref, values_ref, out_ref):
    index = index_ref[...]
    values = values_ref[...]
    excites, entries = values.shape
    high = values.astype(jnp.bfloat16)
    rest = values - high.astype(jnp.float32)
    middle = rest.astype(jnp.bfloat16)
    low = (rest - middle.astype(jnp.float32)).astype(jnp.bfloat16)
    split = jnp.concatenate([high, middle, low], axis=0)
    chip = index // (NC * ROWS)

    def table(at, size):
        rows = lax.broadcasted_iota(jnp.int32, (size, entries), 0)
        return jnp.where(rows == at, 1.0, 0.0).astype(jnp.bfloat16)

    def summed(masks, place_table):
        rows = [split * mask.astype(jnp.bfloat16) for mask in masks]
        placed = lax.dot_general(
            jnp.concatenate(rows, axis=0),
            place_table,
            (((1,), (1,)), ((), ())),
            preferred_element_type=jnp.float32,
        )
        placed = placed.reshape(len(masks), 3, excites, place_table.shape[0])
        return placed[:, 0] + (placed[:, 1] + placed[:, 2])

    def mask_of(condition):
        return jnp.broadcast_to(jnp.where(condition, 1.0, 0.0), (3 * excites, entries))

    near = table(index % (NC * ROWS), NC * ROWS)
    spot = index // ROWS % NC * 64 + index // (NC * ROWS) * 32 + index % 32
    pivot = table(spot, ROWS)
    for x in range(NX):
        sums = summed([mask_of(chip == x * NZ + z) for z in range(NZ)], near)
        for z in range(NZ):
            out_ref[x, 2 * z] = sums[z, :, :ROWS]
            out_ref[x, 2 * z + 1] = sums[z, :, ROWS:]
        held = (index < 2 * WIDTH) & (index % ROWS // 32 == x)
        out_ref[x, 2 * NZ] = summed([mask_of(held)], pivot)[0]


def dense_blocks(rhs_index, rhs_values):
    excites, entries = rhs_values.shape
    return pl.pallas_call(
        dense_kernel,
        out_shape=jax.ShapeDtypeStruct((NX, NZ * NC + 1, excites, ROWS), jnp.float32),
        compiler_params=pltpu.CompilerParams(vmem_limit_bytes=32 * 2**20),
        cost_estimate=pl.CostEstimate(
            flops=6 * excites * entries * ROWS * 64, bytes_accessed=800000, transcendentals=0
        ),
    )(rhs_index.reshape(1, entries), rhs_values)


def halved(full, at, core):
    block = take(full, at % NX)
    pairs = block[: NZ * NC].reshape(NZ, NC, *block.shape[1:])
    return jnp.concatenate([jnp.where(core == 0, pairs[:, 0], pairs[:, 1]), block[NZ * NC :]])


def forcing_core(full):
    _, x, _, c = place()
    s = sign(c)

    def parts(sgn, core):
        return jnp.concatenate(
            [take(full, (x + sgn + NX) % NX), halved(full, x + 2, core), halved(full, x, core)]
        )

    return parts(s, c) + swap_core(parts(-s, 1 - c))


def forcing_x(summed):
    _, _, _, c = place()
    count = NZ * NC + 1
    lone = jnp.where((jnp.arange(NZ + 1) < NZ)[:, None, None] | (c == 0), 1.0, 0.0)
    side = cube_send(summed[:count], lambda i, j, k: (i + sign(k), j, k))
    across = cube_send(summed[count : count + NZ + 1] * lone, lambda i, j, k: (i + 2, j, k))
    return side, across, summed[count + NZ + 1 :] * lone


def forcing_z(side, across, own):
    _, _, z, c = place()
    s = sign(c)
    own = own + across
    is_c = (jnp.arange(NC) == c)[None, :, None, None]
    pairs = side[: NZ * NC].reshape(NZ, NC, *side.shape[1:])
    pairs = pairs + jnp.where(is_c, own[:NZ, None], 0.0)
    pivot = side[NZ * NC :] + own[NZ:]

    def rows(sgn, core):
        near = [take(pairs, (z + n * sgn + NZ) % NZ) for n in (1, 2, 3)]
        far = [take(take(pairs, at % NZ), core)[None] for at in (z + 4, z)]
        return jnp.concatenate(near + far + [pivot])

    summed = rows(s, c) + swap_core(rows(-s, 1 - c))
    first = jnp.where(c == 0, summed[8:9], 0.0)
    got = [
        cube_send(
            jnp.concatenate([summed[2 * n - 2 : 2 * n], summed[8:9]]),
            lambda i, j, k: (i, j + n * sign(k), k),
        )
        for n in (1, 2, 3)
    ]
    far = cube_send(jnp.concatenate([summed[6:7], first]), lambda i, j, k: (i, j + 4, k))
    near = got[0] + got[1] + got[2]
    mine = take(near[:2], c) + far[0] + summed[7]
    partial = near[2] + far[1] + first[0]
    back = swap_core(jnp.stack([take(near[:2], 1 - c), partial]))
    return mine + back[0], partial + back[1]


def at_core(core, value):
    zero = jnp.zeros_like(value)
    return jnp.concatenate([jnp.where(core == 0, value, zero), jnp.where(core == 0, zero, value)])


def scatter_x(block):
    low = lax.axis_index("cube") % NC == 0
    got = swap_core(jnp.where(low, block[96:], block[32:64]))
    message = jnp.concatenate([jnp.where(low, block[32:64], block[96:]), got])
    side = cube_send(
        message, lambda i, j, k: (sign(k), j, k) if i == 0 and j < 2 else None
    )
    far = cube_send(block[64:96], lambda i, j, k: (2, j, k) if i == 0 and j < 2 else None)
    return message, side, far


def scatter_z(kept, side, far):
    _, x, z, c = place()
    low = c == 0
    side = jnp.where(low, side, jnp.concatenate([side[32:], side[:32]]))
    mine = side + at_core(c, jnp.where(x == 0, kept, far))
    whole = mine + swap_core(mine)

    def piece(p):
        return jnp.concatenate([whole[8 * p : 8 * p + 8], whole[32 + 8 * p : 40 + 8 * p]])

    near = cube_send(
        jnp.where(low, piece(1), piece(2)),
        lambda i, j, k: (i, (-1 - k if j == 0 else 2 + k), k) if j < 2 else None,
    )
    far = cube_send(
        jnp.where(low, whole[24:32], whole[56:]),
        lambda i, j, k: (i, (-3 if j == 0 else 4), k) if j < 2 else None,
    )
    return jnp.where((z < 2) & low, piece(0), 0.0), near, far


def scattered(own, near, far):
    share = own + near + at_core(lax.axis_index("cube") % NC, far)
    return share + swap_core(share)


def gather_z(share):
    low = lax.axis_index("cube") % NC == 0
    own = jnp.where(low, share[:8], share[8:])
    parts = [own]
    for n in (1, 2, 3):
        parts.append(cube_send(share, lambda i, j, k: (i, j + n * sign(k), k)))
    parts.append(cube_send(own, lambda i, j, k: (i, j + 4, k)))
    return parts


def gather_x(mine, theirs):
    block = jnp.concatenate([mine, theirs])
    side = cube_send(block, lambda i, j, k: (i + sign(k), j, k))
    far = cube_send(mine, lambda i, j, k: (i + 2, j, k))
    return block, side, far


def gathered(block, side, far):
    return jnp.concatenate([block, side, far, swap_core(side), swap_core(far)])


def ids_8(x, z, c):
    x, z = x % NX, z % NZ
    lower = (z == 0) | (z > 4)
    pos = jnp.where(lower, (NZ - z) % NZ, z - 1)
    base = (jnp.where(lower, 0, NC) + c) * ROWS + x * 32 + pos * 8
    return base + jnp.arange(8, dtype=jnp.int32)


def ids_16(x, z):
    return jnp.concatenate([ids_8(x, z, 0), ids_8(x, z, 1)])


def ids_64(x, z, c):
    s = sign(c)
    parts = [ids_16(x, z - n * s + NZ) for n in (1, 2, 3)]
    return jnp.concatenate([ids_8(x, z, c)] + parts + [ids_8(x, z + 4, c)])


def ids_128(x, z, c):
    return jnp.concatenate([ids_64(x, z, c), ids_64(x, z, 1 - c)])


def gathered_ids():
    _, x, z, c = place()
    s = sign(c)
    return jnp.concatenate(
        [
            ids_128(x, z, c),
            ids_128(x - s + NX, z, c),
            ids_64(x + 2, z, c),
            ids_128(x + s + NX, z, 1 - c),
            ids_64(x + 2, z, 1 - c),
        ]
    )


def group_order():
    _, x, z, c = place()
    ids = ids_128(x, z, c)
    return ids // ROWS % NC * 64 + ids // WIDTH * 32 + ids % 32


def one_hot_to(ids, size):
    return (jnp.arange(size, dtype=jnp.int32)[:, None] == ids[None, :]).astype(jnp.float32)


def from_first(value):
    got = [lax.ppermute(value, "blk", [(i, (i + d) % NY) for i in range(NY)]) for d in range(1, NY)]
    rank = lax.axis_index("blk")
    out = value
    for d in range(1, NY):
        out = jnp.where(rank == d, got[d - 1], out)
    return out


def shards(front_entries, child_blocks, child_map, pivot_inverse, rhs_index, rhs_values):
    rank, x, z, c = place()
    blk = lax.axis_index("blk")
    holder_one, holder_two = rank < 2, (rank >= 2) & (rank < 4)
    matrix = assemble(front_entries, child_blocks, child_map)

    message, side, far = scatter_x(matrix)
    full = dense_blocks(*after((rhs_index, rhs_values), message))
    side, far, full = lax.optimization_barrier((side, far, full))

    own, near, far = scatter_z(matrix[:32], side, far)
    summed = forcing_core(full)
    own, near, far, summed = lax.optimization_barrier((own, near, far, summed))

    forcing_parts = forcing_x(summed)
    parts = gather_z(scattered(own, near, far))
    forcing, pivots = forcing_z(*forcing_parts)
    parts, forcing, pivots, pivot_inverse = lax.optimization_barrier(
        (parts, forcing, pivots, pivot_inverse)
    )

    cut = CHUNKS[0][1]
    mine = jnp.concatenate([part[:, :cut] for part in parts])
    head = gather_x(mine, swap_core(mine))
    mine = jnp.concatenate([part[:, cut:] for part in parts])
    theirs = swap_core(mine)
    piece = dot(one_hot_to(group_order(), ROWS).T, pivots.T)
    piece = jnp.pad(piece, ((0, 0), (0, 128 - piece.shape[1])))
    mine = jnp.concatenate([mine, piece[:64]], axis=1)
    theirs = jnp.concatenate([theirs, piece[64:]], axis=1)
    head, mine, theirs = lax.optimization_barrier((head, mine, theirs))
    tail = gather_x(mine, theirs)

    first, second = pivot_inverse[0], pivot_inverse[1]
    ids = gathered_ids()
    table = one_hot_to(ids, 2 * WIDTH)
    head = gathered(*head)
    left, right = matrix[:, :WIDTH], matrix[:, WIDTH : 2 * WIDTH]
    l1 = dot(left, first)
    turned = dot(dot(l1, table[:WIDTH]), head[:, WIDTH : 2 * WIDTH])
    reduced = right - turned
    l2 = dot(reduced, second)
    start = rank % 2 * ROWS
    pick_one = lax.dynamic_slice(first, (start, 0), (ROWS, WIDTH))
    pick_two = lax.dynamic_slice(second, (start, 0), (ROWS, WIDTH))
    lead = jnp.where(holder_two, pick_two, l2)
    back = dot(dot(dot(lead, table[WIDTH:]), head[:, :WIDTH]), first)
    panel = jnp.concatenate(
        [
            jnp.where(holder_one, left, l1),
            jnp.where(holder_one, right, jnp.where(holder_two, reduced, l2)),
        ],
        axis=1,
    )
    factors = jnp.where(
        holder_two,
        jnp.concatenate([l1, back], axis=1),
        jnp.concatenate([l1 - back, l2], axis=1),
    )
    factors = from_first(factors)
    zeros = jnp.zeros((ROWS, WIDTH), jnp.float32)
    front_left = jnp.where(
        holder_one,
        0.0,
        jnp.where(holder_two, jnp.concatenate([factors[:, :WIDTH], zeros], axis=1), factors),
    )
    forcing_left = jnp.where(
        holder_one,
        jnp.concatenate([-pick_one, zeros], axis=1),
        jnp.where(
            holder_two, jnp.concatenate([factors[:, WIDTH:], -pick_two], axis=1), factors
        ),
    )
    turned_left = dot(jnp.concatenate([front_left, forcing_left], axis=0), table)

    tail = gathered(*tail)
    width = CHUNKS[1][1] - CHUNKS[1][0]
    body = matrix[:, 512:] - dot(turned_left[:ROWS], tail[:, :width])
    head_out = matrix[:, :512] - dot(turned_left[:ROWS], head)
    head_out = jnp.where(blk == 0, panel, head_out)
    front = jnp.concatenate([head_out, body], axis=1)
    excites = forcing.shape[0]
    change = dot(turned_left[ROWS:], tail[:, width : width + excites]).T
    solved = jnp.where(rank < 4, 0.0, forcing) - change
    return front, solved


def solution(mesh):
    in_specs = (P("cube", "blk"), P("cube", "blk"), P(), P(), P("cube"), P("blk", "cube"))
    out_specs = (P("cube", "blk"), P("blk", "cube"))
    return jax.shard_map(shards, mesh=mesh, in_specs=in_specs, out_specs=out_specs, check_vma=False)
```

```python
import jax
import jax.numpy as jnp
import numpy as np
from jax import lax
from jax.experimental import pallas as pl
from jax.experimental.pallas import tpu as pltpu
from jax.sharding import PartitionSpec as P

NX, NZ, NC, NY = 4, 8, 2, 4
ROWS = 128
WIDTH = 256
HIGH = lax.Precision.HIGHEST


def dot(left, right):
    return jnp.dot(left, right, precision=HIGH, preferred_element_type=jnp.float32)


def after(value, *others):
    return lax.optimization_barrier((value, others))[0]


def cube_send(value, target):
    pairs = []
    for x in range(NX):
        for z in range(NZ):
            for c in range(NC):
                to = target(x, z, c)
                if to is not None:
                    tx, tz, tc = to
                    pairs.append(
                        ((x * NZ + z) * NC + c, ((tx % NX) * NZ + tz % NZ) * NC + tc % NC)
                    )
    return lax.ppermute(value, "cube", pairs)


def swap_core(value):
    return cube_send(value, lambda x, z, c: (x, z, 1 - c))


def place():
    rank = lax.axis_index("cube")
    return rank, rank >> 4, rank >> 1 & 7, rank & 1


def spread_columns(rows, targets, col_base, block):
    count = rows.shape[0]
    blocks = targets.shape[0] // block
    local = (targets - col_base).reshape(blocks, block) - 2 * block * jnp.arange(
        blocks, dtype=jnp.int32
    )[:, None]
    table = (local[:, :, None] == jnp.arange(2 * block, dtype=jnp.int32)[None, None, :]).astype(
        jnp.float32
    )
    shaped = rows.reshape(count, blocks, block)
    placed = jnp.einsum(
        "rbt,btu->rbu", shaped, table, precision=HIGH, preferred_element_type=jnp.float32
    )
    return placed.reshape(count, blocks * 2 * block)


def assemble(front_entries, child_blocks, child_map):
    rows_dev, front_cols = front_entries.shape
    child_cols = child_blocks.shape[1]
    half_rows = rows_dev // 2
    cube_rank = lax.axis_index("cube")
    blk_rank = lax.axis_index("blk")
    parity = cube_rank % 2
    lower_half = child_blocks[:half_rows]
    upper_half = child_blocks[half_rows:]
    kept_rows = jnp.where(parity == 0, lower_half, upper_half)
    sent_rows = jnp.where(parity == 0, upper_half, lower_half)
    arrived = swap_core(sent_rows)
    child_start = cube_rank // 2 * rows_dev + parity * half_rows
    col_first = blk_rank * child_cols
    own_rows = lax.dynamic_slice(child_map, (parity, child_start), (1, half_rows))[0]
    other_rows = lax.dynamic_slice(child_map, (1 - parity, child_start), (1, half_rows))[0]
    own_cols = lax.dynamic_slice(child_map, (parity, col_first), (1, child_cols))[0]
    other_cols = lax.dynamic_slice(child_map, (1 - parity, col_first), (1, child_cols))[0]
    row_base = cube_rank * rows_dev
    col_base = blk_rank * front_cols
    placed = jnp.concatenate(
        [
            spread_columns(kept_rows, own_cols, col_base, rows_dev),
            spread_columns(arrived, other_cols, col_base, rows_dev),
        ],
        axis=0,
    )
    targets = jnp.concatenate([own_rows, other_rows]) - row_base
    row_table = (jnp.arange(rows_dev, dtype=jnp.int32)[:, None] == targets[None, :]).astype(
        jnp.float32
    )
    return front_entries + dot(row_table, placed)


def sign(core):
    return 1 - 2 * core


def local(kernel, place_scalars, arrays, shapes, flops=10**6):
    size = sum(4 * int(np.prod(shape)) for shape in shapes)
    return pl.pallas_call(
        kernel,
        out_shape=[jax.ShapeDtypeStruct(shape, jnp.float32) for shape in shapes],
        in_specs=[pl.BlockSpec(memory_space=pltpu.SMEM)]
        + [pl.BlockSpec(memory_space=pltpu.VMEM)] * len(arrays),
        out_specs=[pl.BlockSpec(memory_space=pltpu.VMEM)] * len(shapes),
        compiler_params=pltpu.CompilerParams(vmem_limit_bytes=40 * 2**20),
        cost_estimate=pl.CostEstimate(flops=flops, bytes_accessed=2 * size, transcendentals=0),
    )(jnp.stack([jnp.asarray(v, jnp.int32) for v in place_scalars]), *arrays)


def dense_kernel(at_ref, index_ref, values_ref, kept_ref, sent_ref):
    x, c = at_ref[0], at_ref[1]
    s = sign(c)
    index = index_ref[...]
    values = values_ref[...]
    excites, entries = values.shape
    high = values.astype(jnp.bfloat16)
    rest = values - high.astype(jnp.float32)
    middle = rest.astype(jnp.bfloat16)
    low = (rest - middle.astype(jnp.float32)).astype(jnp.bfloat16)
    split = jnp.concatenate([high, middle, low], axis=0)
    chip = index >> 8

    def table(at, size):
        rows = lax.broadcasted_iota(jnp.int32, (size, entries), 0)
        return jnp.where(rows == at, 1.0, 0.0).astype(jnp.bfloat16)

    def summed(masks, place_table):
        rows = [split * mask.astype(jnp.bfloat16) for mask in masks]
        placed = lax.dot_general(
            jnp.concatenate(rows, axis=0),
            place_table,
            (((1,), (1,)), ((), ())),
            preferred_element_type=jnp.float32,
        )
        placed = placed.reshape(len(masks), 3, excites, place_table.shape[0])
        return placed[:, 0] + (placed[:, 1] + placed[:, 2])

    def mask_of(condition):
        return jnp.broadcast_to(jnp.where(condition, 1.0, 0.0), (3 * excites, entries))

    near = table(index & 255, NC * ROWS)
    pivot = table((index >> 7 & 1) * 64 + (index >> 8) * 32 + (index & 31), ROWS)

    def blocks(at):
        sums = summed([mask_of(chip == at * NZ + z) for z in range(NZ)], near)
        held = (index < 2 * WIDTH) & (index >> 5 & 3 == at)
        return sums, summed([mask_of(held)], pivot)[0]

    for ref, at in ((kept_ref, x + s & 3), (sent_ref, x - s & 3)):
        sums, group = blocks(at)
        for z in range(NZ):
            ref[2 * z] = sums[z, :, :ROWS]
            ref[2 * z + 1] = sums[z, :, ROWS:]
        ref[2 * NZ] = group
    for start, at in ((17, x + 2 & 3), (26, x)):
        sums, group = blocks(at)
        for z in range(NZ):
            first, second = sums[z, :, :ROWS], sums[z, :, ROWS:]
            kept_ref[start + z] = jnp.where(c == 0, first, second)
            sent_ref[start + z] = jnp.where(c == 0, second, first)
        kept_ref[start + NZ] = jnp.where(c == 0, group, 0.0)
        sent_ref[start + NZ] = jnp.where(c == 0, 0.0, group)


def forcing_core(rhs_index, rhs_values):
    _, x, _, c = place()
    entries = rhs_values.shape[1]
    shape = (35, rhs_values.shape[0], ROWS)
    kept, sent = local(
        dense_kernel,
        (x, c),
        (rhs_index.reshape(1, entries), rhs_values),
        (shape, shape),
        flops=10**9,
    )
    return kept + swap_core(sent)


def forcing_x(summed):
    side = cube_send(summed[:17], lambda i, j, k: (i + sign(k), j, k))
    across = cube_send(summed[17:26], lambda i, j, k: (i + 2, j, k))
    return side, across, summed[26:]


def rows_kernel(at_ref, side_ref, across_ref, own_ref, kept_ref, sent_ref):
    z, c = at_ref[0], at_ref[1]
    s = sign(c)
    for ref, sgn in ((kept_ref, s), (sent_ref, -s)):
        for n in (1, 2, 3):
            i = z + n * sgn & 7
            for k in range(NC):
                mine = own_ref[i] + across_ref[i]
                ref[2 * n - 2 + k] = side_ref[2 * i + k] + jnp.where(c == k, mine, 0.0)
    for slot, i in ((6, z + 4 & 7), (7, z)):
        kept_ref[slot] = side_ref[2 * i + c] + (own_ref[i] + across_ref[i])
        sent_ref[slot] = side_ref[2 * i + 1 - c]
    pivot = side_ref[16] + (own_ref[8] + across_ref[8])
    kept_ref[8] = pivot
    sent_ref[8] = pivot


def forcing_rows(side, across, own):
    _, _, z, c = place()
    kept, sent = local(rows_kernel, (z, c), (side, across, own), (own.shape, own.shape))
    return kept, swap_core(sent)


def scatter_x(block):
    return [
        cube_send(
            block[32 * d : 32 * d + 32],
            lambda i, j, k: (d, j, k) if i == 0 and j < 2 else None,
        )
        for d in range(1, NX)
    ]


def scatter_z(quarter):
    return [
        cube_send(
            quarter[8 * d : 8 * d + 8],
            lambda i, j, k: (i, (-d if j == 0 else 1 + d), k) if j < 2 else None,
        )
        for d in range(1, NZ // 2)
    ]


def message_kernel(at_ref, share_ref, other_ref, kept_ref, came_ref, *out_refs):
    c, turn = at_ref[0], at_ref[1]
    low = c == 0
    width = share_ref.shape[1]

    def columns(ref):
        left, right = ref[:, :WIDTH], ref[:, WIDTH : 2 * WIDTH]
        yield 0, jnp.where(turn == 1, right, left)
        yield WIDTH, jnp.where(turn == 1, left, right)
        yield 2 * WIDTH, ref[:, 2 * WIDTH :]

    summed = [kept_ref[i] + came_ref[i] for i in range(9)]
    for (at, mine), (_, other) in zip(columns(share_ref), columns(other_ref)):
        span = slice(at, at + mine.shape[1])
        for ref in out_refs[:3]:
            ref[:8, span] = jnp.where(low, mine, other)
            ref[8:, span] = jnp.where(low, other, mine)
        out_refs[3][:, span] = mine
    for n, ref in enumerate(out_refs[:3]):
        for i, block in enumerate((summed[2 * n], summed[2 * n + 1], summed[8])):
            ref[:, width + i * ROWS : width + (i + 1) * ROWS] = block
    first = jnp.where(low, summed[8], 0.0)
    for i, block in enumerate((summed[6][:8], summed[6][8:], first[:8], first[8:])):
        out_refs[3][:, width + i * ROWS : width + (i + 1) * ROWS] = block
    out_refs[4][0] = summed[7]
    out_refs[4][1] = first


def unpack_kernel(at_ref, own_ref, one_ref, two_ref, three_ref, far_ref, left_ref, *out_refs):
    low = at_ref[0] == 0
    head_ref, tail_ref, mine_ref, back_ref = out_refs
    width = WIDTH + tail_ref.shape[1]
    row = 0
    for ref in (own_ref, one_ref, two_ref, three_ref, far_ref):
        count = ref.shape[0]
        head_ref[row : row + count] = ref[:, :WIDTH]
        tail_ref[row : row + count] = ref[:, WIDTH:width]
        row += count
    spans = [slice(width + i * ROWS, width + (i + 1) * ROWS) for i in range(4)]
    sums = [one_ref[:, at] + two_ref[:, at] + three_ref[:, at] for at in spans[:3]]
    far = [far_ref[:, at] for at in spans]
    mine_ref[0] = (
        jnp.where(low, sums[0], sums[1])
        + jnp.concatenate([far[0], far[1]], axis=0)
        + left_ref[0]
    )
    pivot = sums[2] + jnp.concatenate([far[2], far[3]], axis=0) + left_ref[1]
    mine_ref[1] = pivot
    back_ref[0] = jnp.where(low, sums[1], sums[0])
    back_ref[1] = pivot


def gather_z(share, kept, came, corner_first):
    c = lax.axis_index("cube") & 1
    width = share.shape[1]
    excites = kept.shape[1]
    near = (2 * excites // 2, width + 3 * ROWS)
    *messages, left = local(
        message_kernel,
        (c, corner_first),
        (share, swap_core(share), kept, came),
        (near, near, near, (8, width + 4 * ROWS), (2, excites, ROWS)),
    )
    got = [
        cube_send(messages[n - 1], lambda i, j, k: (i, j + n * sign(k), k)) for n in (1, 2, 3)
    ]
    far = cube_send(messages[3], lambda i, j, k: (i, j + 4, k))
    head, tail, mine, back = local(
        unpack_kernel,
        (c,),
        (messages[3], *got, far, left),
        ((64, WIDTH), (64, width - WIDTH), (2, excites, ROWS), (2, excites, ROWS)),
    )
    return head, tail, mine, swap_core(back)


def tail_kernel(at_ref, mine_ref, theirs_ref, ours_ref, back_ref, order_ref, *out_refs):
    all_ref, forcing_ref = out_refs
    count, width = mine_ref.shape
    forcing_ref[...] = ours_ref[0] + back_ref[0]
    pivots = ours_ref[1] + back_ref[1]
    excites = pivots.shape[0]
    spots = lax.broadcasted_iota(jnp.int32, (ROWS, ROWS), 0)
    table = jnp.where(spots == order_ref[...], 1.0, 0.0)
    ordered = dot(pivots, table)
    filler = jnp.zeros((ROWS - excites, ROWS), jnp.float32)
    columns = jnp.concatenate([ordered, filler], axis=0).T
    all_ref[:count, :width] = mine_ref[...]
    all_ref[count:, :width] = theirs_ref[...]
    all_ref[:, width:] = columns


def gather_x(block, mine):
    side = cube_send(block, lambda i, j, k: (i + sign(k), j, k))
    far = cube_send(mine, lambda i, j, k: (i + 2, j, k))
    return side, far


def chain_x(block, half):
    side = cube_send(block, lambda i, j, k: (i + sign(k), j, k))
    far = cube_send(side[:half], lambda i, j, k: (i + sign(k), j, k))
    return side, far


def rows_8(dx, dz, core):
    return [(*dx, *dz, core, r) for r in range(8)]


def rows_64(dx, flip):
    s = -1 if flip else 1
    out = rows_8(dx, (0, 0), 2 + flip)
    for n in (1, 2, 3):
        out += rows_8(dx, (-n * s, 0), 0) + rows_8(dx, (-n * s, 0), 1)
    return out + rows_8(dx, (0, 4), 2 + flip)


def rows_128(dx, flip):
    return rows_64(dx, flip) + rows_64(dx, 1 - flip)


def row_ids(rows):
    _, x, z, c = place()
    s = sign(c)
    xs, x0, zs, z0, core, r = (np.array(v, np.int32)[None] for v in zip(*rows))
    at_x = x + xs * s + x0 & 3
    at_z = z + zs * s + z0 & 7
    core = jnp.where(core > 1, c ^ (core - 2), core)
    lower = (at_z == 0) | (at_z > 4)
    pos = jnp.where(lower, 8 - at_z & 7, at_z - 1)
    return (jnp.where(lower, 0, NC) + core) * ROWS + at_x * 32 + pos * 8 + r


def gathered_ids():
    return row_ids(
        rows_128((0, 0), 0)
        + rows_128((-1, 0), 0)
        + rows_64((0, 2), 0)
        + rows_128((1, 0), 1)
        + rows_64((0, 2), 1)
    )


def group_order():
    ids = row_ids(rows_128((0, 0), 0))
    return (ids >> 7 & 1) * 64 + (ids >> 8) * 32 + (ids & 31)


def local_table(ids, first, count):
    rows = lax.broadcasted_iota(jnp.int32, (count, ids.shape[1]), 0) + first
    return jnp.where(rows == ids, 1.0, 0.0)


def factors_kernel(
    at_ref, panel_ref, pivots_ref, ids_ref, block_ref, side_ref, far_ref, side2_ref, far2_ref,
    out_ref, factors_ref, head_ref
):
    holder, start = at_ref[0], at_ref[1]
    two = holder == 2
    row = 0
    for ref in (block_ref, side_ref, far_ref, side2_ref, far2_ref):
        head_ref[row : row + ref.shape[0]] = ref[...]
        row += ref.shape[0]
    head = head_ref[...]
    ids = ids_ref[...]
    left, right = panel_ref[:, :WIDTH], panel_ref[:, WIDTH:]
    first, second = pivots_ref[0], pivots_ref[1]
    l1 = dot(left, first)
    reduced = right - dot(dot(l1, local_table(ids, 0, WIDTH)), head)
    l2 = dot(reduced, second)
    start = pl.multiple_of(start, ROWS)
    lead = jnp.where(two, pivots_ref[1, pl.ds(start, ROWS), :], l2)
    back = dot(dot(dot(lead, local_table(ids, WIDTH, WIDTH)), head), first)
    out_ref[:, :WIDTH] = jnp.where(holder == 1, left, l1)
    out_ref[:, WIDTH:] = jnp.where(holder == 1, right, jnp.where(two, reduced, l2))
    factors_ref[:, :WIDTH] = jnp.where(two, l1, l1 - back)
    factors_ref[:, WIDTH:] = jnp.where(two, back, l2)


def left_kernel(
    at_ref, own_ref, one_ref, two_ref, three_ref, pivots_ref, ids_ref, head_ref, matrix_ref,
    panel_ref, turned_ref, out_ref
):
    holder, start, blk = at_ref[0], at_ref[1], at_ref[2]
    one, two = holder == 1, holder == 2
    factors = own_ref[...]
    for d, ref in enumerate((one_ref, two_ref, three_ref)):
        factors = jnp.where(blk == d + 1, ref[...], factors)
    first, second = factors[:, :WIDTH], factors[:, WIDTH:]
    start = pl.multiple_of(start, ROWS)
    pick_one = pivots_ref[0, pl.ds(start, ROWS), :]
    pick_two = pivots_ref[1, pl.ds(start, ROWS), :]
    lead = jnp.concatenate(
        [
            jnp.where(one, 0.0, first),
            jnp.where(one, -pick_one, jnp.where(two, second, first)),
        ],
        axis=0,
    )
    rest = jnp.concatenate(
        [
            jnp.where(holder > 0, 0.0, second),
            jnp.where(one, 0.0, jnp.where(two, -pick_two, second)),
        ],
        axis=0,
    )
    ids = ids_ref[...]
    turned = dot(lead, local_table(ids, 0, WIDTH)) + dot(rest, local_table(ids, WIDTH, WIDTH))
    turned_ref[...] = turned
    change = dot(turned[:ROWS], head_ref[...])
    out_ref[...] = jnp.where(blk == 0, panel_ref[...], matrix_ref[...] - change)


def from_first(value):
    return [
        lax.ppermute(value, "blk", [(i, (i + d) % NY) for i in range(NY)]) for d in range(1, NY)
    ]


def shards(front_entries, child_blocks, child_map, pivot_inverse, rhs_index, rhs_values):
    rank, x, z, c = place()
    blk = lax.axis_index("blk")
    holder = jnp.where(rank < 2, 1, jnp.where(rank < 4, 2, 0))
    start = (rank & 1) * ROWS
    matrix = assemble(front_entries, child_blocks, child_map)

    corner_first = (blk == 0) & ((z == 0) | (z > 4))
    sent = scatter_x(matrix)
    across_x = forcing_x(forcing_core(rhs_index, rhs_values))
    sent, across_x = lax.optimization_barrier((sent, across_x))

    quarter = jnp.where(x == 0, matrix[:32], 0.0) + sent[0] + sent[1] + sent[2]
    sent = scatter_z(quarter)
    kept, came = forcing_rows(*across_x)
    sent, quarter, kept, came = lax.optimization_barrier((sent, quarter, kept, came))

    share = jnp.where(z < 2, quarter[:8], 0.0) + sent[0] + sent[1] + sent[2]
    head, mine, ours, back = gather_z(share, kept, came, corner_first)
    head, mine, pivot_inverse = lax.optimization_barrier((head, mine, pivot_inverse))

    block = jnp.concatenate([head, swap_core(head)])
    head = (block, *gather_x(block, head))
    count, width = mine.shape
    excites = ours.shape[1]
    block, forcing = local(
        tail_kernel,
        (c,),
        (mine, swap_core(mine), ours, back, group_order()),
        ((2 * count, width + ROWS), ours.shape[1:]),
    )
    head, block = lax.optimization_barrier((head, block))
    side, far = chain_x(block, count)

    ids = gathered_ids()
    head_side, head_far = head[1:]
    panel, factors, head = local(
        factors_kernel,
        (holder, start),
        (matrix[:, : 2 * WIDTH], pivot_inverse, ids, *head, swap_core(head_side), swap_core(head_far)),
        ((ROWS, 2 * WIDTH), (ROWS, 2 * WIDTH), (2 * WIDTH, WIDTH)),
        flops=4 * 10**9,
    )
    turned_left, head_out = local(
        left_kernel,
        (holder, start, blk),
        (factors, *from_first(factors), pivot_inverse, ids, head, matrix[:, :WIDTH], panel[:, :WIDTH]),
        ((2 * ROWS, 2 * WIDTH), (ROWS, WIDTH)),
        flops=10**9,
    )
    own = jnp.concatenate([block, side, far])
    rest = jnp.concatenate([swap_core(side), swap_core(far)])
    cut = own.shape[0]
    body = matrix[:, WIDTH:] - dot(turned_left[:ROWS, :cut], own[:, :width])
    change = dot(turned_left[ROWS:, :cut], own[:, width : width + excites])
    body = body - dot(turned_left[:ROWS, cut:], rest[:, :width])
    change = change + dot(turned_left[ROWS:, cut:], rest[:, width : width + excites])
    front = jnp.concatenate(
        [
            head_out,
            jnp.where(blk == 0, panel[:, WIDTH:], body[:, :WIDTH]),
            body[:, WIDTH:],
        ],
        axis=1,
    )
    solved = jnp.where(rank < 4, 0.0, forcing) - change.T
    return front, solved


def solution(mesh):
    in_specs = (P("cube", "blk"), P("cube", "blk"), P(), P(), P("cube"), P("blk", "cube"))
    out_specs = (P("cube", "blk"), P("blk", "cube"))
    return jax.shard_map(shards, mesh=mesh, in_specs=in_specs, out_specs=out_specs, check_vma=False)
```

```python
import jax
import jax.numpy as jnp
import numpy as np
from jax import lax
from jax.experimental import pallas as pl
from jax.experimental.pallas import tpu as pltpu
from jax.sharding import PartitionSpec as P

NX, NZ, NC, NY = 4, 8, 2, 4
ROWS = 128
WIDTH = 256
HEAD = 512
HIGH = lax.Precision.HIGHEST


def dot(left, right):
    return jnp.dot(left, right, precision=HIGH, preferred_element_type=jnp.float32)


def after(value, *others):
    return lax.optimization_barrier((value, others))[0]


def cube_send(value, target):
    pairs = []
    for x in range(NX):
        for z in range(NZ):
            for c in range(NC):
                to = target(x, z, c)
                if to is not None:
                    tx, tz, tc = to
                    pairs.append(
                        ((x * NZ + z) * NC + c, ((tx % NX) * NZ + tz % NZ) * NC + tc % NC)
                    )
    return lax.ppermute(value, "cube", pairs)


def swap_core(value):
    return cube_send(value, lambda x, z, c: (x, z, 1 - c))


def place():
    rank = lax.axis_index("cube")
    return rank, rank >> 4, rank >> 1 & 7, rank & 1


def sign(core):
    return 1 - 2 * core


def local(kernel, place_scalars, arrays, shapes, flops=10**6):
    size = sum(4 * int(np.prod(shape)) for shape in shapes)
    return pl.pallas_call(
        kernel,
        out_shape=[jax.ShapeDtypeStruct(shape, jnp.float32) for shape in shapes],
        in_specs=[pl.BlockSpec(memory_space=pltpu.SMEM)]
        + [pl.BlockSpec(memory_space=pltpu.VMEM)] * len(arrays),
        out_specs=[pl.BlockSpec(memory_space=pltpu.VMEM)] * len(shapes),
        compiler_params=pltpu.CompilerParams(vmem_limit_bytes=40 * 2**20),
        cost_estimate=pl.CostEstimate(flops=flops, bytes_accessed=2 * size, transcendentals=0),
    )(jnp.stack([jnp.asarray(v, jnp.int32) for v in place_scalars]), *arrays)


def split(values):
    high = values.astype(jnp.bfloat16)
    rest = values - high.astype(jnp.float32)
    middle = rest.astype(jnp.bfloat16)
    return high, middle, (rest - middle.astype(jnp.float32)).astype(jnp.bfloat16)


def assemble_kernel(at_ref, front_ref, child_ref, came_ref, rows_ref, cols_ref, out_ref):
    parity, row_base, col_base = at_ref[0], at_ref[1], at_ref[2]
    count, width = came_ref.shape
    kept = child_ref[pl.ds(pl.multiple_of(parity * count, count), count), :]
    came = came_ref[...]
    even = parity == 0
    children = [jnp.where(even, kept, came), jnp.where(even, came, kept)]
    children = [jnp.concatenate(split(child), axis=0) for child in children]
    spots = lax.broadcasted_iota(jnp.int32, (ROWS, ROWS), 0) + row_base
    row_table = jnp.where(spots == rows_ref[...], 1.0, 0.0).astype(jnp.bfloat16)
    targets = lax.broadcasted_iota(jnp.int32, (2 * ROWS, ROWS), 0) + col_base
    for b in range(width // ROWS):
        span = slice(b * ROWS, (b + 1) * ROWS)
        out_span = slice(2 * b * ROWS, 2 * (b + 1) * ROWS)
        placed = []
        for k, child in enumerate(children):
            table = jnp.where(targets + 2 * b * ROWS == cols_ref[k : k + 1, span], 1.0, 0.0)
            parts = lax.dot_general(
                child[:, span],
                table.astype(jnp.bfloat16),
                (((1,), (1,)), ((), ())),
                preferred_element_type=jnp.float32,
            )
            placed.append(parts[:count] + (parts[count : 2 * count] + parts[2 * count :]))
        parts = jnp.concatenate(split(jnp.concatenate(placed, axis=0)), axis=1)
        sums = jnp.dot(row_table, parts, preferred_element_type=jnp.float32)
        size = 2 * ROWS
        sums = sums[:, :size] + (sums[:, size : 2 * size] + sums[:, 2 * size :])
        out_ref[:, out_span] = front_ref[:, out_span] + sums


def assemble(front_entries, child_blocks, child_map):
    rows_dev, front_cols = front_entries.shape
    child_cols = child_blocks.shape[1]
    half_rows = rows_dev // 2
    rank, _, _, parity = place()
    blk = lax.axis_index("blk")
    sent_rows = lax.dynamic_slice_in_dim(child_blocks, (1 - parity) * half_rows, half_rows)
    child_start = (rank >> 1) * rows_dev + parity * half_rows
    rows = lax.dynamic_slice(child_map, (0, child_start), (2, half_rows)).reshape(1, rows_dev)
    cols = lax.dynamic_slice(child_map, (0, blk * child_cols), (2, child_cols))
    return local(
        assemble_kernel,
        (parity, rank * rows_dev, blk * front_cols),
        (front_entries, child_blocks, swap_core(sent_rows), rows, cols),
        (front_entries.shape,),
        flops=10**9,
    )[0]


def dense_kernel(at_ref, index_ref, values_ref, kept_ref, sent_ref):
    x, c = at_ref[0], at_ref[1]
    s = sign(c)
    index = index_ref[...]
    values = values_ref[...]
    excites, entries = values.shape
    parts = jnp.concatenate(split(values), axis=0)
    chip = index >> 8

    def table(at, size):
        rows = lax.broadcasted_iota(jnp.int32, (size, entries), 0)
        return jnp.where(rows == at, 1.0, 0.0).astype(jnp.bfloat16)

    def summed(masks, place_table):
        rows = [parts * mask.astype(jnp.bfloat16) for mask in masks]
        placed = lax.dot_general(
            jnp.concatenate(rows, axis=0),
            place_table,
            (((1,), (1,)), ((), ())),
            preferred_element_type=jnp.float32,
        )
        placed = placed.reshape(len(masks), 3, excites, place_table.shape[0])
        return placed[:, 0] + (placed[:, 1] + placed[:, 2])

    def mask_of(condition):
        return jnp.broadcast_to(jnp.where(condition, 1.0, 0.0), (3 * excites, entries))

    near = table(index & 255, NC * ROWS)
    pivot = table((index >> 7 & 1) * 64 + (index >> 8) * 32 + (index & 31), ROWS)

    def blocks(at):
        sums = summed([mask_of(chip == at * NZ + z) for z in range(NZ)], near)
        held = (index < 2 * WIDTH) & (index >> 5 & 3 == at)
        return sums, summed([mask_of(held)], pivot)[0]

    for ref, at in ((kept_ref, x + s & 3), (sent_ref, x - s & 3)):
        sums, group = blocks(at)
        for z in range(NZ):
            ref[2 * z] = sums[z, :, :ROWS]
            ref[2 * z + 1] = sums[z, :, ROWS:]
        ref[2 * NZ] = group
    for start, at in ((17, x + 2 & 3), (26, x)):
        sums, group = blocks(at)
        for z in range(NZ):
            first, second = sums[z, :, :ROWS], sums[z, :, ROWS:]
            kept_ref[start + z] = jnp.where(c == 0, first, second)
            sent_ref[start + z] = jnp.where(c == 0, second, first)
        kept_ref[start + NZ] = jnp.where(c == 0, group, 0.0)
        sent_ref[start + NZ] = jnp.where(c == 0, 0.0, group)


def forcing_core(rhs_index, rhs_values):
    _, x, _, c = place()
    entries = rhs_values.shape[1]
    shape = (35, rhs_values.shape[0], ROWS)
    kept, sent = local(
        dense_kernel,
        (x, c),
        (rhs_index.reshape(1, entries), rhs_values),
        (shape, shape),
        flops=10**9,
    )
    return kept + swap_core(sent)


def forcing_x(summed):
    side = cube_send(summed[:17], lambda i, j, k: (i + sign(k), j, k))
    across = cube_send(summed[17:26], lambda i, j, k: (i + 2, j, k))
    return side, across, summed[26:]


def rows_kernel(at_ref, side_ref, across_ref, own_ref, kept_ref, sent_ref):
    z, c = at_ref[0], at_ref[1]
    s = sign(c)
    for ref, sgn in ((kept_ref, s), (sent_ref, -s)):
        for n in (1, 2, 3):
            i = z + n * sgn & 7
            for k in range(NC):
                mine = own_ref[i] + across_ref[i]
                ref[2 * n - 2 + k] = side_ref[2 * i + k] + jnp.where(c == k, mine, 0.0)
    for slot, i in ((6, z + 4 & 7), (7, z)):
        kept_ref[slot] = side_ref[2 * i + c] + (own_ref[i] + across_ref[i])
        sent_ref[slot] = side_ref[2 * i + 1 - c]
    pivot = side_ref[16] + (own_ref[8] + across_ref[8])
    kept_ref[8] = pivot
    sent_ref[8] = pivot


def forcing_rows(side, across, own):
    _, _, z, c = place()
    kept, sent = local(rows_kernel, (z, c), (side, across, own), (own.shape, own.shape))
    return kept, swap_core(sent)


def scatter_x(block):
    return [
        cube_send(
            block[32 * d : 32 * d + 32],
            lambda i, j, k: (d, j, k) if i == 0 and j < 2 else None,
        )
        for d in range(1, NX)
    ]


def scatter_z(quarter):
    return [
        cube_send(
            quarter[8 * d : 8 * d + 8],
            lambda i, j, k: (i, (-d if j == 0 else 1 + d), k) if j < 2 else None,
        )
        for d in range(1, NZ // 2)
    ]


def message_kernel(at_ref, share_ref, other_ref, kept_ref, came_ref, *out_refs):
    c, turn = at_ref[0], at_ref[1]
    low = c == 0
    head_ref, near_refs, far_ref, left_ref = out_refs[0], out_refs[1:4], out_refs[4], out_refs[5]
    width = share_ref.shape[1] - HEAD

    def columns(ref):
        left, right = ref[:, :WIDTH], ref[:, WIDTH:HEAD]
        turned = [jnp.where(turn == 1, right, left), jnp.where(turn == 1, left, right)]
        return jnp.concatenate(turned, axis=1), ref[:, HEAD:]

    summed = [kept_ref[i] + came_ref[i] for i in range(9)]
    (head, tail), (head_other, tail_other) = columns(share_ref), columns(other_ref)
    head_ref[:8] = jnp.where(low, head, head_other)
    head_ref[8:] = jnp.where(low, head_other, head)
    out_refs[6][...] = head
    for n, ref in enumerate(near_refs):
        ref[:8, :width] = jnp.where(low, tail, tail_other)
        ref[8:, :width] = jnp.where(low, tail_other, tail)
        for i, block in enumerate((summed[2 * n], summed[2 * n + 1], summed[8])):
            ref[:, width + i * ROWS : width + (i + 1) * ROWS] = block
    far_ref[:, :width] = tail
    first = jnp.where(low, summed[8], 0.0)
    for i, block in enumerate((summed[6][:8], summed[6][8:], first[:8], first[8:])):
        far_ref[:, width + i * ROWS : width + (i + 1) * ROWS] = block
    left_ref[0] = summed[7]
    left_ref[1] = first


def unpack_kernel(at_ref, own_ref, one_ref, two_ref, three_ref, far_ref, left_ref, *out_refs):
    low = at_ref[0] == 0
    tail_ref, mine_ref, back_ref = out_refs
    width = tail_ref.shape[1]
    row = 0
    for ref in (own_ref, one_ref, two_ref, three_ref, far_ref):
        count = ref.shape[0]
        tail_ref[row : row + count] = ref[:, :width]
        row += count
    spans = [slice(width + i * ROWS, width + (i + 1) * ROWS) for i in range(4)]
    sums = [one_ref[:, at] + two_ref[:, at] + three_ref[:, at] for at in spans[:3]]
    far = [far_ref[:, at] for at in spans]
    mine_ref[0] = (
        jnp.where(low, sums[0], sums[1])
        + jnp.concatenate([far[0], far[1]], axis=0)
        + left_ref[0]
    )
    pivot = sums[2] + jnp.concatenate([far[2], far[3]], axis=0) + left_ref[1]
    mine_ref[1] = pivot
    back_ref[0] = jnp.where(low, sums[1], sums[0])
    back_ref[1] = pivot


def stack_kernel(_, *refs):
    row = 0
    for ref in refs[:-1]:
        refs[-1][row : row + ref.shape[0]] = ref[...]
        row += ref.shape[0]


def stacked(*arrays):
    rows = sum(array.shape[0] for array in arrays)
    return local(stack_kernel, (0,), arrays, ((rows, arrays[0].shape[1]),))[0]


def rows_along_z(messages, far):
    got = [
        cube_send(message, lambda i, j, k: (i, j + n * sign(k), k))
        for n, message in enumerate(messages, 1)
    ]
    return got + [cube_send(far, lambda i, j, k: (i, j + 4, k))]


def tail_kernel(at_ref, mine_ref, theirs_ref, ours_ref, back_ref, order_ref, *out_refs):
    all_ref, forcing_ref = out_refs
    count, width = mine_ref.shape
    forcing_ref[...] = ours_ref[0] + back_ref[0]
    pivots = ours_ref[1] + back_ref[1]
    excites = pivots.shape[0]
    spots = lax.broadcasted_iota(jnp.int32, (ROWS, ROWS), 0)
    table = jnp.where(spots == order_ref[...], 1.0, 0.0)
    ordered = dot(pivots, table)
    filler = jnp.zeros((ROWS - excites, ROWS), jnp.float32)
    columns = jnp.concatenate([ordered, filler], axis=0).T
    all_ref[:count, :width] = mine_ref[...]
    all_ref[count:, :width] = theirs_ref[...]
    all_ref[:, width:] = columns


def gather_x(block, mine):
    side = cube_send(block, lambda i, j, k: (i + sign(k), j, k))
    far = cube_send(mine, lambda i, j, k: (i + 2, j, k))
    return side, far


def rows_8(dx, dz, core):
    return [(*dx, *dz, core, r) for r in range(8)]


def rows_64(dx, flip):
    s = -1 if flip else 1
    out = rows_8(dx, (0, 0), 2 + flip)
    for n in (1, 2, 3):
        out += rows_8(dx, (-n * s, 0), 0) + rows_8(dx, (-n * s, 0), 1)
    return out + rows_8(dx, (0, 4), 2 + flip)


def rows_128(dx, flip):
    return rows_64(dx, flip) + rows_64(dx, 1 - flip)


def row_ids(rows):
    _, x, z, c = place()
    s = sign(c)
    xs, x0, zs, z0, core, r = (np.array(v, np.int32)[None] for v in zip(*rows))
    at_x = x + xs * s + x0 & 3
    at_z = z + zs * s + z0 & 7
    core = jnp.where(core > 1, c ^ (core - 2), core)
    lower = (at_z == 0) | (at_z > 4)
    pos = jnp.where(lower, 8 - at_z & 7, at_z - 1)
    return (jnp.where(lower, 0, NC) + core) * ROWS + at_x * 32 + pos * 8 + r


def gathered_ids():
    return row_ids(
        rows_128((0, 0), 0)
        + rows_128((-1, 0), 0)
        + rows_64((0, 2), 0)
        + rows_128((1, 0), 1)
        + rows_64((0, 2), 1)
    )


def group_order():
    ids = row_ids(rows_128((0, 0), 0))
    return (ids >> 7 & 1) * 64 + (ids >> 8) * 32 + (ids & 31)


def local_table(ids, first, count):
    rows = lax.broadcasted_iota(jnp.int32, (count, ids.shape[1]), 0) + first
    return jnp.where(rows == ids, 1.0, 0.0)


def factors_kernel(
    at_ref, panel_ref, pivots_ref, ids_ref, block_ref, side_ref, far_ref, side2_ref, far2_ref,
    out_ref, factors_ref, head_ref
):
    holder, start = at_ref[0], at_ref[1]
    two = holder == 2
    row = 0
    for ref in (block_ref, side_ref, far_ref, side2_ref, far2_ref):
        head_ref[row : row + ref.shape[0]] = ref[...]
        row += ref.shape[0]
    head = head_ref[:, :WIDTH]
    ids = ids_ref[...]
    left, right = panel_ref[:, :WIDTH], panel_ref[:, WIDTH:]
    first, second = pivots_ref[0], pivots_ref[1]
    l1 = dot(left, first)
    reduced = right - dot(dot(l1, local_table(ids, 0, WIDTH)), head)
    l2 = dot(reduced, second)
    start = pl.multiple_of(start, ROWS)
    lead = jnp.where(two, pivots_ref[1, pl.ds(start, ROWS), :], l2)
    back = dot(dot(dot(lead, local_table(ids, WIDTH, WIDTH)), head), first)
    out_ref[:, :WIDTH] = jnp.where(holder == 1, left, l1)
    out_ref[:, WIDTH:] = jnp.where(holder == 1, right, jnp.where(two, reduced, l2))
    factors_ref[:, :WIDTH] = jnp.where(two, l1, l1 - back)
    factors_ref[:, WIDTH:] = jnp.where(two, back, l2)


def left_kernel(
    at_ref, own_ref, one_ref, two_ref, three_ref, pivots_ref, ids_ref, head_ref, matrix_ref,
    panel_ref, turned_ref, out_ref
):
    holder, start, blk = at_ref[0], at_ref[1], at_ref[2]
    one, two = holder == 1, holder == 2
    factors = own_ref[...]
    for d, ref in enumerate((one_ref, two_ref, three_ref)):
        factors = jnp.where(blk == d + 1, ref[...], factors)
    first, second = factors[:, :WIDTH], factors[:, WIDTH:]
    start = pl.multiple_of(start, ROWS)
    pick_one = pivots_ref[0, pl.ds(start, ROWS), :]
    pick_two = pivots_ref[1, pl.ds(start, ROWS), :]
    lead = jnp.concatenate(
        [
            jnp.where(one, 0.0, first),
            jnp.where(one, -pick_one, jnp.where(two, second, first)),
        ],
        axis=0,
    )
    rest = jnp.concatenate(
        [
            jnp.where(holder > 0, 0.0, second),
            jnp.where(one, 0.0, jnp.where(two, -pick_two, second)),
        ],
        axis=0,
    )
    ids = ids_ref[...]
    turned = dot(lead, local_table(ids, 0, WIDTH)) + dot(rest, local_table(ids, WIDTH, WIDTH))
    turned_ref[...] = turned
    change = dot(turned[:ROWS], head_ref[...])
    out_ref[...] = jnp.where(blk == 0, panel_ref[...], matrix_ref[...] - change)


def own_kernel(_, left_ref, matrix_ref, block_ref, side_ref, far_ref, body_ref, change_ref):
    width = body_ref.shape[1]
    rows = jnp.concatenate([block_ref[...], side_ref[...], far_ref[...]], axis=0)
    cut = rows.shape[0]
    left = left_ref[:, :cut]
    for at in range(0, width, WIDTH):
        change = dot(left[:ROWS], rows[:, at : at + WIDTH])
        body_ref[:, at : at + WIDTH] = matrix_ref[:, HEAD + at : HEAD + at + WIDTH] - change
    change_ref[...] = dot(left[ROWS:], rows[:, width:])


def final_kernel(
    at_ref, left_ref, head_ref, body_ref, change_ref, forcing_ref, side_ref, far_ref,
    front_ref, solved_ref
):
    width = body_ref.shape[1]
    rows = jnp.concatenate([side_ref[...], far_ref[...]], axis=0)
    left = left_ref[:, left_ref.shape[1] - rows.shape[0] :]
    front_ref[:, :HEAD] = head_ref[...]
    for at in range(0, width, WIDTH):
        change = dot(left[:ROWS], rows[:, at : at + WIDTH])
        front_ref[:, HEAD + at : HEAD + at + WIDTH] = body_ref[:, at : at + WIDTH] - change
    change = change_ref[...] + dot(left[ROWS:], rows[:, width:])
    kept = jnp.where(at_ref[0] > 0, 0.0, forcing_ref[...])
    solved_ref[...] = kept - change.T[: kept.shape[0]]


def from_first(value):
    return [
        lax.ppermute(value, "blk", [(i, (i + d) % NY) for i in range(NY)]) for d in range(1, NY)
    ]


def shards(front_entries, child_blocks, child_map, pivot_inverse, rhs_index, rhs_values):
    rank, x, z, c = place()
    blk = lax.axis_index("blk")
    holder = jnp.where(rank < 2, 1, jnp.where(rank < 4, 2, 0))
    start = (rank & 1) * ROWS
    matrix = assemble(front_entries, child_blocks, child_map)

    corner_first = (blk == 0) & ((z == 0) | (z > 4))
    sent = scatter_x(matrix)
    across_x = forcing_x(forcing_core(rhs_index, rhs_values))
    sent, across_x = lax.optimization_barrier((sent, across_x))

    quarter = jnp.where(x == 0, matrix[:32], 0.0) + sent[0] + sent[1] + sent[2]
    sent = scatter_z(quarter)
    kept, came = forcing_rows(*across_x)
    sent, quarter, kept, came = lax.optimization_barrier((sent, quarter, kept, came))

    share = jnp.where(z < 2, quarter[:8], 0.0) + sent[0] + sent[1] + sent[2]
    width = share.shape[1] - HEAD
    excites = kept.shape[1]
    head, *near, far, left, head_own = local(
        message_kernel,
        (c, corner_first),
        (share, swap_core(share), kept, came),
        ((16, HEAD),)
        + ((16, width + 3 * ROWS),) * 3
        + ((8, width + 4 * ROWS), (2, excites, ROWS), (8, HEAD)),
    )
    head = rows_along_z([head] * 3, head_own)
    last = cube_send(near[2], lambda i, j, k: (i, j + 3 * sign(k), k))
    head, last, near, far, left = lax.optimization_barrier((head, last, near, far, left))

    head = stacked(head_own, *head)
    block = stacked(head, swap_core(head))
    head = (block, *gather_x(block, head))
    one, two, four = rows_along_z(near[:2], far)
    got = (one, two, last, four)
    head, got, far, left, pivot_inverse = lax.optimization_barrier(
        (head, got, far, left, pivot_inverse)
    )
    count = 64
    mine, ours, back = local(
        unpack_kernel,
        (c,),
        (far, *got, left),
        ((count, width), (2, excites, ROWS), (2, excites, ROWS)),
    )
    back = swap_core(back)
    block, forcing = local(
        tail_kernel,
        (c,),
        (mine, swap_core(mine), ours, back, group_order()),
        ((2 * count, width + ROWS), ours.shape[1:]),
    )
    side = cube_send(block, lambda i, j, k: (i + sign(k), j, k))

    ids = gathered_ids()
    head_side, head_far = head[1:]
    panel, factors, head = local(
        factors_kernel,
        (holder, start),
        (matrix[:, : 2 * WIDTH], pivot_inverse, ids, *head, swap_core(head_side), swap_core(head_far)),
        ((ROWS, 2 * WIDTH), (ROWS, 2 * WIDTH), (2 * WIDTH, HEAD)),
        flops=4 * 10**9,
    )
    side, panel = lax.optimization_barrier((side, panel))
    far = cube_send(side[:count], lambda i, j, k: (i + sign(k), j, k))
    turned_left, head_out = local(
        left_kernel,
        (holder, start, blk),
        (factors, *from_first(factors), pivot_inverse, ids, head, matrix[:, :HEAD], panel),
        ((2 * ROWS, 2 * WIDTH), (ROWS, HEAD)),
        flops=5 * 10**9,
    )
    body, change = local(
        own_kernel,
        (0,),
        (turned_left, matrix, block, side, far),
        ((ROWS, width), (ROWS, ROWS)),
        flops=5 * 10**9,
    )
    front, solved = local(
        final_kernel,
        (holder,),
        (turned_left, head_out, body, change, forcing, swap_core(side), swap_core(far)),
        (matrix.shape, forcing.shape),
        flops=10**9,
    )
    return front, solved


def solution(mesh):
    in_specs = (P("cube", "blk"), P("cube", "blk"), P(), P(), P("cube"), P("blk", "cube"))
    out_specs = (P("cube", "blk"), P("blk", "cube"))
    return jax.shard_map(shards, mesh=mesh, in_specs=in_specs, out_specs=out_specs, check_vma=False)
```

```python
import jax
import jax.numpy as jnp
import numpy as np
from jax import lax
from jax.experimental import pallas as pl
from jax.experimental.pallas import tpu as pltpu
from jax.sharding import PartitionSpec as P

NX, NZ, NC, NY = 4, 8, 2, 4
ROWS = 128
WIDTH = 256
HIGH = lax.Precision.HIGHEST


def dot(left, right):
    return jnp.dot(left, right, precision=HIGH, preferred_element_type=jnp.float32)


def after(value, *others):
    return lax.optimization_barrier((value, others))[0]


def cube_send(value, target):
    pairs = []
    for x in range(NX):
        for z in range(NZ):
            for c in range(NC):
                to = target(x, z, c)
                if to is not None:
                    tx, tz, tc = to
                    pairs.append(
                        ((x * NZ + z) * NC + c, ((tx % NX) * NZ + tz % NZ) * NC + tc % NC)
                    )
    return lax.ppermute(value, "cube", pairs)


def swap_core(value):
    return cube_send(value, lambda x, z, c: (x, z, 1 - c))


def place():
    rank = lax.axis_index("cube")
    return rank, rank >> 4, rank >> 1 & 7, rank & 1


def sign(core):
    return 1 - 2 * core


def local(kernel, place_scalars, arrays, shapes, flops=10**6):
    size = sum(4 * int(np.prod(shape)) for shape in shapes)
    return pl.pallas_call(
        kernel,
        out_shape=[jax.ShapeDtypeStruct(shape, jnp.float32) for shape in shapes],
        in_specs=[pl.BlockSpec(memory_space=pltpu.SMEM)]
        + [pl.BlockSpec(memory_space=pltpu.VMEM)] * len(arrays),
        out_specs=[pl.BlockSpec(memory_space=pltpu.VMEM)] * len(shapes),
        compiler_params=pltpu.CompilerParams(vmem_limit_bytes=40 * 2**20),
        cost_estimate=pl.CostEstimate(flops=flops, bytes_accessed=2 * size, transcendentals=0),
    )(jnp.stack([jnp.asarray(v, jnp.int32) for v in place_scalars]), *arrays)


def split(values):
    high = values.astype(jnp.bfloat16)
    rest = values - high.astype(jnp.float32)
    middle = rest.astype(jnp.bfloat16)
    return high, middle, (rest - middle.astype(jnp.float32)).astype(jnp.bfloat16)


def assemble_kernel(at_ref, front_ref, child_ref, came_ref, rows_ref, cols_ref, out_ref):
    parity, row_base, col_base = at_ref[0], at_ref[1], at_ref[2]
    count, width = came_ref.shape
    kept = child_ref[pl.ds(pl.multiple_of(parity * count, count), count), :]
    came = came_ref[...]
    even = parity == 0
    children = [jnp.where(even, kept, came), jnp.where(even, came, kept)]
    children = [jnp.concatenate(split(child), axis=0) for child in children]
    spots = lax.broadcasted_iota(jnp.int32, (ROWS, ROWS), 0) + row_base
    row_table = jnp.where(spots == rows_ref[...], 1.0, 0.0).astype(jnp.bfloat16)
    targets = lax.broadcasted_iota(jnp.int32, (2 * ROWS, ROWS), 0) + col_base
    for b in range(width // ROWS):
        span = slice(b * ROWS, (b + 1) * ROWS)
        out_span = slice(2 * b * ROWS, 2 * (b + 1) * ROWS)
        placed = []
        for k, child in enumerate(children):
            table = jnp.where(targets + 2 * b * ROWS == cols_ref[k : k + 1, span], 1.0, 0.0)
            parts = lax.dot_general(
                child[:, span],
                table.astype(jnp.bfloat16),
                (((1,), (1,)), ((), ())),
                preferred_element_type=jnp.float32,
            )
            placed.append(parts[:count] + (parts[count : 2 * count] + parts[2 * count :]))
        parts = jnp.concatenate(split(jnp.concatenate(placed, axis=0)), axis=1)
        sums = jnp.dot(row_table, parts, preferred_element_type=jnp.float32)
        size = 2 * ROWS
        sums = sums[:, :size] + (sums[:, size : 2 * size] + sums[:, 2 * size :])
        out_ref[:, out_span] = front_ref[:, out_span] + sums


def assemble(front_entries, child_blocks, child_map):
    rows_dev, front_cols = front_entries.shape
    child_cols = child_blocks.shape[1]
    half_rows = rows_dev // 2
    rank, _, _, parity = place()
    blk = lax.axis_index("blk")
    sent_rows = lax.dynamic_slice_in_dim(child_blocks, (1 - parity) * half_rows, half_rows)
    child_start = (rank >> 1) * rows_dev + parity * half_rows
    rows = lax.dynamic_slice(child_map, (0, child_start), (2, half_rows)).reshape(1, rows_dev)
    cols = lax.dynamic_slice(child_map, (0, blk * child_cols), (2, child_cols))
    return local(
        assemble_kernel,
        (parity, rank * rows_dev, blk * front_cols),
        (front_entries, child_blocks, swap_core(sent_rows), rows, cols),
        (front_entries.shape,),
        flops=10**9,
    )[0]


def dense_kernel(at_ref, index_ref, values_ref, kept_ref, sent_ref):
    x, c = at_ref[0], at_ref[1]
    s = sign(c)
    index = index_ref[...]
    values = values_ref[...]
    excites, entries = values.shape
    parts = jnp.concatenate(split(values), axis=0)
    chip = index >> 8

    def table(at, size):
        rows = lax.broadcasted_iota(jnp.int32, (size, entries), 0)
        return jnp.where(rows == at, 1.0, 0.0).astype(jnp.bfloat16)

    def summed(masks, place_table):
        rows = [parts * mask.astype(jnp.bfloat16) for mask in masks]
        placed = lax.dot_general(
            jnp.concatenate(rows, axis=0),
            place_table,
            (((1,), (1,)), ((), ())),
            preferred_element_type=jnp.float32,
        )
        placed = placed.reshape(len(masks), 3, excites, place_table.shape[0])
        return placed[:, 0] + (placed[:, 1] + placed[:, 2])

    def mask_of(condition):
        return jnp.broadcast_to(jnp.where(condition, 1.0, 0.0), (3 * excites, entries))

    near = table(index & 255, NC * ROWS)
    pivot = table((index >> 7 & 1) * 64 + (index >> 8) * 32 + (index & 31), ROWS)

    def blocks(at):
        sums = summed([mask_of(chip == at * NZ + z) for z in range(NZ)], near)
        held = (index < 2 * WIDTH) & (index >> 5 & 3 == at)
        return sums, summed([mask_of(held)], pivot)[0]

    for ref, at in ((kept_ref, x + s & 3), (sent_ref, x - s & 3)):
        sums, group = blocks(at)
        for z in range(NZ):
            ref[2 * z] = sums[z, :, :ROWS]
            ref[2 * z + 1] = sums[z, :, ROWS:]
        ref[2 * NZ] = group
    for start, at in ((17, x + 2 & 3), (26, x)):
        sums, group = blocks(at)
        for z in range(NZ):
            first, second = sums[z, :, :ROWS], sums[z, :, ROWS:]
            kept_ref[start + z] = jnp.where(c == 0, first, second)
            sent_ref[start + z] = jnp.where(c == 0, second, first)
        kept_ref[start + NZ] = jnp.where(c == 0, group, 0.0)
        sent_ref[start + NZ] = jnp.where(c == 0, 0.0, group)


def forcing_core(rhs_index, rhs_values):
    _, x, _, c = place()
    entries = rhs_values.shape[1]
    shape = (35, rhs_values.shape[0], ROWS)
    kept, sent = local(
        dense_kernel,
        (x, c),
        (rhs_index.reshape(1, entries), rhs_values),
        (shape, shape),
        flops=10**9,
    )
    return kept + swap_core(sent)


def forcing_x(summed):
    side = cube_send(summed[:17], lambda i, j, k: (i + sign(k), j, k))
    across = cube_send(summed[17:26], lambda i, j, k: (i + 2, j, k))
    return side, across, summed[26:]


def rows_kernel(at_ref, side_ref, across_ref, own_ref, kept_ref, sent_ref):
    z, c = at_ref[0], at_ref[1]
    s = sign(c)
    for ref, sgn in ((kept_ref, s), (sent_ref, -s)):
        for n in (1, 2, 3):
            i = z + n * sgn & 7
            for k in range(NC):
                mine = own_ref[i] + across_ref[i]
                ref[2 * n - 2 + k] = side_ref[2 * i + k] + jnp.where(c == k, mine, 0.0)
    for slot, i in ((6, z + 4 & 7), (7, z)):
        kept_ref[slot] = side_ref[2 * i + c] + (own_ref[i] + across_ref[i])
        sent_ref[slot] = side_ref[2 * i + 1 - c]
    pivot = side_ref[16] + (own_ref[8] + across_ref[8])
    kept_ref[8] = pivot
    sent_ref[8] = pivot


def forcing_rows(side, across, own):
    _, _, z, c = place()
    kept, sent = local(rows_kernel, (z, c), (side, across, own), (own.shape, own.shape))
    return kept, swap_core(sent)


def scatter_x(block):
    def target(d):
        return lambda i, j, k: ({0: d, d: 0}[i], j, k) if i in (0, d) and j < 2 else None

    return [cube_send(block[32 * d : 32 * d + 32], target(d)) for d in range(1, NX)]


def scatter_z(quarter):
    def target(d):
        to = {0: NZ - d, NZ - d: 0, 1: 1 + d, 1 + d: 1}
        return lambda i, j, k: (i, to[j], k) if j in to else None

    return [cube_send(quarter[8 * d : 8 * d + 8], target(d)) for d in range(1, NZ // 2)]


def stack_kernel(_, *refs):
    row = 0
    for ref in refs[:-1]:
        refs[-1][row : row + ref.shape[0]] = ref[...]
        row += ref.shape[0]


def stacked(*arrays):
    rows = sum(array.shape[0] for array in arrays)
    return local(stack_kernel, (0,), arrays, ((rows, arrays[0].shape[1]),))[0]


def message_kernel(at_ref, share_ref, other_ref, kept_ref, came_ref, *out_refs):
    c, turn = at_ref[0], at_ref[1]
    low = c == 0
    width = share_ref.shape[1]

    def columns(ref):
        left, right = ref[:, :WIDTH], ref[:, WIDTH : 2 * WIDTH]
        yield 0, jnp.where(turn == 1, right, left)
        yield WIDTH, jnp.where(turn == 1, left, right)
        yield 2 * WIDTH, ref[:, 2 * WIDTH :]

    summed = [kept_ref[i] + came_ref[i] for i in range(9)]
    for (at, mine), (_, other) in zip(columns(share_ref), columns(other_ref)):
        span = slice(at, at + mine.shape[1])
        for ref in out_refs[:3]:
            ref[:8, span] = jnp.where(low, mine, other)
            ref[8:, span] = jnp.where(low, other, mine)
        out_refs[3][:, span] = mine
    for n, ref in enumerate(out_refs[:3]):
        for i, block in enumerate((summed[2 * n], summed[2 * n + 1], summed[8])):
            ref[:, width + i * ROWS : width + (i + 1) * ROWS] = block
    first = jnp.where(low, summed[8], 0.0)
    for i, block in enumerate((summed[6][:8], summed[6][8:], first[:8], first[8:])):
        out_refs[3][:, width + i * ROWS : width + (i + 1) * ROWS] = block
    out_refs[4][0] = summed[7]
    out_refs[4][1] = first


def unpack_kernel(at_ref, own_ref, one_ref, two_ref, three_ref, far_ref, left_ref, *out_refs):
    low = at_ref[0] == 0
    head_ref, tail_ref, mine_ref, back_ref = out_refs
    width = WIDTH + tail_ref.shape[1]
    row = 0
    for ref in (own_ref, one_ref, two_ref, three_ref, far_ref):
        count = ref.shape[0]
        head_ref[row : row + count] = ref[:, :WIDTH]
        tail_ref[row : row + count] = ref[:, WIDTH:width]
        row += count
    spans = [slice(width + i * ROWS, width + (i + 1) * ROWS) for i in range(4)]
    sums = [one_ref[:, at] + two_ref[:, at] + three_ref[:, at] for at in spans[:3]]
    far = [far_ref[:, at] for at in spans]
    mine_ref[0] = (
        jnp.where(low, sums[0], sums[1])
        + jnp.concatenate([far[0], far[1]], axis=0)
        + left_ref[0]
    )
    pivot = sums[2] + jnp.concatenate([far[2], far[3]], axis=0) + left_ref[1]
    mine_ref[1] = pivot
    back_ref[0] = jnp.where(low, sums[1], sums[0])
    back_ref[1] = pivot


def gather_z(share, kept, came, corner_first):
    c = lax.axis_index("cube") & 1
    width = share.shape[1]
    excites = kept.shape[1]
    near = (2 * excites // 2, width + 3 * ROWS)
    *messages, left = local(
        message_kernel,
        (c, corner_first),
        (share, swap_core(share), kept, came),
        (near, near, near, (8, width + 4 * ROWS), (2, excites, ROWS)),
    )
    got = [
        cube_send(messages[n - 1], lambda i, j, k: (i, j + n * sign(k), k)) for n in (1, 2, 3)
    ]
    far = cube_send(messages[3], lambda i, j, k: (i, j + 4, k))
    head, tail, mine, back = local(
        unpack_kernel,
        (c,),
        (messages[3], *got, far, left),
        ((64, WIDTH), (64, width - WIDTH), (2, excites, ROWS), (2, excites, ROWS)),
    )
    return head, tail, mine, swap_core(back)


def tail_kernel(at_ref, mine_ref, theirs_ref, ours_ref, back_ref, order_ref, *out_refs):
    all_ref, forcing_ref = out_refs
    count, width = mine_ref.shape
    forcing_ref[...] = ours_ref[0] + back_ref[0]
    pivots = ours_ref[1] + back_ref[1]
    excites = pivots.shape[0]
    spots = lax.broadcasted_iota(jnp.int32, (ROWS, ROWS), 0)
    table = jnp.where(spots == order_ref[...], 1.0, 0.0)
    ordered = dot(pivots, table)
    filler = jnp.zeros((ROWS - excites, ROWS), jnp.float32)
    columns = jnp.concatenate([ordered, filler], axis=0).T
    all_ref[:count, :width] = mine_ref[...]
    all_ref[count:, :width] = theirs_ref[...]
    all_ref[:, width:] = columns


def gather_x(block, mine):
    side = cube_send(block, lambda i, j, k: (i + sign(k), j, k))
    far = cube_send(mine, lambda i, j, k: (i + 2, j, k))
    return side, far


def rows_8(dx, dz, core):
    return [(*dx, *dz, core, r) for r in range(8)]


def rows_64(dx, flip):
    s = -1 if flip else 1
    out = rows_8(dx, (0, 0), 2 + flip)
    for n in (1, 2, 3):
        out += rows_8(dx, (-n * s, 0), 0) + rows_8(dx, (-n * s, 0), 1)
    return out + rows_8(dx, (0, 4), 2 + flip)


def rows_128(dx, flip):
    return rows_64(dx, flip) + rows_64(dx, 1 - flip)


def row_ids(rows):
    _, x, z, c = place()
    s = sign(c)
    xs, x0, zs, z0, core, r = (np.array(v, np.int32)[None] for v in zip(*rows))
    at_x = x + xs * s + x0 & 3
    at_z = z + zs * s + z0 & 7
    core = jnp.where(core > 1, c ^ (core - 2), core)
    lower = (at_z == 0) | (at_z > 4)
    pos = jnp.where(lower, 8 - at_z & 7, at_z - 1)
    return (jnp.where(lower, 0, NC) + core) * ROWS + at_x * 32 + pos * 8 + r


def gathered_ids():
    return row_ids(
        rows_128((0, 0), 0)
        + rows_128((-1, 0), 0)
        + rows_64((0, 2), 0)
        + rows_128((1, 0), 1)
        + rows_64((0, 2), 1)
    )


def group_order():
    ids = row_ids(rows_128((0, 0), 0))
    return (ids >> 7 & 1) * 64 + (ids >> 8) * 32 + (ids & 31)


def local_table(ids, first, count):
    rows = lax.broadcasted_iota(jnp.int32, (count, ids.shape[1]), 0) + first
    return jnp.where(rows == ids, 1.0, 0.0)


def factors_kernel(
    at_ref, panel_ref, pivots_ref, ids_ref, block_ref, side_ref, far_ref, side2_ref, far2_ref,
    out_ref, factors_ref, head_ref
):
    holder, start = at_ref[0], at_ref[1]
    two = holder == 2
    row = 0
    for ref in (block_ref, side_ref, far_ref, side2_ref, far2_ref):
        head_ref[row : row + ref.shape[0]] = ref[...]
        row += ref.shape[0]
    head = head_ref[...]
    ids = ids_ref[...]
    left, right = panel_ref[:, :WIDTH], panel_ref[:, WIDTH:]
    first, second = pivots_ref[0], pivots_ref[1]
    l1 = dot(left, first)
    reduced = right - dot(dot(l1, local_table(ids, 0, WIDTH)), head)
    l2 = dot(reduced, second)
    start = pl.multiple_of(start, ROWS)
    lead = jnp.where(two, pivots_ref[1, pl.ds(start, ROWS), :], l2)
    back = dot(dot(dot(lead, local_table(ids, WIDTH, WIDTH)), head), first)
    out_ref[:, :WIDTH] = jnp.where(holder == 1, left, l1)
    out_ref[:, WIDTH:] = jnp.where(holder == 1, right, jnp.where(two, reduced, l2))
    factors_ref[:, :WIDTH] = jnp.where(two, l1, l1 - back)
    factors_ref[:, WIDTH:] = jnp.where(two, back, l2)


def left_kernel(
    at_ref, own_ref, one_ref, two_ref, three_ref, pivots_ref, ids_ref, head_ref, matrix_ref,
    panel_ref, turned_ref, out_ref
):
    holder, start, blk = at_ref[0], at_ref[1], at_ref[2]
    one, two = holder == 1, holder == 2
    factors = own_ref[...]
    for d, ref in enumerate((one_ref, two_ref, three_ref)):
        factors = jnp.where(blk == d + 1, ref[...], factors)
    first, second = factors[:, :WIDTH], factors[:, WIDTH:]
    start = pl.multiple_of(start, ROWS)
    pick_one = pivots_ref[0, pl.ds(start, ROWS), :]
    pick_two = pivots_ref[1, pl.ds(start, ROWS), :]
    lead = jnp.concatenate(
        [
            jnp.where(one, 0.0, first),
            jnp.where(one, -pick_one, jnp.where(two, second, first)),
        ],
        axis=0,
    )
    rest = jnp.concatenate(
        [
            jnp.where(holder > 0, 0.0, second),
            jnp.where(one, 0.0, jnp.where(two, -pick_two, second)),
        ],
        axis=0,
    )
    ids = ids_ref[...]
    turned = dot(lead, local_table(ids, 0, WIDTH)) + dot(rest, local_table(ids, WIDTH, WIDTH))
    turned_ref[...] = turned
    change = dot(turned[:ROWS], head_ref[...])
    out_ref[...] = jnp.where(blk == 0, panel_ref[...], matrix_ref[...] - change)


def halves(values):
    high = values.astype(jnp.bfloat16)
    return high, (values - high.astype(jnp.float32)).astype(jnp.bfloat16)


def dot3(left, rows):
    (high, low), (rows_high, rows_low) = left, halves(rows)
    count = high.shape[0]
    both = jnp.dot(
        jnp.concatenate([high, low], axis=0), rows_high, preferred_element_type=jnp.float32
    )
    rest = jnp.dot(high, rows_low, preferred_element_type=jnp.float32)
    return both[:count] + (both[count:] + rest)


def own_kernel(at_ref, left_ref, matrix_ref, block_ref, side_ref, body_ref, change_ref):
    width = body_ref.shape[1]
    rows = jnp.concatenate([block_ref[...], side_ref[...]], axis=0)
    cut = rows.shape[0]
    front, forcing = halves(left_ref[:ROWS, :cut]), halves(left_ref[ROWS:, :cut])
    for at in range(0, width, WIDTH):
        span = slice(at, at + WIDTH)
        change = dot3(front, rows[:, span])
        body_ref[:, span] = matrix_ref[:, WIDTH + at : 2 * WIDTH + at] - change
    change_ref[...] = dot3(forcing, rows[:, width:])


def final_kernel(
    at_ref, left_ref, head_ref, panel_ref, body_ref, change_ref, forcing_ref, far_ref, side2_ref,
    far2_ref, front_ref, solved_ref
):
    holder, blk = at_ref[0], at_ref[1]
    width = body_ref.shape[1]
    rows = jnp.concatenate([far_ref[...], side2_ref[...], far2_ref[...]], axis=0)
    cut = left_ref.shape[1] - rows.shape[0]
    front, forcing = halves(left_ref[:ROWS, cut:]), halves(left_ref[ROWS:, cut:])
    for at in range(0, width, WIDTH):
        span = slice(at, at + WIDTH)
        value = body_ref[:, span] - dot3(front, rows[:, span])
        if at == 0:
            value = jnp.where(blk == 0, panel_ref[:, WIDTH:], value)
        front_ref[:, WIDTH + at : 2 * WIDTH + at] = value
    front_ref[:, :WIDTH] = head_ref[...]
    change = change_ref[...] + dot3(forcing, rows[:, width:])
    kept = jnp.where(holder > 0, 0.0, forcing_ref[...])
    solved_ref[...] = kept - change.T[: kept.shape[0]]


def from_first(value):
    return [
        lax.ppermute(value, "blk", [(i, (i + d) % NY) for i in range(NY)]) for d in range(1, NY)
    ]


def shards(front_entries, child_blocks, child_map, pivot_inverse, rhs_index, rhs_values):
    rank, x, z, c = place()
    blk = lax.axis_index("blk")
    holder = jnp.where(rank < 2, 1, jnp.where(rank < 4, 2, 0))
    start = (rank & 1) * ROWS
    matrix = assemble(front_entries, child_blocks, child_map)

    corner_first = (blk == 0) & ((z == 0) | (z > 4))
    sent = scatter_x(matrix)
    across_x = forcing_x(forcing_core(rhs_index, rhs_values))
    sent, across_x = lax.optimization_barrier((sent, across_x))

    quarter = jnp.where(x == 0, matrix[:32], sent[0] + sent[1] + sent[2])
    sent = scatter_z(quarter)
    kept, came = forcing_rows(*across_x)
    sent, quarter, kept, came = lax.optimization_barrier((sent, quarter, kept, came))

    share = jnp.where(z < 2, quarter[:8], sent[0] + sent[1] + sent[2])
    head, mine, ours, back = gather_z(share, kept, came, corner_first)
    head, mine, pivot_inverse = lax.optimization_barrier((head, mine, pivot_inverse))

    block = stacked(head, swap_core(head))
    head = (block, *gather_x(block, head))
    count, width = mine.shape
    excites = ours.shape[1]
    block, forcing = local(
        tail_kernel,
        (c,),
        (mine, swap_core(mine), ours, back, group_order()),
        ((2 * count, width + ROWS), ours.shape[1:]),
    )
    head, block = lax.optimization_barrier((head, block))
    side = cube_send(block, lambda i, j, k: (i + sign(k), j, k))

    ids = gathered_ids()
    head_side, head_far = head[1:]
    panel, factors, head = local(
        factors_kernel,
        (holder, start),
        (matrix[:, : 2 * WIDTH], pivot_inverse, ids, *head, swap_core(head_side), swap_core(head_far)),
        ((ROWS, 2 * WIDTH), (ROWS, 2 * WIDTH), (2 * WIDTH, WIDTH)),
        flops=4 * 10**9,
    )
    side, panel = lax.optimization_barrier((side, panel))
    far = cube_send(side[:count], lambda i, j, k: (i + sign(k), j, k))
    turned_left, head_out = local(
        left_kernel,
        (holder, start, blk),
        (factors, *from_first(factors), pivot_inverse, ids, head, matrix[:, :WIDTH], panel[:, :WIDTH]),
        ((2 * ROWS, 2 * WIDTH), (ROWS, WIDTH)),
        flops=5 * 10**9,
    )
    body, change = local(
        own_kernel,
        (0,),
        (turned_left, matrix, block, side),
        ((ROWS, width), (ROWS, ROWS)),
        flops=10 * 10**9,
    )
    front, solved = local(
        final_kernel,
        (holder, blk),
        (turned_left, head_out, panel, body, change, forcing, far, swap_core(side), swap_core(far)),
        (matrix.shape, forcing.shape),
        flops=1 * 10**9,
    )
    return front, solved


def solution(mesh):
    in_specs = (P("cube", "blk"), P("cube", "blk"), P(), P(), P("cube"), P("blk", "cube"))
    out_specs = (P("cube", "blk"), P("blk", "cube"))
    return jax.shard_map(shards, mesh=mesh, in_specs=in_specs, out_specs=out_specs, check_vma=False)
```

```python
import jax
import jax.numpy as jnp
import numpy as np
from jax import lax
from jax.experimental import pallas as pl
from jax.experimental.pallas import tpu as pltpu
from jax.sharding import PartitionSpec as P

NX, NZ, NC, NY = 4, 8, 2, 4
ROWS = 128
WIDTH = 256
HIGH = lax.Precision.HIGHEST


def dot(left, right):
    return jnp.dot(left, right, precision=HIGH, preferred_element_type=jnp.float32)


def after(value, *others):
    return lax.optimization_barrier((value, others))[0]


def cube_send(value, target):
    pairs = []
    for x in range(NX):
        for z in range(NZ):
            for c in range(NC):
                to = target(x, z, c)
                if to is not None:
                    tx, tz, tc = to
                    pairs.append(
                        ((x * NZ + z) * NC + c, ((tx % NX) * NZ + tz % NZ) * NC + tc % NC)
                    )
    return lax.ppermute(value, "cube", pairs)


def swap_core(value):
    return cube_send(value, lambda x, z, c: (x, z, 1 - c))


def place():
    rank = lax.axis_index("cube")
    return rank, rank >> 4, rank >> 1 & 7, rank & 1


def sign(core):
    return 1 - 2 * core


def local(kernel, place_scalars, arrays, shapes, flops=10**6):
    size = sum(4 * int(np.prod(shape)) for shape in shapes)
    return pl.pallas_call(
        kernel,
        out_shape=[jax.ShapeDtypeStruct(shape, jnp.float32) for shape in shapes],
        in_specs=[pl.BlockSpec(memory_space=pltpu.SMEM)]
        + [pl.BlockSpec(memory_space=pltpu.VMEM)] * len(arrays),
        out_specs=[pl.BlockSpec(memory_space=pltpu.VMEM)] * len(shapes),
        compiler_params=pltpu.CompilerParams(vmem_limit_bytes=40 * 2**20),
        cost_estimate=pl.CostEstimate(flops=flops, bytes_accessed=2 * size, transcendentals=0),
    )(jnp.stack([jnp.asarray(v, jnp.int32) for v in place_scalars]), *arrays)


def split(values):
    high = values.astype(jnp.bfloat16)
    rest = values - high.astype(jnp.float32)
    middle = rest.astype(jnp.bfloat16)
    return high, middle, (rest - middle.astype(jnp.float32)).astype(jnp.bfloat16)


def assemble_kernel(at_ref, front_ref, child_ref, came_ref, rows_ref, cols_ref, out_ref):
    parity, row_base, col_base = at_ref[0], at_ref[1], at_ref[2]
    count, width = came_ref.shape
    kept = child_ref[pl.ds(pl.multiple_of(parity * count, count), count), :]
    came = came_ref[...]
    even = parity == 0
    children = [jnp.where(even, kept, came), jnp.where(even, came, kept)]
    children = [jnp.concatenate(split(child), axis=0) for child in children]
    spots = lax.broadcasted_iota(jnp.int32, (ROWS, ROWS), 0) + row_base
    row_table = jnp.where(spots == rows_ref[...], 1.0, 0.0).astype(jnp.bfloat16)
    targets = lax.broadcasted_iota(jnp.int32, (2 * ROWS, ROWS), 0) + col_base
    for b in range(width // ROWS):
        span = slice(b * ROWS, (b + 1) * ROWS)
        out_span = slice(2 * b * ROWS, 2 * (b + 1) * ROWS)
        placed = []
        for k, child in enumerate(children):
            table = jnp.where(targets + 2 * b * ROWS == cols_ref[k : k + 1, span], 1.0, 0.0)
            parts = lax.dot_general(
                child[:, span],
                table.astype(jnp.bfloat16),
                (((1,), (1,)), ((), ())),
                preferred_element_type=jnp.float32,
            )
            placed.append(parts[:count] + (parts[count : 2 * count] + parts[2 * count :]))
        parts = jnp.concatenate(split(jnp.concatenate(placed, axis=0)), axis=1)
        sums = jnp.dot(row_table, parts, preferred_element_type=jnp.float32)
        size = 2 * ROWS
        sums = sums[:, :size] + (sums[:, size : 2 * size] + sums[:, 2 * size :])
        out_ref[:, out_span] = front_ref[:, out_span] + sums


def assemble(front_entries, child_blocks, child_map):
    rows_dev, front_cols = front_entries.shape
    child_cols = child_blocks.shape[1]
    half_rows = rows_dev // 2
    rank, _, _, parity = place()
    blk = lax.axis_index("blk")
    sent_rows = lax.dynamic_slice_in_dim(child_blocks, (1 - parity) * half_rows, half_rows)
    child_start = (rank >> 1) * rows_dev + parity * half_rows
    rows = lax.dynamic_slice(child_map, (0, child_start), (2, half_rows)).reshape(1, rows_dev)
    cols = lax.dynamic_slice(child_map, (0, blk * child_cols), (2, child_cols))
    return local(
        assemble_kernel,
        (parity, rank * rows_dev, blk * front_cols),
        (front_entries, child_blocks, swap_core(sent_rows), rows, cols),
        (front_entries.shape,),
        flops=10**9,
    )[0]


def dense_kernel(at_ref, index_ref, values_ref, kept_ref, sent_ref):
    x, c = at_ref[0], at_ref[1]
    s = sign(c)
    index = index_ref[...]
    values = values_ref[...]
    excites, entries = values.shape
    parts = jnp.concatenate(split(values), axis=0)
    chip = index >> 8

    def table(at, size):
        rows = lax.broadcasted_iota(jnp.int32, (size, entries), 0)
        return jnp.where(rows == at, 1.0, 0.0).astype(jnp.bfloat16)

    def summed(masks, place_table):
        rows = [parts * mask.astype(jnp.bfloat16) for mask in masks]
        placed = lax.dot_general(
            jnp.concatenate(rows, axis=0),
            place_table,
            (((1,), (1,)), ((), ())),
            preferred_element_type=jnp.float32,
        )
        placed = placed.reshape(len(masks), 3, excites, place_table.shape[0])
        return placed[:, 0] + (placed[:, 1] + placed[:, 2])

    def mask_of(condition):
        return jnp.broadcast_to(jnp.where(condition, 1.0, 0.0), (3 * excites, entries))

    near = table(index & 255, NC * ROWS)
    pivot = table((index >> 7 & 1) * 64 + (index >> 8) * 32 + (index & 31), ROWS)

    def blocks(at):
        sums = summed([mask_of(chip == at * NZ + z) for z in range(NZ)], near)
        held = (index < 2 * WIDTH) & (index >> 5 & 3 == at)
        return sums, summed([mask_of(held)], pivot)[0]

    for ref, at in ((kept_ref, x + s & 3), (sent_ref, x - s & 3)):
        sums, group = blocks(at)
        for z in range(NZ):
            ref[2 * z] = sums[z, :, :ROWS]
            ref[2 * z + 1] = sums[z, :, ROWS:]
        ref[2 * NZ] = group
    for start, at in ((17, x + 2 & 3), (26, x)):
        sums, group = blocks(at)
        for z in range(NZ):
            first, second = sums[z, :, :ROWS], sums[z, :, ROWS:]
            kept_ref[start + z] = jnp.where(c == 0, first, second)
            sent_ref[start + z] = jnp.where(c == 0, second, first)
        kept_ref[start + NZ] = jnp.where(c == 0, group, 0.0)
        sent_ref[start + NZ] = jnp.where(c == 0, 0.0, group)


def forcing_core(rhs_index, rhs_values):
    _, x, _, c = place()
    entries = rhs_values.shape[1]
    shape = (35, rhs_values.shape[0], ROWS)
    kept, sent = local(
        dense_kernel,
        (x, c),
        (rhs_index.reshape(1, entries), rhs_values),
        (shape, shape),
        flops=10**9,
    )
    return kept + swap_core(sent)


def forcing_x(summed):
    side = cube_send(summed[:17], lambda i, j, k: (i + sign(k), j, k))
    across = cube_send(summed[17:26], lambda i, j, k: (i + 2, j, k))
    return side, across, summed[26:]


def rows_kernel(at_ref, side_ref, across_ref, own_ref, kept_ref, sent_ref):
    z, c = at_ref[0], at_ref[1]
    s = sign(c)
    for ref, sgn in ((kept_ref, s), (sent_ref, -s)):
        for n in (1, 2, 3):
            i = z + n * sgn & 7
            for k in range(NC):
                mine = own_ref[i] + across_ref[i]
                ref[2 * n - 2 + k] = side_ref[2 * i + k] + jnp.where(c == k, mine, 0.0)
    for slot, i in ((6, z + 4 & 7), (7, z)):
        kept_ref[slot] = side_ref[2 * i + c] + (own_ref[i] + across_ref[i])
        sent_ref[slot] = side_ref[2 * i + 1 - c]
    pivot = side_ref[16] + (own_ref[8] + across_ref[8])
    kept_ref[8] = pivot
    sent_ref[8] = pivot


def forcing_rows(side, across, own):
    _, _, z, c = place()
    kept, sent = local(rows_kernel, (z, c), (side, across, own), (own.shape, own.shape))
    return kept, swap_core(sent)


def scatter_x(block):
    return [
        cube_send(
            block[32 * d : 32 * d + 32],
            lambda i, j, k: (d, j, k) if i == 0 and j < 2 else None,
        )
        for d in range(1, NX)
    ]


def scatter_z(quarter):
    return [
        cube_send(
            quarter[8 * d : 8 * d + 8],
            lambda i, j, k: (i, (-d if j == 0 else 1 + d), k) if j < 2 else None,
        )
        for d in range(1, NZ // 2)
    ]


def message_kernel(at_ref, share_ref, other_ref, kept_ref, came_ref, *out_refs):
    c, turn = at_ref[0], at_ref[1]
    low = c == 0
    width = share_ref.shape[1]

    def columns(ref):
        left, right = ref[:, :WIDTH], ref[:, WIDTH : 2 * WIDTH]
        yield 0, jnp.where(turn == 1, right, left)
        yield WIDTH, jnp.where(turn == 1, left, right)
        yield 2 * WIDTH, ref[:, 2 * WIDTH :]

    summed = [kept_ref[i] + came_ref[i] for i in range(9)]
    for (at, mine), (_, other) in zip(columns(share_ref), columns(other_ref)):
        span = slice(at, at + mine.shape[1])
        for ref in out_refs[:3]:
            ref[:8, span] = jnp.where(low, mine, other)
            ref[8:, span] = jnp.where(low, other, mine)
        out_refs[3][:, span] = mine
    for n, ref in enumerate(out_refs[:3]):
        for i, block in enumerate((summed[2 * n], summed[2 * n + 1], summed[8])):
            ref[:, width + i * ROWS : width + (i + 1) * ROWS] = block
    first = jnp.where(low, summed[8], 0.0)
    for i, block in enumerate((summed[6][:8], summed[6][8:], first[:8], first[8:])):
        out_refs[3][:, width + i * ROWS : width + (i + 1) * ROWS] = block
    out_refs[4][0] = summed[7]
    out_refs[4][1] = first


def unpack_kernel(at_ref, own_ref, one_ref, two_ref, three_ref, far_ref, left_ref, *out_refs):
    low = at_ref[0] == 0
    head_ref, tail_ref, mine_ref, back_ref = out_refs
    width = WIDTH + tail_ref.shape[1]
    row = 0
    for ref in (own_ref, one_ref, two_ref, three_ref, far_ref):
        count = ref.shape[0]
        head_ref[row : row + count] = ref[:, :WIDTH]
        tail_ref[row : row + count] = ref[:, WIDTH:width]
        row += count
    spans = [slice(width + i * ROWS, width + (i + 1) * ROWS) for i in range(4)]
    sums = [one_ref[:, at] + two_ref[:, at] + three_ref[:, at] for at in spans[:3]]
    far = [far_ref[:, at] for at in spans]
    mine_ref[0] = (
        jnp.where(low, sums[0], sums[1])
        + jnp.concatenate([far[0], far[1]], axis=0)
        + left_ref[0]
    )
    pivot = sums[2] + jnp.concatenate([far[2], far[3]], axis=0) + left_ref[1]
    mine_ref[1] = pivot
    back_ref[0] = jnp.where(low, sums[1], sums[0])
    back_ref[1] = pivot


def gather_z(share, kept, came, corner_first):
    c = lax.axis_index("cube") & 1
    width = share.shape[1]
    excites = kept.shape[1]
    near = (2 * excites // 2, width + 3 * ROWS)
    *messages, left = local(
        message_kernel,
        (c, corner_first),
        (share, swap_core(share), kept, came),
        (near, near, near, (8, width + 4 * ROWS), (2, excites, ROWS)),
    )
    got = [
        cube_send(messages[n - 1], lambda i, j, k: (i, j + n * sign(k), k)) for n in (1, 2, 3)
    ]
    far = cube_send(messages[3], lambda i, j, k: (i, j + 4, k))
    head, tail, mine, back = local(
        unpack_kernel,
        (c,),
        (messages[3], *got, far, left),
        ((64, WIDTH), (64, width - WIDTH), (2, excites, ROWS), (2, excites, ROWS)),
    )
    return head, tail, mine, swap_core(back)


def tail_kernel(at_ref, mine_ref, theirs_ref, ours_ref, back_ref, order_ref, *out_refs):
    all_ref, forcing_ref = out_refs
    count, width = mine_ref.shape
    forcing_ref[...] = ours_ref[0] + back_ref[0]
    pivots = ours_ref[1] + back_ref[1]
    excites = pivots.shape[0]
    spots = lax.broadcasted_iota(jnp.int32, (ROWS, ROWS), 0)
    table = jnp.where(spots == order_ref[...], 1.0, 0.0)
    ordered = dot(pivots, table)
    filler = jnp.zeros((ROWS - excites, ROWS), jnp.float32)
    columns = jnp.concatenate([ordered, filler], axis=0).T
    all_ref[:count, :width] = mine_ref[...]
    all_ref[count:, :width] = theirs_ref[...]
    all_ref[:, width:] = columns


def rows_8(dx, dz, core):
    return [(*dx, *dz, core, r) for r in range(8)]


def rows_64(dx, flip):
    s = -1 if flip else 1
    out = rows_8(dx, (0, 0), 2 + flip)
    for n in (1, 2, 3):
        out += rows_8(dx, (-n * s, 0), 0) + rows_8(dx, (-n * s, 0), 1)
    return out + rows_8(dx, (0, 4), 2 + flip)


def rows_128(dx, flip):
    return rows_64(dx, flip) + rows_64(dx, 1 - flip)


def row_ids(rows):
    _, x, z, c = place()
    s = sign(c)
    xs, x0, zs, z0, core, r = (np.array(v, np.int32)[None] for v in zip(*rows))
    at_x = x + xs * s + x0 & 3
    at_z = z + zs * s + z0 & 7
    core = jnp.where(core > 1, c ^ (core - 2), core)
    lower = (at_z == 0) | (at_z > 4)
    pos = jnp.where(lower, 8 - at_z & 7, at_z - 1)
    return (jnp.where(lower, 0, NC) + core) * ROWS + at_x * 32 + pos * 8 + r


def head_ids():
    return row_ids(
        sum((rows_64((0, dx), flip) for flip in range(NC) for dx in (0, -1, 1, 2)), [])
    )


def tail_ids():
    return row_ids(
        rows_128((0, 0), 0)
        + rows_128((-1, 0), 0)
        + rows_64((0, 2), 0)
        + rows_128((1, 0), 1)
        + rows_64((0, 2), 1)
    )


def group_order():
    ids = row_ids(rows_128((0, 0), 0))
    return (ids >> 7 & 1) * 64 + (ids >> 8) * 32 + (ids & 31)


def spread(values, ids, first):
    count, width = values.shape
    rows = lax.broadcasted_iota(jnp.int32, (width, ids.shape[1]), 0) + first
    table = jnp.where(rows == ids, 1.0, 0.0).astype(jnp.bfloat16)
    parts = jnp.dot(
        jnp.concatenate(split(values), axis=0), table, preferred_element_type=jnp.float32
    )
    return parts[:count] + (parts[count : 2 * count] + parts[2 * count :])


def factors_kernel(
    at_ref, panel_ref, pivots_ref, ids_ref, a_ref, b_ref, c_ref, d_ref, other_ref,
    out_ref, factors_ref, head_ref
):
    holder, start = at_ref[0], at_ref[1]
    two = holder == 2
    row = 0
    for ref in (a_ref, b_ref, c_ref, d_ref, other_ref):
        head_ref[row : row + ref.shape[0]] = ref[...]
        row += ref.shape[0]
    head = head_ref[...]
    ids = ids_ref[...]
    left, right = panel_ref[:, :WIDTH], panel_ref[:, WIDTH:]
    first, second = pivots_ref[0], pivots_ref[1]
    l1 = dot(left, first)
    reduced = right - dot(spread(l1, ids, 0), head)
    l2 = dot(reduced, second)
    start = pl.multiple_of(start, ROWS)
    lead = jnp.where(two, pivots_ref[1, pl.ds(start, ROWS), :], l2)
    back = dot(dot(spread(lead, ids, WIDTH), head), first)
    out_ref[:, :WIDTH] = jnp.where(holder == 1, left, l1)
    out_ref[:, WIDTH:] = jnp.where(holder == 1, right, jnp.where(two, reduced, l2))
    factors_ref[:, :WIDTH] = jnp.where(two, l1, l1 - back)
    factors_ref[:, WIDTH:] = jnp.where(two, back, l2)


def left_kernel(
    at_ref, own_ref, one_ref, two_ref, three_ref, pivots_ref, ids_ref, head_ids_ref, head_ref,
    matrix_ref, panel_ref, turned_ref, out_ref
):
    holder, start, blk = at_ref[0], at_ref[1], at_ref[2]
    one, two = holder == 1, holder == 2
    factors = own_ref[...]
    for d, ref in enumerate((one_ref, two_ref, three_ref)):
        factors = jnp.where(blk == d + 1, ref[...], factors)
    first, second = factors[:, :WIDTH], factors[:, WIDTH:]
    start = pl.multiple_of(start, ROWS)
    pick_one = pivots_ref[0, pl.ds(start, ROWS), :]
    pick_two = pivots_ref[1, pl.ds(start, ROWS), :]
    front = jnp.where(one, 0.0, first), jnp.where(holder > 0, 0.0, second)
    forcing = (
        jnp.where(one, -pick_one, jnp.where(two, second, first)),
        jnp.where(one, 0.0, jnp.where(two, -pick_two, second)),
    )
    ids = ids_ref[...]
    lead = jnp.concatenate([front[0], forcing[0]], axis=0)
    rest = jnp.concatenate([front[1], forcing[1]], axis=0)
    turned_ref[...] = spread(lead, ids, 0) + spread(rest, ids, WIDTH)
    ids = head_ids_ref[...]
    turned = spread(front[0], ids, 0) + spread(front[1], ids, WIDTH)
    change = dot3(halves(turned), head_ref[...])
    out_ref[...] = jnp.where(blk == 0, panel_ref[...], matrix_ref[...] - change)


def halves(values):
    high = values.astype(jnp.bfloat16)
    return high, (values - high.astype(jnp.float32)).astype(jnp.bfloat16)


def dot3(left, rows):
    (high, low), (rows_high, rows_low) = left, halves(rows)
    count = high.shape[0]
    both = jnp.dot(
        jnp.concatenate([high, low], axis=0), rows_high, preferred_element_type=jnp.float32
    )
    rest = jnp.dot(high, rows_low, preferred_element_type=jnp.float32)
    return both[:count] + (both[count:] + rest)


def own_kernel(at_ref, left_ref, matrix_ref, block_ref, side_ref, body_ref, change_ref):
    width = body_ref.shape[1]
    rows = jnp.concatenate([block_ref[...], side_ref[...]], axis=0)
    cut = rows.shape[0]
    front, forcing = halves(left_ref[:ROWS, :cut]), halves(left_ref[ROWS:, :cut])
    for at in range(0, width, WIDTH):
        span = slice(at, at + WIDTH)
        change = dot3(front, rows[:, span])
        body_ref[:, span] = matrix_ref[:, WIDTH + at : 2 * WIDTH + at] - change
    change_ref[...] = dot3(forcing, rows[:, width:])


def final_kernel(
    at_ref, left_ref, head_ref, panel_ref, body_ref, change_ref, forcing_ref, far_ref, side2_ref,
    far2_ref, front_ref, solved_ref
):
    holder, blk = at_ref[0], at_ref[1]
    width = body_ref.shape[1]
    rows = jnp.concatenate([far_ref[...], side2_ref[...], far2_ref[...]], axis=0)
    cut = left_ref.shape[1] - rows.shape[0]
    front, forcing = halves(left_ref[:ROWS, cut:]), halves(left_ref[ROWS:, cut:])
    for at in range(0, width, WIDTH):
        span = slice(at, at + WIDTH)
        value = body_ref[:, span] - dot3(front, rows[:, span])
        if at == 0:
            value = jnp.where(blk == 0, panel_ref[:, WIDTH:], value)
        front_ref[:, WIDTH + at : 2 * WIDTH + at] = value
    front_ref[:, :WIDTH] = head_ref[...]
    change = change_ref[...] + dot3(forcing, rows[:, width:])
    kept = jnp.where(holder > 0, 0.0, forcing_ref[...])
    solved_ref[...] = kept - change.T[: kept.shape[0]]


def from_first(value):
    return [
        lax.ppermute(value, "blk", [(i, (i + d) % NY) for i in range(NY)]) for d in range(1, NY)
    ]


def shards(front_entries, child_blocks, child_map, pivot_inverse, rhs_index, rhs_values):
    rank, x, z, c = place()
    blk = lax.axis_index("blk")
    holder = jnp.where(rank < 2, 1, jnp.where(rank < 4, 2, 0))
    start = (rank & 1) * ROWS
    matrix = assemble(front_entries, child_blocks, child_map)

    corner_first = (blk == 0) & ((z == 0) | (z > 4))
    sent = scatter_x(matrix)
    across_x = forcing_x(forcing_core(rhs_index, rhs_values))
    sent, across_x = lax.optimization_barrier((sent, across_x))

    quarter = jnp.where(x == 0, matrix[:32], sent[0] + sent[1] + sent[2])
    sent = scatter_z(quarter)
    kept, came = forcing_rows(*across_x)
    sent, quarter, kept, came = lax.optimization_barrier((sent, quarter, kept, came))

    share = jnp.where(z < 2, quarter[:8], sent[0] + sent[1] + sent[2])
    head, mine, ours, back = gather_z(share, kept, came, corner_first)
    head, mine, pivot_inverse = lax.optimization_barrier((head, mine, pivot_inverse))

    head = [head] + [cube_send(head, lambda i, j, k: (i + d, j, k)) for d in (1, -1, 2)]
    count, width = mine.shape
    excites = ours.shape[1]
    block, forcing = local(
        tail_kernel,
        (c,),
        (mine, swap_core(mine), ours, back, group_order()),
        ((2 * count, width + ROWS), ours.shape[1:]),
    )
    side = cube_send(block, lambda i, j, k: (i + sign(k), j, k))

    ids, ids_of_head = tail_ids(), head_ids()
    other = swap_core(jnp.concatenate(head))
    panel, factors, head = local(
        factors_kernel,
        (holder, start),
        (matrix[:, : 2 * WIDTH], pivot_inverse, ids_of_head, *head, other),
        ((ROWS, 2 * WIDTH), (ROWS, 2 * WIDTH), (2 * WIDTH, WIDTH)),
        flops=4 * 10**9,
    )
    side, panel = lax.optimization_barrier((side, panel))
    far = cube_send(side[:count], lambda i, j, k: (i + sign(k), j, k))
    turned_left, head_out = local(
        left_kernel,
        (holder, start, blk),
        (factors, *from_first(factors), pivot_inverse, ids, ids_of_head, head)
        + (matrix[:, :WIDTH], panel[:, :WIDTH]),
        ((2 * ROWS, 2 * WIDTH), (ROWS, WIDTH)),
        flops=5 * 10**9,
    )
    body, change = local(
        own_kernel,
        (0,),
        (turned_left, matrix, block, side),
        ((ROWS, width), (ROWS, ROWS)),
        flops=10 * 10**9,
    )
    front, solved = local(
        final_kernel,
        (holder, blk),
        (turned_left, head_out, panel, body, change, forcing, far, swap_core(side), swap_core(far)),
        (matrix.shape, forcing.shape),
        flops=1 * 10**9,
    )
    return front, solved


def solution(mesh):
    in_specs = (P("cube", "blk"), P("cube", "blk"), P(), P(), P("cube"), P("blk", "cube"))
    out_specs = (P("cube", "blk"), P("blk", "cube"))
    return jax.shard_map(shards, mesh=mesh, in_specs=in_specs, out_specs=out_specs, check_vma=False)
```

```python
import jax
import jax.numpy as jnp
import numpy as np
from jax import lax
from jax.experimental import pallas as pl
from jax.experimental.pallas import tpu as pltpu
from jax.sharding import PartitionSpec as P

NX, NZ, NC, NY = 4, 8, 2, 4
ROWS = 128
WIDTH = 256
X_ORDER = (3, 1, 2)
Z_ORDER = (3, 2, 1)
Y_ORDER = (3, 1, 2)
HIGH = lax.Precision.HIGHEST


def dot(left, right):
    return jnp.dot(left, right, precision=HIGH, preferred_element_type=jnp.float32)


def after(value, *others):
    return lax.optimization_barrier((value, others))[0]


def cube_send(value, target):
    pairs = []
    for x in range(NX):
        for z in range(NZ):
            for c in range(NC):
                to = target(x, z, c)
                if to is not None:
                    tx, tz, tc = to
                    pairs.append(
                        ((x * NZ + z) * NC + c, ((tx % NX) * NZ + tz % NZ) * NC + tc % NC)
                    )
    return lax.ppermute(value, "cube", pairs)


def swap_core(value):
    return cube_send(value, lambda x, z, c: (x, z, 1 - c))


def place():
    rank = lax.axis_index("cube")
    return rank, rank >> 4, rank >> 1 & 7, rank & 1


def sign(core):
    return 1 - 2 * core


def local(kernel, place_scalars, arrays, shapes, flops=10**6):
    size = sum(4 * int(np.prod(shape)) for shape in shapes)
    return pl.pallas_call(
        kernel,
        out_shape=[jax.ShapeDtypeStruct(shape, jnp.float32) for shape in shapes],
        in_specs=[pl.BlockSpec(memory_space=pltpu.SMEM)]
        + [pl.BlockSpec(memory_space=pltpu.VMEM)] * len(arrays),
        out_specs=[pl.BlockSpec(memory_space=pltpu.VMEM)] * len(shapes),
        compiler_params=pltpu.CompilerParams(vmem_limit_bytes=40 * 2**20),
        cost_estimate=pl.CostEstimate(flops=flops, bytes_accessed=2 * size, transcendentals=0),
    )(jnp.stack([jnp.asarray(v, jnp.int32) for v in place_scalars]), *arrays)


def split(values):
    high = values.astype(jnp.bfloat16)
    rest = values - high.astype(jnp.float32)
    middle = rest.astype(jnp.bfloat16)
    return high, middle, (rest - middle.astype(jnp.float32)).astype(jnp.bfloat16)


def assemble_kernel(at_ref, front_ref, child_ref, came_ref, rows_ref, cols_ref, out_ref):
    parity, row_base, col_base = at_ref[0], at_ref[1], at_ref[2]
    count, width = came_ref.shape
    kept = child_ref[pl.ds(pl.multiple_of(parity * count, count), count), :]
    came = came_ref[...]
    even = parity == 0
    children = [jnp.where(even, kept, came), jnp.where(even, came, kept)]
    children = [jnp.concatenate(split(child), axis=0) for child in children]
    spots = lax.broadcasted_iota(jnp.int32, (ROWS, ROWS), 0) + row_base
    row_table = jnp.where(spots == rows_ref[...], 1.0, 0.0).astype(jnp.bfloat16)
    targets = lax.broadcasted_iota(jnp.int32, (2 * ROWS, ROWS), 0) + col_base
    for b in range(width // ROWS):
        span = slice(b * ROWS, (b + 1) * ROWS)
        out_span = slice(2 * b * ROWS, 2 * (b + 1) * ROWS)
        placed = []
        for k, child in enumerate(children):
            table = jnp.where(targets + 2 * b * ROWS == cols_ref[k : k + 1, span], 1.0, 0.0)
            parts = lax.dot_general(
                child[:, span],
                table.astype(jnp.bfloat16),
                (((1,), (1,)), ((), ())),
                preferred_element_type=jnp.float32,
            )
            placed.append(parts[:count] + (parts[count : 2 * count] + parts[2 * count :]))
        parts = jnp.concatenate(split(jnp.concatenate(placed, axis=0)), axis=1)
        sums = jnp.dot(row_table, parts, preferred_element_type=jnp.float32)
        size = 2 * ROWS
        sums = sums[:, :size] + (sums[:, size : 2 * size] + sums[:, 2 * size :])
        out_ref[:, out_span] = front_ref[:, out_span] + sums


def assemble(front_entries, child_blocks, child_map):
    rows_dev, front_cols = front_entries.shape
    child_cols = child_blocks.shape[1]
    half_rows = rows_dev // 2
    rank, _, _, parity = place()
    blk = lax.axis_index("blk")
    sent_rows = lax.dynamic_slice_in_dim(child_blocks, (1 - parity) * half_rows, half_rows)
    child_start = (rank >> 1) * rows_dev + parity * half_rows
    rows = lax.dynamic_slice(child_map, (0, child_start), (2, half_rows)).reshape(1, rows_dev)
    cols = lax.dynamic_slice(child_map, (0, blk * child_cols), (2, child_cols))
    return local(
        assemble_kernel,
        (parity, rank * rows_dev, blk * front_cols),
        (front_entries, child_blocks, swap_core(sent_rows), rows, cols),
        (front_entries.shape,),
        flops=10**9,
    )[0]


def dense_kernel(at_ref, index_ref, values_ref, kept_ref, sent_ref):
    x, c = at_ref[0], at_ref[1]
    s = sign(c)
    index = index_ref[...]
    values = values_ref[...]
    excites, entries = values.shape
    parts = jnp.concatenate(split(values), axis=0)
    chip = index >> 8

    def table(at, size):
        rows = lax.broadcasted_iota(jnp.int32, (size, entries), 0)
        return jnp.where(rows == at, 1.0, 0.0).astype(jnp.bfloat16)

    def summed(masks, place_table):
        rows = [parts * mask.astype(jnp.bfloat16) for mask in masks]
        placed = lax.dot_general(
            jnp.concatenate(rows, axis=0),
            place_table,
            (((1,), (1,)), ((), ())),
            preferred_element_type=jnp.float32,
        )
        placed = placed.reshape(len(masks), 3, excites, place_table.shape[0])
        return placed[:, 0] + (placed[:, 1] + placed[:, 2])

    def mask_of(condition):
        return jnp.broadcast_to(jnp.where(condition, 1.0, 0.0), (3 * excites, entries))

    near = table(index & 255, NC * ROWS)
    pivot = table((index >> 7 & 1) * 64 + (index >> 8) * 32 + (index & 31), ROWS)

    def blocks(at):
        sums = summed([mask_of(chip == at * NZ + z) for z in range(NZ)], near)
        held = (index < 2 * WIDTH) & (index >> 5 & 3 == at)
        return sums, summed([mask_of(held)], pivot)[0]

    for ref, at in ((kept_ref, x + s & 3), (sent_ref, x - s & 3)):
        sums, group = blocks(at)
        for z in range(NZ):
            ref[2 * z] = sums[z, :, :ROWS]
            ref[2 * z + 1] = sums[z, :, ROWS:]
        ref[2 * NZ] = group
    for start, at in ((17, x + 2 & 3), (26, x)):
        sums, group = blocks(at)
        for z in range(NZ):
            first, second = sums[z, :, :ROWS], sums[z, :, ROWS:]
            kept_ref[start + z] = jnp.where(c == 0, first, second)
            sent_ref[start + z] = jnp.where(c == 0, second, first)
        kept_ref[start + NZ] = jnp.where(c == 0, group, 0.0)
        sent_ref[start + NZ] = jnp.where(c == 0, 0.0, group)


def forcing_core(rhs_index, rhs_values):
    _, x, _, c = place()
    entries = rhs_values.shape[1]
    shape = (35, rhs_values.shape[0], ROWS)
    kept, sent = local(
        dense_kernel,
        (x, c),
        (rhs_index.reshape(1, entries), rhs_values),
        (shape, shape),
        flops=10**9,
    )
    return kept + swap_core(sent)


def forcing_x(summed):
    side = cube_send(summed[:17], lambda i, j, k: (i + sign(k), j, k))
    across = cube_send(summed[17:26], lambda i, j, k: (i + 2, j, k))
    return side, across, summed[26:]


def rows_kernel(at_ref, side_ref, across_ref, own_ref, kept_ref, sent_ref):
    z, c = at_ref[0], at_ref[1]
    s = sign(c)
    for ref, sgn in ((kept_ref, s), (sent_ref, -s)):
        for n in (1, 2, 3):
            i = z + n * sgn & 7
            for k in range(NC):
                mine = own_ref[i] + across_ref[i]
                ref[2 * n - 2 + k] = side_ref[2 * i + k] + jnp.where(c == k, mine, 0.0)
    for slot, i in ((6, z + 4 & 7), (7, z)):
        kept_ref[slot] = side_ref[2 * i + c] + (own_ref[i] + across_ref[i])
        sent_ref[slot] = side_ref[2 * i + 1 - c]
    pivot = side_ref[16] + (own_ref[8] + across_ref[8])
    kept_ref[8] = pivot
    sent_ref[8] = pivot


def forcing_rows(side, across, own):
    _, _, z, c = place()
    kept, sent = local(rows_kernel, (z, c), (side, across, own), (own.shape, own.shape))
    return kept, swap_core(sent)


def scatter_x(block):
    return [
        cube_send(
            block[32 * d : 32 * d + 32],
            lambda i, j, k: (d, j, k) if i == 0 and j < 2 else None,
        )
        for d in X_ORDER
    ]


def scatter_z(quarter):
    return [
        cube_send(
            quarter[8 * d : 8 * d + 8],
            lambda i, j, k: (i, (-d if j == 0 else 1 + d), k) if j < 2 else None,
        )
        for d in range(1, NZ // 2)
    ]


def message_kernel(at_ref, share_ref, other_ref, kept_ref, came_ref, *out_refs):
    c, turn = at_ref[0], at_ref[1]
    low = c == 0
    width = share_ref.shape[1]

    def columns(ref):
        left, right = ref[:, :WIDTH], ref[:, WIDTH : 2 * WIDTH]
        yield 0, jnp.where(turn == 1, right, left)
        yield WIDTH, jnp.where(turn == 1, left, right)
        yield 2 * WIDTH, ref[:, 2 * WIDTH :]

    summed = [kept_ref[i] + came_ref[i] for i in range(9)]
    for (at, mine), (_, other) in zip(columns(share_ref), columns(other_ref)):
        span = slice(at, at + mine.shape[1])
        for ref in out_refs[:3]:
            ref[:8, span] = jnp.where(low, mine, other)
            ref[8:, span] = jnp.where(low, other, mine)
        out_refs[3][:, span] = mine
    for n, ref in enumerate(out_refs[:3]):
        for i, block in enumerate((summed[2 * n], summed[2 * n + 1], summed[8])):
            ref[:, width + i * ROWS : width + (i + 1) * ROWS] = block
    first = jnp.where(low, summed[8], 0.0)
    for i, block in enumerate((summed[6][:8], summed[6][8:], first[:8], first[8:])):
        out_refs[3][:, width + i * ROWS : width + (i + 1) * ROWS] = block
    out_refs[4][0] = summed[7]
    out_refs[4][1] = first


def unpack_kernel(at_ref, own_ref, far_ref, three_ref, two_ref, one_ref, left_ref, *out_refs):
    low = at_ref[0] == 0
    head_ref, tail_ref, mine_ref, back_ref = out_refs
    width = WIDTH + tail_ref.shape[1]
    row = 0
    for ref in (own_ref, one_ref, two_ref, three_ref, far_ref):
        count = ref.shape[0]
        head_ref[row : row + count] = ref[:, :WIDTH]
        tail_ref[row : row + count] = ref[:, WIDTH:width]
        row += count
    spans = [slice(width + i * ROWS, width + (i + 1) * ROWS) for i in range(4)]
    sums = [one_ref[:, at] + two_ref[:, at] + three_ref[:, at] for at in spans[:3]]
    far = [far_ref[:, at] for at in spans]
    mine_ref[0] = (
        jnp.where(low, sums[0], sums[1])
        + jnp.concatenate([far[0], far[1]], axis=0)
        + left_ref[0]
    )
    pivot = sums[2] + jnp.concatenate([far[2], far[3]], axis=0) + left_ref[1]
    mine_ref[1] = pivot
    back_ref[0] = jnp.where(low, sums[1], sums[0])
    back_ref[1] = pivot


def gather_z(share, kept, came, corner_first):
    c = lax.axis_index("cube") & 1
    width = share.shape[1]
    excites = kept.shape[1]
    near = (2 * excites // 2, width + 3 * ROWS)
    *messages, left = local(
        message_kernel,
        (c, corner_first),
        (share, swap_core(share), kept, came),
        (near, near, near, (8, width + 4 * ROWS), (2, excites, ROWS)),
    )
    far = cube_send(messages[3], lambda i, j, k: (i, j + 4, k))
    got = {
        n: cube_send(messages[n - 1], lambda i, j, k: (i, j + n * sign(k), k)) for n in Z_ORDER
    }
    got = [got[n] for n in (1, 2, 3)]
    head, tail, mine, back = local(
        unpack_kernel,
        (c,),
        (messages[3], far, *got[::-1], left),
        ((64, WIDTH), (64, width - WIDTH), (2, excites, ROWS), (2, excites, ROWS)),
    )
    return head, tail, mine, swap_core(back)


def tail_kernel(at_ref, mine_ref, theirs_ref, ours_ref, back_ref, order_ref, *out_refs):
    all_ref, forcing_ref = out_refs
    count, width = mine_ref.shape
    forcing_ref[...] = ours_ref[0] + back_ref[0]
    pivots = ours_ref[1] + back_ref[1]
    excites = pivots.shape[0]
    spots = lax.broadcasted_iota(jnp.int32, (ROWS, ROWS), 0)
    table = jnp.where(spots == order_ref[...], 1.0, 0.0)
    ordered = dot(pivots, table)
    filler = jnp.zeros((ROWS - excites, ROWS), jnp.float32)
    columns = jnp.concatenate([ordered, filler], axis=0).T
    all_ref[:count, :width] = mine_ref[...]
    all_ref[count:, :width] = theirs_ref[...]
    all_ref[:, width:] = columns


def rows_8(dx, dz, core):
    return [(*dx, *dz, core, r) for r in range(8)]


def rows_64(dx, flip):
    s = -1 if flip else 1
    out = rows_8(dx, (0, 0), 2 + flip)
    for n in (1, 2, 3):
        out += rows_8(dx, (-n * s, 0), 0) + rows_8(dx, (-n * s, 0), 1)
    return out + rows_8(dx, (0, 4), 2 + flip)


def rows_128(dx, flip):
    return rows_64(dx, flip) + rows_64(dx, 1 - flip)


def row_ids(rows):
    _, x, z, c = place()
    s = sign(c)
    xs, x0, zs, z0, core, r = (np.array(v, np.int32)[None] for v in zip(*rows))
    at_x = x + xs * s + x0 & 3
    at_z = z + zs * s + z0 & 7
    core = jnp.where(core > 1, c ^ (core - 2), core)
    lower = (at_z == 0) | (at_z > 4)
    pos = jnp.where(lower, 8 - at_z & 7, at_z - 1)
    return (jnp.where(lower, 0, NC) + core) * ROWS + at_x * 32 + pos * 8 + r


def head_ids():
    return row_ids(
        sum((rows_64((0, dx), flip) for flip in range(NC) for dx in (0, -1, 1, 2)), [])
    )


def tail_ids():
    return row_ids(
        rows_128((0, 0), 0)
        + rows_128((-1, 0), 0)
        + rows_64((0, 2), 0)
        + rows_128((1, 0), 1)
        + rows_64((0, 2), 1)
    )


def group_order():
    ids = row_ids(rows_128((0, 0), 0))
    return (ids >> 7 & 1) * 64 + (ids >> 8) * 32 + (ids & 31)


def spread(values, ids, first):
    count, width = values.shape
    rows = lax.broadcasted_iota(jnp.int32, (width, ids.shape[1]), 0) + first
    table = jnp.where(rows == ids, 1.0, 0.0).astype(jnp.bfloat16)
    parts = jnp.dot(
        jnp.concatenate(split(values), axis=0), table, preferred_element_type=jnp.float32
    )
    return parts[:count] + (parts[count : 2 * count] + parts[2 * count :])


def factors_kernel(
    at_ref, panel_ref, pivots_ref, ids_ref, a_ref, b_ref, c_ref, d_ref, other_ref,
    out_ref, factors_ref, head_ref
):
    holder, start = at_ref[0], at_ref[1]
    two = holder == 2
    row = 0
    for ref in (a_ref, b_ref, c_ref, d_ref, other_ref):
        head_ref[row : row + ref.shape[0]] = ref[...]
        row += ref.shape[0]
    head = head_ref[...]
    ids = ids_ref[...]
    left, right = panel_ref[:, :WIDTH], panel_ref[:, WIDTH:]
    first, second = pivots_ref[0], pivots_ref[1]
    l1 = dot(left, first)
    reduced = right - dot(spread(l1, ids, 0), head)
    l2 = dot(reduced, second)
    start = pl.multiple_of(start, ROWS)
    lead = jnp.where(two, pivots_ref[1, pl.ds(start, ROWS), :], l2)
    back = dot(dot(spread(lead, ids, WIDTH), head), first)
    out_ref[:, :WIDTH] = jnp.where(holder == 1, left, l1)
    out_ref[:, WIDTH:] = jnp.where(holder == 1, right, jnp.where(two, reduced, l2))
    factors_ref[:, :WIDTH] = jnp.where(two, l1, l1 - back)
    factors_ref[:, WIDTH:] = jnp.where(two, back, l2)


def left_kernel(
    at_ref, own_ref, three_ref, one_ref, two_ref, pivots_ref, ids_ref, head_ids_ref, head_ref,
    matrix_ref, panel_ref, turned_ref, out_ref
):
    holder, start, blk = at_ref[0], at_ref[1], at_ref[2]
    one, two = holder == 1, holder == 2
    factors = own_ref[...]
    for d, ref in enumerate((one_ref, two_ref, three_ref)):
        factors = jnp.where(blk == d + 1, ref[...], factors)
    first, second = factors[:, :WIDTH], factors[:, WIDTH:]
    start = pl.multiple_of(start, ROWS)
    pick_one = pivots_ref[0, pl.ds(start, ROWS), :]
    pick_two = pivots_ref[1, pl.ds(start, ROWS), :]
    front = jnp.where(one, 0.0, first), jnp.where(holder > 0, 0.0, second)
    forcing = (
        jnp.where(one, -pick_one, jnp.where(two, second, first)),
        jnp.where(one, 0.0, jnp.where(two, -pick_two, second)),
    )
    ids = ids_ref[...]
    lead = jnp.concatenate([front[0], forcing[0]], axis=0)
    rest = jnp.concatenate([front[1], forcing[1]], axis=0)
    turned_ref[...] = spread(lead, ids, 0) + spread(rest, ids, WIDTH)
    ids = head_ids_ref[...]
    turned = spread(front[0], ids, 0) + spread(front[1], ids, WIDTH)
    change = dot3(halves(turned), head_ref[...])
    out_ref[...] = jnp.where(blk == 0, panel_ref[...], matrix_ref[...] - change)


def halves(values):
    high = values.astype(jnp.bfloat16)
    return high, (values - high.astype(jnp.float32)).astype(jnp.bfloat16)


def dot3(left, rows):
    (high, low), (rows_high, rows_low) = left, halves(rows)
    count = high.shape[0]
    both = jnp.dot(
        jnp.concatenate([high, low], axis=0), rows_high, preferred_element_type=jnp.float32
    )
    rest = jnp.dot(high, rows_low, preferred_element_type=jnp.float32)
    return both[:count] + (both[count:] + rest)


def first_kernel(at_ref, left_ref, matrix_ref, block_ref, side_ref, body_ref, change_ref):
    width = body_ref.shape[1]
    rows = jnp.concatenate([block_ref[...], side_ref[...]], axis=0)
    cut = rows.shape[0]
    front, forcing = halves(left_ref[:ROWS, :cut]), halves(left_ref[ROWS:, :cut])
    for at in range(0, width, WIDTH):
        span = slice(at, at + WIDTH)
        change = dot3(front, rows[:, span])
        body_ref[:, span] = matrix_ref[:, WIDTH + at : 2 * WIDTH + at] - change
    change_ref[...] = dot3(forcing, rows[:, width:])


def second_kernel(
    at_ref, left_ref, body_ref, change_ref, far_ref, side_ref, out_ref, out_change_ref
):
    width = body_ref.shape[1]
    rows = jnp.concatenate([far_ref[...], side_ref[...]], axis=0)
    start = 256
    span = slice(start, start + rows.shape[0])
    front, forcing = halves(left_ref[:ROWS, span]), halves(left_ref[ROWS:, span])
    for at in range(0, width, WIDTH):
        span = slice(at, at + WIDTH)
        out_ref[:, span] = body_ref[:, span] - dot3(front, rows[:, span])
    out_change_ref[...] = change_ref[...] + dot3(forcing, rows[:, width:])


def final_kernel(
    at_ref, left_ref, head_ref, panel_ref, body_ref, change_ref, forcing_ref, far_ref,
    front_ref, solved_ref
):
    holder, blk = at_ref[0], at_ref[1]
    width = body_ref.shape[1]
    cut = left_ref.shape[1] - far_ref.shape[0]
    front, forcing = halves(left_ref[:ROWS, cut:]), halves(left_ref[ROWS:, cut:])
    front_ref[:, :WIDTH] = head_ref[...]
    for at in range(0, width, WIDTH):
        span = slice(at, at + WIDTH)
        value = body_ref[:, span] - dot3(front, far_ref[:, span])
        if at == 0:
            value = jnp.where(blk == 0, panel_ref[:, WIDTH:], value)
        front_ref[:, WIDTH + at : 2 * WIDTH + at] = value
    change = change_ref[...] + dot3(forcing, far_ref[:, width:])
    kept = jnp.where(holder > 0, 0.0, forcing_ref[...])
    solved_ref[...] = kept - change.T[: kept.shape[0]]


def from_first(value):
    got = {
        d: lax.ppermute(value, "blk", [(i, (i + d) % NY) for i in range(NY)]) for d in Y_ORDER
    }
    return [got[d] for d in Y_ORDER]


def shards(front_entries, child_blocks, child_map, pivot_inverse, rhs_index, rhs_values):
    rank, x, z, c = place()
    blk = lax.axis_index("blk")
    holder = jnp.where(rank < 2, 1, jnp.where(rank < 4, 2, 0))
    start = (rank & 1) * ROWS
    matrix = assemble(front_entries, child_blocks, child_map)

    corner_first = (blk == 0) & ((z == 0) | (z > 4))
    sent = scatter_x(matrix)
    across_x = forcing_x(forcing_core(rhs_index, rhs_values))
    sent, across_x = lax.optimization_barrier((sent, across_x))

    quarter = jnp.where(x == 0, matrix[:32], sent[0] + sent[1] + sent[2])
    sent = scatter_z(quarter)
    kept, came = forcing_rows(*across_x)
    sent, quarter, kept, came = lax.optimization_barrier((sent, quarter, kept, came))

    share = jnp.where(z < 2, quarter[:8], sent[0] + sent[1] + sent[2])
    head, mine, ours, back = gather_z(share, kept, came, corner_first)
    head, mine, pivot_inverse = lax.optimization_barrier((head, mine, pivot_inverse))

    head = [head] + [cube_send(head, lambda i, j, k: (i + d, j, k)) for d in (1, -1, 2)]
    count, width = mine.shape
    excites = ours.shape[1]
    block, forcing = local(
        tail_kernel,
        (c,),
        (mine, swap_core(mine), ours, back, group_order()),
        ((2 * count, width + ROWS), ours.shape[1:]),
    )
    side = cube_send(block, lambda i, j, k: (i + sign(k), j, k))

    ids, ids_of_head = tail_ids(), head_ids()
    other = swap_core(jnp.concatenate(head))
    panel, factors, head = local(
        factors_kernel,
        (holder, start),
        (matrix[:, : 2 * WIDTH], pivot_inverse, ids_of_head, *head, other),
        ((ROWS, 2 * WIDTH), (ROWS, 2 * WIDTH), (2 * WIDTH, WIDTH)),
        flops=4 * 10**9,
    )
    side, panel = lax.optimization_barrier((side, panel))
    far = cube_send(side[:count], lambda i, j, k: (i + sign(k), j, k))
    turned_left, head_out = local(
        left_kernel,
        (holder, start, blk),
        (factors, *from_first(factors), pivot_inverse, ids, ids_of_head, head)
        + (matrix[:, :WIDTH], panel[:, :WIDTH]),
        ((2 * ROWS, 2 * WIDTH), (ROWS, WIDTH)),
        flops=5 * 10**9,
    )
    shapes = ((ROWS, width), (ROWS, ROWS))
    body, change = local(
        first_kernel, (0,), (turned_left, matrix, block, side), shapes, flops=10**10
    )
    body, change = local(
        second_kernel, (0,), (turned_left, body, change, far, swap_core(side)), shapes, flops=10**9
    )
    front, solved = local(
        final_kernel,
        (holder, blk),
        (turned_left, head_out, panel, body, change, forcing, swap_core(far)),
        (matrix.shape, forcing.shape),
        flops=10**9,
    )
    return front, solved


def solution(mesh):
    in_specs = (P("cube", "blk"), P("cube", "blk"), P(), P(), P("cube"), P("blk", "cube"))
    out_specs = (P("cube", "blk"), P("blk", "cube"))
    return jax.shard_map(shards, mesh=mesh, in_specs=in_specs, out_specs=out_specs, check_vma=False)
```

```python
import jax
import jax.numpy as jnp
import numpy as np
from jax import lax
from jax.experimental import pallas as pl
from jax.experimental.pallas import tpu as pltpu
from jax.sharding import PartitionSpec as P

NX, NZ, NC, NY = 4, 8, 2, 4
ROWS = 128
WIDTH = 256
X_ORDER = (3, 1, 2)
Z_ORDER = (3, 2, 1)
Y_ORDER = (3, 1, 2)
HIGH = lax.Precision.HIGHEST


def dot(left, right):
    return jnp.dot(left, right, precision=HIGH, preferred_element_type=jnp.float32)


def after(value, *others):
    return lax.optimization_barrier((value, others))[0]


def cube_send(value, target):
    pairs = []
    for x in range(NX):
        for z in range(NZ):
            for c in range(NC):
                to = target(x, z, c)
                if to is not None:
                    tx, tz, tc = to
                    pairs.append(
                        ((x * NZ + z) * NC + c, ((tx % NX) * NZ + tz % NZ) * NC + tc % NC)
                    )
    return lax.ppermute(value, "cube", pairs)


def swap_core(value):
    return cube_send(value, lambda x, z, c: (x, z, 1 - c))


def place():
    rank = lax.axis_index("cube")
    return rank, rank >> 4, rank >> 1 & 7, rank & 1


def sign(core):
    return 1 - 2 * core


def local(kernel, place_scalars, arrays, shapes, flops=10**6):
    size = sum(4 * int(np.prod(shape)) for shape in shapes)
    return pl.pallas_call(
        kernel,
        out_shape=[jax.ShapeDtypeStruct(shape, jnp.float32) for shape in shapes],
        in_specs=[pl.BlockSpec(memory_space=pltpu.SMEM)]
        + [pl.BlockSpec(memory_space=pltpu.VMEM)] * len(arrays),
        out_specs=[pl.BlockSpec(memory_space=pltpu.VMEM)] * len(shapes),
        compiler_params=pltpu.CompilerParams(vmem_limit_bytes=40 * 2**20),
        cost_estimate=pl.CostEstimate(flops=flops, bytes_accessed=2 * size, transcendentals=0),
    )(jnp.stack([jnp.asarray(v, jnp.int32) for v in place_scalars]), *arrays)


def split(values):
    high = values.astype(jnp.bfloat16)
    rest = values - high.astype(jnp.float32)
    middle = rest.astype(jnp.bfloat16)
    return high, middle, (rest - middle.astype(jnp.float32)).astype(jnp.bfloat16)


def assemble_kernel(at_ref, front_ref, child_ref, came_ref, rows_ref, cols_ref, out_ref):
    parity, row_base, col_base = at_ref[0], at_ref[1], at_ref[2]
    count, width = came_ref.shape
    kept = child_ref[pl.ds(pl.multiple_of(parity * count, count), count), :]
    came = came_ref[...]
    even = parity == 0
    children = [jnp.where(even, kept, came), jnp.where(even, came, kept)]
    children = [jnp.concatenate(split(child), axis=0) for child in children]
    spots = lax.broadcasted_iota(jnp.int32, (ROWS, ROWS), 0) + row_base
    row_table = jnp.where(spots == rows_ref[...], 1.0, 0.0).astype(jnp.bfloat16)
    targets = lax.broadcasted_iota(jnp.int32, (2 * ROWS, ROWS), 0) + col_base
    for b in range(width // ROWS):
        span = slice(b * ROWS, (b + 1) * ROWS)
        out_span = slice(2 * b * ROWS, 2 * (b + 1) * ROWS)
        placed = []
        for k, child in enumerate(children):
            table = jnp.where(targets + 2 * b * ROWS == cols_ref[k : k + 1, span], 1.0, 0.0)
            parts = lax.dot_general(
                child[:, span],
                table.astype(jnp.bfloat16),
                (((1,), (1,)), ((), ())),
                preferred_element_type=jnp.float32,
            )
            placed.append(parts[:count] + (parts[count : 2 * count] + parts[2 * count :]))
        parts = jnp.concatenate(split(jnp.concatenate(placed, axis=0)), axis=1)
        sums = jnp.dot(row_table, parts, preferred_element_type=jnp.float32)
        size = 2 * ROWS
        sums = sums[:, :size] + (sums[:, size : 2 * size] + sums[:, 2 * size :])
        out_ref[:, out_span] = front_ref[:, out_span] + sums


def assemble(front_entries, child_blocks, child_map):
    rows_dev, front_cols = front_entries.shape
    child_cols = child_blocks.shape[1]
    half_rows = rows_dev // 2
    rank, _, _, parity = place()
    blk = lax.axis_index("blk")
    sent_rows = lax.dynamic_slice_in_dim(child_blocks, (1 - parity) * half_rows, half_rows)
    child_start = (rank >> 1) * rows_dev + parity * half_rows
    rows = lax.dynamic_slice(child_map, (0, child_start), (2, half_rows)).reshape(1, rows_dev)
    cols = lax.dynamic_slice(child_map, (0, blk * child_cols), (2, child_cols))
    return local(
        assemble_kernel,
        (parity, rank * rows_dev, blk * front_cols),
        (front_entries, child_blocks, swap_core(sent_rows), rows, cols),
        (front_entries.shape,),
        flops=10**9,
    )[0]


def dense_kernel(at_ref, index_ref, values_ref, kept_ref, sent_ref):
    x, c = at_ref[0], at_ref[1]
    s = sign(c)
    index = index_ref[...]
    values = values_ref[...]
    excites, entries = values.shape
    parts = jnp.concatenate(split(values), axis=0)
    chip = index >> 8

    def table(at, size):
        rows = lax.broadcasted_iota(jnp.int32, (size, entries), 0)
        return jnp.where(rows == at, 1.0, 0.0).astype(jnp.bfloat16)

    def summed(masks, place_table):
        rows = [parts * mask.astype(jnp.bfloat16) for mask in masks]
        placed = lax.dot_general(
            jnp.concatenate(rows, axis=0),
            place_table,
            (((1,), (1,)), ((), ())),
            preferred_element_type=jnp.float32,
        )
        placed = placed.reshape(len(masks), 3, excites, place_table.shape[0])
        return placed[:, 0] + (placed[:, 1] + placed[:, 2])

    def mask_of(condition):
        return jnp.broadcast_to(jnp.where(condition, 1.0, 0.0), (3 * excites, entries))

    near = table(index & 255, NC * ROWS)
    pivot = table((index >> 7 & 1) * 64 + (index >> 8) * 32 + (index & 31), ROWS)

    def blocks(at):
        sums = summed([mask_of(chip == at * NZ + z) for z in range(NZ)], near)
        held = (index < 2 * WIDTH) & (index >> 5 & 3 == at)
        return sums, summed([mask_of(held)], pivot)[0]

    for ref, at in ((kept_ref, x + s & 3), (sent_ref, x - s & 3)):
        sums, group = blocks(at)
        for z in range(NZ):
            ref[2 * z] = sums[z, :, :ROWS]
            ref[2 * z + 1] = sums[z, :, ROWS:]
        ref[2 * NZ] = group
    for start, at in ((17, x + 2 & 3), (26, x)):
        sums, group = blocks(at)
        for z in range(NZ):
            first, second = sums[z, :, :ROWS], sums[z, :, ROWS:]
            kept_ref[start + z] = jnp.where(c == 0, first, second)
            sent_ref[start + z] = jnp.where(c == 0, second, first)
        kept_ref[start + NZ] = jnp.where(c == 0, group, 0.0)
        sent_ref[start + NZ] = jnp.where(c == 0, 0.0, group)


def forcing_core(rhs_index, rhs_values):
    _, x, _, c = place()
    entries = rhs_values.shape[1]
    shape = (35, rhs_values.shape[0], ROWS)
    kept, sent = local(
        dense_kernel,
        (x, c),
        (rhs_index.reshape(1, entries), rhs_values),
        (shape, shape),
        flops=10**9,
    )
    return kept + swap_core(sent)


def forcing_x(summed):
    side = cube_send(summed[:17], lambda i, j, k: (i + sign(k), j, k))
    across = cube_send(summed[17:26], lambda i, j, k: (i + 2, j, k))
    return side, across, summed[26:]


def rows_kernel(at_ref, side_ref, across_ref, own_ref, kept_ref, sent_ref):
    z, c = at_ref[0], at_ref[1]
    s = sign(c)
    for ref, sgn in ((kept_ref, s), (sent_ref, -s)):
        for n in (1, 2, 3):
            i = z + n * sgn & 7
            for k in range(NC):
                mine = own_ref[i] + across_ref[i]
                ref[2 * n - 2 + k] = side_ref[2 * i + k] + jnp.where(c == k, mine, 0.0)
    for slot, i in ((6, z + 4 & 7), (7, z)):
        kept_ref[slot] = side_ref[2 * i + c] + (own_ref[i] + across_ref[i])
        sent_ref[slot] = side_ref[2 * i + 1 - c]
    pivot = side_ref[16] + (own_ref[8] + across_ref[8])
    kept_ref[8] = pivot
    sent_ref[8] = pivot


def forcing_rows(side, across, own):
    _, _, z, c = place()
    kept, sent = local(rows_kernel, (z, c), (side, across, own), (own.shape, own.shape))
    return kept, swap_core(sent)


def scatter_x(block):
    return [
        cube_send(
            block[32 * d : 32 * d + 32],
            lambda i, j, k: (d, j, k) if i == 0 and j < 2 else None,
        )
        for d in X_ORDER
    ]


def scatter_z(quarter):
    return [
        cube_send(
            quarter[8 * d : 8 * d + 8],
            lambda i, j, k: (i, (-d if j == 0 else 1 + d), k) if j < 2 else None,
        )
        for d in range(1, NZ // 2)
    ]


def message_kernel(at_ref, share_ref, other_ref, kept_ref, came_ref, *out_refs):
    c, turn = at_ref[0], at_ref[1]
    low = c == 0
    width = share_ref.shape[1]

    def columns(ref):
        left, right = ref[:, :WIDTH], ref[:, WIDTH : 2 * WIDTH]
        yield 0, jnp.where(turn == 1, right, left)
        yield WIDTH, jnp.where(turn == 1, left, right)
        yield 2 * WIDTH, ref[:, 2 * WIDTH :]

    summed = [kept_ref[i] + came_ref[i] for i in range(9)]
    for (at, mine), (_, other) in zip(columns(share_ref), columns(other_ref)):
        span = slice(at, at + mine.shape[1])
        for ref in out_refs[:3]:
            ref[:8, span] = jnp.where(low, mine, other)
            ref[8:, span] = jnp.where(low, other, mine)
        out_refs[3][:, span] = mine
    for n, ref in enumerate(out_refs[:3]):
        for i, block in enumerate((summed[2 * n], summed[2 * n + 1], summed[8])):
            ref[:, width + i * ROWS : width + (i + 1) * ROWS] = block
    first = jnp.where(low, summed[8], 0.0)
    out_refs[2][:, width + 3 * ROWS :] = summed[6]
    for i, block in enumerate((summed[6][:8], summed[6][8:], first[:8], first[8:])):
        out_refs[3][:, width + i * ROWS : width + (i + 1) * ROWS] = block
    out_refs[4][0] = summed[7]
    out_refs[4][1] = first


def unpack_kernel(
    at_ref, own_ref, up_ref, down_ref, three_ref, two_ref, one_ref, left_ref, *out_refs
):
    low = at_ref[0] == 0
    head_ref, tail_ref, mine_ref, back_ref = out_refs
    width = WIDTH + tail_ref.shape[1]
    row = 0
    far_rows = jnp.where(low, up_ref[...], down_ref[...])
    for rows in (own_ref, one_ref, two_ref, three_ref, far_rows):
        count = rows.shape[0]
        head_ref[row : row + count] = rows[:, :WIDTH]
        tail_ref[row : row + count] = rows[:, WIDTH:width]
        row += count
    spans = [slice(width + i * ROWS, width + (i + 1) * ROWS) for i in range(4)]
    sums = [one_ref[:, at] + two_ref[:, at] + three_ref[:, at] for at in spans[:3]]
    far = [far_rows[:, at] for at in spans]
    mine_ref[0] = (
        jnp.where(low, sums[0], sums[1])
        + jnp.concatenate([far[0], far[1]], axis=0)
        + left_ref[0]
    )
    pivot = sums[2] + jnp.concatenate([far[2], far[3]], axis=0) + left_ref[1]
    mine_ref[1] = pivot
    back_ref[0] = jnp.where(low, sums[1], sums[0])
    back_ref[1] = pivot


def gather_z(share, kept, came, corner_first):
    c = lax.axis_index("cube") & 1
    width = share.shape[1]
    excites = kept.shape[1]
    near = (2 * excites // 2, width + 3 * ROWS)
    *messages, left = local(
        message_kernel,
        (c, corner_first),
        (share, swap_core(share), kept, came),
        (near, near, (near[0], near[1] + ROWS), (8, width + 4 * ROWS), (2, excites, ROWS)),
    )
    got = {
        n: cube_send(messages[n - 1], lambda i, j, k: (i, j + n * sign(k), k)) for n in Z_ORDER
    }
    up = cube_send(messages[3], lambda i, j, k: (i, j + 4, k) if k == 0 else None)
    extra = got[3][:, near[1] :]
    down = jnp.concatenate(
        [got[3][8:, :width], extra[:8], extra[8:], jnp.zeros((8, 2 * ROWS), jnp.float32)], axis=1
    )
    down = cube_send(down, lambda i, j, k: (i, j - 1, k) if k == 1 else None)
    head, tail, mine, back = local(
        unpack_kernel,
        (c,),
        (messages[3], up, down, got[3], got[2], got[1], left),
        ((64, WIDTH), (64, width - WIDTH), (2, excites, ROWS), (2, excites, ROWS)),
    )
    return head, tail, mine, swap_core(back)


def tail_kernel(at_ref, mine_ref, theirs_ref, ours_ref, back_ref, order_ref, *out_refs):
    all_ref, forcing_ref = out_refs
    count, width = mine_ref.shape
    forcing_ref[...] = ours_ref[0] + back_ref[0]
    pivots = ours_ref[1] + back_ref[1]
    excites = pivots.shape[0]
    spots = lax.broadcasted_iota(jnp.int32, (ROWS, ROWS), 0)
    table = jnp.where(spots == order_ref[...], 1.0, 0.0)
    ordered = dot(pivots, table)
    filler = jnp.zeros((ROWS - excites, ROWS), jnp.float32)
    columns = jnp.concatenate([ordered, filler], axis=0).T
    all_ref[:count, :width] = mine_ref[...]
    all_ref[count:, :width] = theirs_ref[...]
    all_ref[:, width:] = columns


def rows_8(dx, dz, core):
    return [(*dx, *dz, core, r) for r in range(8)]


def rows_64(dx, flip):
    s = -1 if flip else 1
    out = rows_8(dx, (0, 0), 2 + flip)
    for n in (1, 2, 3):
        out += rows_8(dx, (-n * s, 0), 0) + rows_8(dx, (-n * s, 0), 1)
    return out + rows_8(dx, (0, 4), 2 + flip)


def rows_128(dx, flip):
    return rows_64(dx, flip) + rows_64(dx, 1 - flip)


def row_ids(rows):
    _, x, z, c = place()
    s = sign(c)
    xs, x0, zs, z0, core, r = (np.array(v, np.int32)[None] for v in zip(*rows))
    at_x = x + xs * s + x0 & 3
    at_z = z + zs * s + z0 & 7
    core = jnp.where(core > 1, c ^ (core - 2), core)
    lower = (at_z == 0) | (at_z > 4)
    pos = jnp.where(lower, 8 - at_z & 7, at_z - 1)
    return (jnp.where(lower, 0, NC) + core) * ROWS + at_x * 32 + pos * 8 + r


def head_ids():
    return row_ids(
        sum((rows_64((0, dx), flip) for flip in range(NC) for dx in (0, -1, 1, 2)), [])
    )


def tail_ids():
    return row_ids(
        rows_128((0, 0), 0)
        + rows_128((-1, 0), 0)
        + rows_64((0, 2), 0)
        + rows_128((1, 0), 1)
        + rows_64((0, 2), 1)
    )


def group_order():
    ids = row_ids(rows_128((0, 0), 0))
    return (ids >> 7 & 1) * 64 + (ids >> 8) * 32 + (ids & 31)


def spread(values, ids, first):
    count, width = values.shape
    rows = lax.broadcasted_iota(jnp.int32, (width, ids.shape[1]), 0) + first
    table = jnp.where(rows == ids, 1.0, 0.0).astype(jnp.bfloat16)
    parts = jnp.dot(
        jnp.concatenate(split(values), axis=0), table, preferred_element_type=jnp.float32
    )
    return parts[:count] + (parts[count : 2 * count] + parts[2 * count :])


def factors_kernel(
    at_ref, panel_ref, pivots_ref, ids_ref, a_ref, b_ref, c_ref, d_ref, other_ref,
    out_ref, factors_ref, head_ref
):
    holder, start = at_ref[0], at_ref[1]
    two = holder == 2
    row = 0
    for ref in (a_ref, b_ref, c_ref, d_ref, other_ref):
        head_ref[row : row + ref.shape[0]] = ref[...]
        row += ref.shape[0]
    head = head_ref[...]
    ids = ids_ref[...]
    left, right = panel_ref[:, :WIDTH], panel_ref[:, WIDTH:]
    first, second = pivots_ref[0], pivots_ref[1]
    l1 = dot(left, first)
    reduced = right - dot(spread(l1, ids, 0), head)
    l2 = dot(reduced, second)
    start = pl.multiple_of(start, ROWS)
    lead = jnp.where(two, pivots_ref[1, pl.ds(start, ROWS), :], l2)
    back = dot(dot(spread(lead, ids, WIDTH), head), first)
    out_ref[:, :WIDTH] = jnp.where(holder == 1, left, l1)
    out_ref[:, WIDTH:] = jnp.where(holder == 1, right, jnp.where(two, reduced, l2))
    factors_ref[:, :WIDTH] = jnp.where(two, l1, l1 - back)
    factors_ref[:, WIDTH:] = jnp.where(two, back, l2)


def left_kernel(
    at_ref, own_ref, three_ref, one_ref, two_ref, pivots_ref, ids_ref, head_ids_ref, head_ref,
    matrix_ref, panel_ref, turned_ref, out_ref
):
    holder, start, blk = at_ref[0], at_ref[1], at_ref[2]
    one, two = holder == 1, holder == 2
    factors = own_ref[...]
    for d, ref in enumerate((one_ref, two_ref, three_ref)):
        factors = jnp.where(blk == d + 1, ref[...], factors)
    first, second = factors[:, :WIDTH], factors[:, WIDTH:]
    start = pl.multiple_of(start, ROWS)
    pick_one = pivots_ref[0, pl.ds(start, ROWS), :]
    pick_two = pivots_ref[1, pl.ds(start, ROWS), :]
    front = jnp.where(one, 0.0, first), jnp.where(holder > 0, 0.0, second)
    forcing = (
        jnp.where(one, -pick_one, jnp.where(two, second, first)),
        jnp.where(one, 0.0, jnp.where(two, -pick_two, second)),
    )
    ids = ids_ref[...]
    lead = jnp.concatenate([front[0], forcing[0]], axis=0)
    rest = jnp.concatenate([front[1], forcing[1]], axis=0)
    turned_ref[...] = spread(lead, ids, 0) + spread(rest, ids, WIDTH)
    ids = head_ids_ref[...]
    turned = spread(front[0], ids, 0) + spread(front[1], ids, WIDTH)
    change = dot3(halves(turned), head_ref[...])
    out_ref[...] = jnp.where(blk == 0, panel_ref[...], matrix_ref[...] - change)


def halves(values):
    high = values.astype(jnp.bfloat16)
    return high, (values - high.astype(jnp.float32)).astype(jnp.bfloat16)


def dot3(left, rows):
    (high, low), (rows_high, rows_low) = left, halves(rows)
    count = high.shape[0]
    both = jnp.dot(
        jnp.concatenate([high, low], axis=0), rows_high, preferred_element_type=jnp.float32
    )
    rest = jnp.dot(high, rows_low, preferred_element_type=jnp.float32)
    return both[:count] + (both[count:] + rest)


def first_kernel(at_ref, left_ref, matrix_ref, block_ref, side_ref, body_ref, change_ref):
    width = body_ref.shape[1]
    rows = jnp.concatenate([block_ref[...], side_ref[...]], axis=0)
    cut = rows.shape[0]
    front, forcing = halves(left_ref[:ROWS, :cut]), halves(left_ref[ROWS:, :cut])
    for at in range(0, width, WIDTH):
        span = slice(at, at + WIDTH)
        change = dot3(front, rows[:, span])
        body_ref[:, span] = matrix_ref[:, WIDTH + at : 2 * WIDTH + at] - change
    change_ref[...] = dot3(forcing, rows[:, width:])


def second_kernel(
    at_ref, left_ref, body_ref, change_ref, far_ref, side_ref, out_ref, out_change_ref
):
    width = body_ref.shape[1]
    rows = jnp.concatenate([far_ref[...], side_ref[...]], axis=0)
    start = 256
    span = slice(start, start + rows.shape[0])
    front, forcing = halves(left_ref[:ROWS, span]), halves(left_ref[ROWS:, span])
    for at in range(0, width, WIDTH):
        span = slice(at, at + WIDTH)
        out_ref[:, span] = body_ref[:, span] - dot3(front, rows[:, span])
    out_change_ref[...] = change_ref[...] + dot3(forcing, rows[:, width:])


def final_kernel(
    at_ref, left_ref, head_ref, panel_ref, body_ref, change_ref, forcing_ref, far_ref,
    front_ref, solved_ref
):
    holder, blk = at_ref[0], at_ref[1]
    width = body_ref.shape[1]
    cut = left_ref.shape[1] - far_ref.shape[0]
    front, forcing = halves(left_ref[:ROWS, cut:]), halves(left_ref[ROWS:, cut:])
    front_ref[:, :WIDTH] = head_ref[...]
    for at in range(0, width, WIDTH):
        span = slice(at, at + WIDTH)
        value = body_ref[:, span] - dot3(front, far_ref[:, span])
        if at == 0:
            value = jnp.where(blk == 0, panel_ref[:, WIDTH:], value)
        front_ref[:, WIDTH + at : 2 * WIDTH + at] = value
    change = change_ref[...] + dot3(forcing, far_ref[:, width:])
    kept = jnp.where(holder > 0, 0.0, forcing_ref[...])
    solved_ref[...] = kept - change.T[: kept.shape[0]]


def from_first(value):
    got = {
        d: lax.ppermute(value, "blk", [(0, d)]) for d in Y_ORDER
    }
    return [got[d] for d in Y_ORDER]


def shards(front_entries, child_blocks, child_map, pivot_inverse, rhs_index, rhs_values):
    rank, x, z, c = place()
    blk = lax.axis_index("blk")
    holder = jnp.where(rank < 2, 1, jnp.where(rank < 4, 2, 0))
    start = (rank & 1) * ROWS
    matrix = assemble(front_entries, child_blocks, child_map)

    corner_first = (blk == 0) & ((z == 0) | (z > 4))
    sent = scatter_x(matrix)
    across_x = forcing_x(forcing_core(rhs_index, rhs_values))
    sent, across_x = lax.optimization_barrier((sent, across_x))

    quarter = jnp.where(x == 0, matrix[:32], sent[0] + sent[1] + sent[2])
    sent = scatter_z(quarter)
    kept, came = forcing_rows(*across_x)
    sent, quarter, kept, came = lax.optimization_barrier((sent, quarter, kept, came))

    share = jnp.where(z < 2, quarter[:8], sent[0] + sent[1] + sent[2])
    head, mine, ours, back = gather_z(share, kept, came, corner_first)
    head, mine, pivot_inverse = lax.optimization_barrier((head, mine, pivot_inverse))

    head = [head] + [cube_send(head, lambda i, j, k: (i + d, j, k)) for d in (1, -1, 2)]
    count, width = mine.shape
    excites = ours.shape[1]
    block, forcing = local(
        tail_kernel,
        (c,),
        (mine, swap_core(mine), ours, back, group_order()),
        ((2 * count, width + ROWS), ours.shape[1:]),
    )
    side = cube_send(block, lambda i, j, k: (i + sign(k), j, k))

    ids, ids_of_head = tail_ids(), head_ids()
    other = swap_core(jnp.concatenate(head))
    panel, factors, head = local(
        factors_kernel,
        (holder, start),
        (matrix[:, : 2 * WIDTH], pivot_inverse, ids_of_head, *head, other),
        ((ROWS, 2 * WIDTH), (ROWS, 2 * WIDTH), (2 * WIDTH, WIDTH)),
        flops=4 * 10**9,
    )
    side, panel = lax.optimization_barrier((side, panel))
    far = cube_send(side[:count], lambda i, j, k: (i + sign(k), j, k))
    turned_left, head_out = local(
        left_kernel,
        (holder, start, blk),
        (factors, *from_first(factors), pivot_inverse, ids, ids_of_head, head)
        + (matrix[:, :WIDTH], panel[:, :WIDTH]),
        ((2 * ROWS, 2 * WIDTH), (ROWS, WIDTH)),
        flops=5 * 10**9,
    )
    shapes = ((ROWS, width), (ROWS, ROWS))
    body, change = local(
        first_kernel, (0,), (turned_left, matrix, block, side), shapes, flops=10**10
    )
    body, change = local(
        second_kernel, (0,), (turned_left, body, change, far, swap_core(side)), shapes, flops=10**9
    )
    front, solved = local(
        final_kernel,
        (holder, blk),
        (turned_left, head_out, panel, body, change, forcing, swap_core(far)),
        (matrix.shape, forcing.shape),
        flops=10**9,
    )
    return front, solved


def solution(mesh):
    in_specs = (P("cube", "blk"), P("cube", "blk"), P(), P(), P("cube"), P("blk", "cube"))
    out_specs = (P("cube", "blk"), P("blk", "cube"))
    return jax.shard_map(shards, mesh=mesh, in_specs=in_specs, out_specs=out_specs, check_vma=False)
```

```python
import jax
import jax.numpy as jnp
import numpy as np
from jax import lax
from jax.experimental import pallas as pl
from jax.experimental.pallas import tpu as pltpu
from jax.sharding import PartitionSpec as P

NX, NZ, NC, NY = 4, 8, 2, 4
ROWS = 128
WIDTH = 256
X_ORDER = (3, 1, 2)
Z_ORDER = (3, 2, 1)
Y_ORDER = (3, 1, 2)
HIGH = lax.Precision.HIGHEST


def dot(left, right):
    return jnp.dot(left, right, precision=HIGH, preferred_element_type=jnp.float32)


def after(value, *others):
    return lax.optimization_barrier((value, others))[0]


def cube_send(value, target):
    pairs = []
    for x in range(NX):
        for z in range(NZ):
            for c in range(NC):
                to = target(x, z, c)
                if to is not None:
                    tx, tz, tc = to
                    pairs.append(
                        ((x * NZ + z) * NC + c, ((tx % NX) * NZ + tz % NZ) * NC + tc % NC)
                    )
    return lax.ppermute(value, "cube", pairs)


def swap_core(value):
    return cube_send(value, lambda x, z, c: (x, z, 1 - c))


def place():
    rank = lax.axis_index("cube")
    return rank, rank >> 4, rank >> 1 & 7, rank & 1


def sign(core):
    return 1 - 2 * core


def local(kernel, place_scalars, arrays, shapes, flops=10**6):
    size = sum(4 * int(np.prod(shape)) for shape in shapes)
    return pl.pallas_call(
        kernel,
        out_shape=[jax.ShapeDtypeStruct(shape, jnp.float32) for shape in shapes],
        in_specs=[pl.BlockSpec(memory_space=pltpu.SMEM)]
        + [pl.BlockSpec(memory_space=pltpu.VMEM)] * len(arrays),
        out_specs=[pl.BlockSpec(memory_space=pltpu.VMEM)] * len(shapes),
        compiler_params=pltpu.CompilerParams(vmem_limit_bytes=40 * 2**20),
        cost_estimate=pl.CostEstimate(flops=flops, bytes_accessed=2 * size, transcendentals=0),
    )(jnp.stack([jnp.asarray(v, jnp.int32) for v in place_scalars]), *arrays)


def split(values):
    high = values.astype(jnp.bfloat16)
    rest = values - high.astype(jnp.float32)
    middle = rest.astype(jnp.bfloat16)
    return high, middle, (rest - middle.astype(jnp.float32)).astype(jnp.bfloat16)


def assemble_kernel(at_ref, front_ref, child_ref, came_ref, rows_ref, cols_ref, out_ref):
    parity, row_base, col_base = at_ref[0], at_ref[1], at_ref[2]
    count, width = came_ref.shape
    kept = child_ref[pl.ds(pl.multiple_of(parity * count, count), count), :]
    came = came_ref[...]
    even = parity == 0
    children = [jnp.where(even, kept, came), jnp.where(even, came, kept)]
    children = [jnp.concatenate(split(child), axis=0) for child in children]
    spots = lax.broadcasted_iota(jnp.int32, (ROWS, ROWS), 0) + row_base
    row_table = jnp.where(spots == rows_ref[...], 1.0, 0.0).astype(jnp.bfloat16)
    targets = lax.broadcasted_iota(jnp.int32, (2 * ROWS, ROWS), 0) + col_base
    for b in range(width // ROWS):
        span = slice(b * ROWS, (b + 1) * ROWS)
        out_span = slice(2 * b * ROWS, 2 * (b + 1) * ROWS)
        placed = []
        for k, child in enumerate(children):
            table = jnp.where(targets + 2 * b * ROWS == cols_ref[k : k + 1, span], 1.0, 0.0)
            parts = lax.dot_general(
                child[:, span],
                table.astype(jnp.bfloat16),
                (((1,), (1,)), ((), ())),
                preferred_element_type=jnp.float32,
            )
            placed.append(parts[:count] + (parts[count : 2 * count] + parts[2 * count :]))
        parts = jnp.concatenate(split(jnp.concatenate(placed, axis=0)), axis=1)
        sums = jnp.dot(row_table, parts, preferred_element_type=jnp.float32)
        size = 2 * ROWS
        sums = sums[:, :size] + (sums[:, size : 2 * size] + sums[:, 2 * size :])
        out_ref[:, out_span] = front_ref[:, out_span] + sums


def assemble(front_entries, child_blocks, child_map):
    rows_dev, front_cols = front_entries.shape
    child_cols = child_blocks.shape[1]
    half_rows = rows_dev // 2
    rank, _, _, parity = place()
    blk = lax.axis_index("blk")
    sent_rows = lax.dynamic_slice_in_dim(child_blocks, (1 - parity) * half_rows, half_rows)
    child_start = (rank >> 1) * rows_dev + parity * half_rows
    rows = lax.dynamic_slice(child_map, (0, child_start), (2, half_rows)).reshape(1, rows_dev)
    cols = lax.dynamic_slice(child_map, (0, blk * child_cols), (2, child_cols))
    return local(
        assemble_kernel,
        (parity, rank * rows_dev, blk * front_cols),
        (front_entries, child_blocks, swap_core(sent_rows), rows, cols),
        (front_entries.shape,),
        flops=10**9,
    )[0]


def dense_kernel(at_ref, index_ref, values_ref, kept_ref, sent_ref):
    x, c = at_ref[0], at_ref[1]
    s = sign(c)
    index = index_ref[...]
    values = values_ref[...]
    excites, entries = values.shape
    parts = jnp.concatenate(split(values), axis=0)
    chip = index >> 8

    def table(at, size):
        rows = lax.broadcasted_iota(jnp.int32, (size, entries), 0)
        return jnp.where(rows == at, 1.0, 0.0).astype(jnp.bfloat16)

    def summed(masks, place_table):
        rows = [parts * mask.astype(jnp.bfloat16) for mask in masks]
        placed = lax.dot_general(
            jnp.concatenate(rows, axis=0),
            place_table,
            (((1,), (1,)), ((), ())),
            preferred_element_type=jnp.float32,
        )
        placed = placed.reshape(len(masks), 3, excites, place_table.shape[0])
        return placed[:, 0] + (placed[:, 1] + placed[:, 2])

    def mask_of(condition):
        return jnp.broadcast_to(jnp.where(condition, 1.0, 0.0), (3 * excites, entries))

    near = table(index & 255, NC * ROWS)
    pivot = table((index >> 7 & 1) * 64 + (index >> 8) * 32 + (index & 31), ROWS)

    def blocks(at):
        sums = summed([mask_of(chip == at * NZ + z) for z in range(NZ)], near)
        held = (index < 2 * WIDTH) & (index >> 5 & 3 == at)
        return sums, summed([mask_of(held)], pivot)[0]

    for ref, at in ((kept_ref, x + s & 3), (sent_ref, x - s & 3)):
        sums, group = blocks(at)
        for z in range(NZ):
            ref[2 * z] = sums[z, :, :ROWS]
            ref[2 * z + 1] = sums[z, :, ROWS:]
        ref[2 * NZ] = group
    for start, at in ((17, x + 2 & 3), (26, x)):
        sums, group = blocks(at)
        for z in range(NZ):
            first, second = sums[z, :, :ROWS], sums[z, :, ROWS:]
            kept_ref[start + z] = jnp.where(c == 0, first, second)
            sent_ref[start + z] = jnp.where(c == 0, second, first)
        kept_ref[start + NZ] = jnp.where(c == 0, group, 0.0)
        sent_ref[start + NZ] = jnp.where(c == 0, 0.0, group)


def forcing_core(rhs_index, rhs_values):
    _, x, _, c = place()
    entries = rhs_values.shape[1]
    shape = (35, rhs_values.shape[0], ROWS)
    kept, sent = local(
        dense_kernel,
        (x, c),
        (rhs_index.reshape(1, entries), rhs_values),
        (shape, shape),
        flops=10**9,
    )
    return kept + swap_core(sent)


def forcing_x(summed):
    side = cube_send(summed[:17], lambda i, j, k: (i + sign(k), j, k))
    across = cube_send(summed[17:26], lambda i, j, k: (i + 2, j, k))
    return side, across, summed[26:]


def rows_kernel(at_ref, side_ref, across_ref, own_ref, kept_ref, sent_ref):
    z, c = at_ref[0], at_ref[1]
    s = sign(c)
    for ref, sgn in ((kept_ref, s), (sent_ref, -s)):
        for n in (1, 2, 3):
            i = z + n * sgn & 7
            for k in range(NC):
                mine = own_ref[i] + across_ref[i]
                ref[2 * n - 2 + k] = side_ref[2 * i + k] + jnp.where(c == k, mine, 0.0)
    for slot, i in ((6, z + 4 & 7), (7, z)):
        kept_ref[slot] = side_ref[2 * i + c] + (own_ref[i] + across_ref[i])
        sent_ref[slot] = side_ref[2 * i + 1 - c]
    pivot = side_ref[16] + (own_ref[8] + across_ref[8])
    kept_ref[8] = pivot
    sent_ref[8] = pivot


def forcing_rows(side, across, own):
    _, _, z, c = place()
    kept, sent = local(rows_kernel, (z, c), (side, across, own), (own.shape, own.shape))
    return kept, swap_core(sent)


def scatter_x(block):
    return [
        cube_send(
            block[32 * d : 32 * d + 32],
            lambda i, j, k: (d, j, k) if i == 0 and j < 2 else None,
        )
        for d in X_ORDER
    ]


def scatter_z(quarter):
    return [
        cube_send(
            quarter[8 * d : 8 * d + 8],
            lambda i, j, k: (i, (-d if j == 0 else 1 + d), k) if j < 2 else None,
        )
        for d in range(1, NZ // 2)
    ]


def message_kernel(at_ref, share_ref, other_ref, kept_ref, came_ref, *out_refs):
    c, turn = at_ref[0], at_ref[1]
    low = c == 0
    width = share_ref.shape[1]

    def columns(ref):
        left, right = ref[:, :WIDTH], ref[:, WIDTH : 2 * WIDTH]
        yield 0, jnp.where(turn == 1, right, left)
        yield WIDTH, jnp.where(turn == 1, left, right)
        yield 2 * WIDTH, ref[:, 2 * WIDTH :]

    summed = [kept_ref[i] + came_ref[i] for i in range(9)]
    for (at, mine), (_, other) in zip(columns(share_ref), columns(other_ref)):
        span = slice(at, at + mine.shape[1])
        for ref in out_refs[:3]:
            ref[:8, span] = jnp.where(low, mine, other)
            ref[8:, span] = jnp.where(low, other, mine)
        out_refs[3][:, span] = mine
    for n, ref in enumerate(out_refs[:3]):
        for i, block in enumerate((summed[2 * n], summed[2 * n + 1], summed[8])):
            ref[:, width + i * ROWS : width + (i + 1) * ROWS] = block
    first = jnp.where(low, summed[8], 0.0)
    out_refs[2][:, width + 3 * ROWS :] = summed[6]
    for i, block in enumerate((summed[6][:8], summed[6][8:], first[:8], first[8:])):
        out_refs[3][:, width + i * ROWS : width + (i + 1) * ROWS] = block
    out_refs[4][0] = summed[7]
    out_refs[4][1] = first


def unpack_kernel(
    at_ref, own_ref, up_ref, down_ref, three_ref, two_ref, one_ref, left_ref, *out_refs
):
    low = at_ref[0] == 0
    head_ref, tail_ref, mine_ref, back_ref = out_refs
    width = WIDTH + tail_ref.shape[1]
    row = 0
    far_rows = jnp.where(low, up_ref[...], down_ref[...])
    for rows in (own_ref, one_ref, two_ref, three_ref, far_rows):
        count = rows.shape[0]
        head_ref[row : row + count] = rows[:, :WIDTH]
        tail_ref[row : row + count] = rows[:, WIDTH:width]
        row += count
    spans = [slice(width + i * ROWS, width + (i + 1) * ROWS) for i in range(4)]
    sums = [one_ref[:, at] + two_ref[:, at] + three_ref[:, at] for at in spans[:3]]
    far = [far_rows[:, at] for at in spans]
    mine_ref[0] = (
        jnp.where(low, sums[0], sums[1])
        + jnp.concatenate([far[0], far[1]], axis=0)
        + left_ref[0]
    )
    pivot = sums[2] + jnp.concatenate([far[2], far[3]], axis=0) + left_ref[1]
    mine_ref[1] = pivot
    back_ref[0] = jnp.where(low, sums[1], sums[0])
    back_ref[1] = pivot


def gather_z(share, kept, came, corner_first):
    c = lax.axis_index("cube") & 1
    width = share.shape[1]
    excites = kept.shape[1]
    near = (2 * excites // 2, width + 3 * ROWS)
    *messages, left = local(
        message_kernel,
        (c, corner_first),
        (share, swap_core(share), kept, came),
        (near, near, (near[0], near[1] + ROWS), (8, width + 4 * ROWS), (2, excites, ROWS)),
    )
    got = {
        n: cube_send(messages[n - 1], lambda i, j, k: (i, j + n * sign(k), k)) for n in Z_ORDER
    }
    up = cube_send(messages[3], lambda i, j, k: (i, j + 4, k) if k == 0 else None)
    extra = got[3][:, near[1] :]
    down = jnp.concatenate(
        [got[3][8:, :width], extra[:8], extra[8:], jnp.zeros((8, 2 * ROWS), jnp.float32)], axis=1
    )
    down = cube_send(down, lambda i, j, k: (i, j - 1, k) if k == 1 else None)
    head, tail, mine, back = local(
        unpack_kernel,
        (c,),
        (messages[3], up, down, got[3], got[2], got[1], left),
        ((64, WIDTH), (64, width - WIDTH), (2, excites, ROWS), (2, excites, ROWS)),
    )
    return head, tail, mine, swap_core(back)


def tail_kernel(at_ref, mine_ref, theirs_ref, ours_ref, back_ref, order_ref, *out_refs):
    all_ref, forcing_ref = out_refs
    count, width = mine_ref.shape
    forcing_ref[...] = ours_ref[0] + back_ref[0]
    pivots = ours_ref[1] + back_ref[1]
    excites = pivots.shape[0]
    spots = lax.broadcasted_iota(jnp.int32, (ROWS, ROWS), 0)
    table = jnp.where(spots == order_ref[...], 1.0, 0.0)
    ordered = dot(pivots, table)
    filler = jnp.zeros((ROWS - excites, ROWS), jnp.float32)
    columns = jnp.concatenate([ordered, filler], axis=0).T
    all_ref[:count, :width] = mine_ref[...]
    all_ref[count:, :width] = theirs_ref[...]
    all_ref[:, width:] = columns


def rows_8(dx, dz, core):
    return [(*dx, *dz, core, r) for r in range(8)]


def rows_64(dx, flip):
    s = -1 if flip else 1
    out = rows_8(dx, (0, 0), 2 + flip)
    for n in (1, 2, 3):
        out += rows_8(dx, (-n * s, 0), 0) + rows_8(dx, (-n * s, 0), 1)
    return out + rows_8(dx, (0, 4), 2 + flip)


def rows_128(dx, flip):
    return rows_64(dx, flip) + rows_64(dx, 1 - flip)


def row_ids(rows):
    _, x, z, c = place()
    s = sign(c)
    xs, x0, zs, z0, core, r = (np.array(v, np.int32)[None] for v in zip(*rows))
    at_x = x + xs * s + x0 & 3
    at_z = z + zs * s + z0 & 7
    core = jnp.where(core > 1, c ^ (core - 2), core)
    lower = (at_z == 0) | (at_z > 4)
    pos = jnp.where(lower, 8 - at_z & 7, at_z - 1)
    return (jnp.where(lower, 0, NC) + core) * ROWS + at_x * 32 + pos * 8 + r


def head_ids():
    return row_ids(
        sum((rows_64((0, dx), flip) for flip in range(NC) for dx in (0, -1, 1, 2)), [])
    )


def tail_ids():
    return row_ids(
        rows_128((0, 0), 0)
        + rows_128((-1, 0), 0)
        + rows_64((0, 2), 0)
        + rows_128((1, 0), 1)
        + rows_64((0, 2), 1)
    )


def group_order():
    ids = row_ids(rows_128((0, 0), 0))
    return (ids >> 7 & 1) * 64 + (ids >> 8) * 32 + (ids & 31)


def spread(values, ids, first):
    count, width = values.shape
    rows = lax.broadcasted_iota(jnp.int32, (width, ids.shape[1]), 0) + first
    table = jnp.where(rows == ids, 1.0, 0.0).astype(jnp.bfloat16)
    parts = jnp.dot(
        jnp.concatenate(split(values), axis=0), table, preferred_element_type=jnp.float32
    )
    return parts[:count] + (parts[count : 2 * count] + parts[2 * count :])


def factors_kernel(
    at_ref, panel_ref, pivots_ref, ids_ref, a_ref, b_ref, c_ref, d_ref, other_ref,
    out_ref, factors_ref, head_ref
):
    holder, start = at_ref[0], at_ref[1]
    two = holder == 2
    row = 0
    for ref in (a_ref, b_ref, c_ref, d_ref, other_ref):
        head_ref[row : row + ref.shape[0]] = ref[...]
        row += ref.shape[0]

    @pl.when(at_ref[2] == 0)
    def _():
        head = head_ref[...]
        ids = ids_ref[...]
        left, right = panel_ref[:, :WIDTH], panel_ref[:, WIDTH:]
        first, second = pivots_ref[0], pivots_ref[1]
        l1 = dot(left, first)
        reduced = right - dot(spread(l1, ids, 0), head)
        l2 = dot(reduced, second)
        lead = jnp.where(two, pivots_ref[1, pl.ds(pl.multiple_of(start, ROWS), ROWS), :], l2)
        back = dot(dot(spread(lead, ids, WIDTH), head), first)
        out_ref[:, :WIDTH] = jnp.where(holder == 1, left, l1)
        out_ref[:, WIDTH:] = jnp.where(holder == 1, right, jnp.where(two, reduced, l2))
        factors_ref[:, :WIDTH] = jnp.where(two, l1, l1 - back)
        factors_ref[:, WIDTH:] = jnp.where(two, back, l2)


def left_kernel(
    at_ref, own_ref, three_ref, one_ref, two_ref, pivots_ref, ids_ref, head_ids_ref, head_ref,
    matrix_ref, panel_ref, turned_ref, out_ref
):
    holder, start, blk = at_ref[0], at_ref[1], at_ref[2]
    one, two = holder == 1, holder == 2
    factors = own_ref[...]
    for d, ref in enumerate((one_ref, two_ref, three_ref)):
        factors = jnp.where(blk == d + 1, ref[...], factors)
    first, second = factors[:, :WIDTH], factors[:, WIDTH:]
    start = pl.multiple_of(start, ROWS)
    pick_one = pivots_ref[0, pl.ds(start, ROWS), :]
    pick_two = pivots_ref[1, pl.ds(start, ROWS), :]
    front = jnp.where(one, 0.0, first), jnp.where(holder > 0, 0.0, second)
    forcing = (
        jnp.where(one, -pick_one, jnp.where(two, second, first)),
        jnp.where(one, 0.0, jnp.where(two, -pick_two, second)),
    )
    ids = ids_ref[...]
    lead = jnp.concatenate([front[0], forcing[0]], axis=0)
    rest = jnp.concatenate([front[1], forcing[1]], axis=0)
    turned_ref[...] = spread(lead, ids, 0) + spread(rest, ids, WIDTH)
    ids = head_ids_ref[...]
    turned = spread(front[0], ids, 0) + spread(front[1], ids, WIDTH)
    change = dot3(halves(turned), head_ref[...])
    out_ref[...] = jnp.where(blk == 0, panel_ref[...], matrix_ref[...] - change)


def halves(values):
    high = values.astype(jnp.bfloat16)
    return high, (values - high.astype(jnp.float32)).astype(jnp.bfloat16)


def dot3(left, rows):
    (high, low), (rows_high, rows_low) = left, halves(rows)
    count = high.shape[0]
    both = jnp.dot(
        jnp.concatenate([high, low], axis=0), rows_high, preferred_element_type=jnp.float32
    )
    rest = jnp.dot(high, rows_low, preferred_element_type=jnp.float32)
    return both[:count] + (both[count:] + rest)


def first_kernel(at_ref, left_ref, matrix_ref, block_ref, side_ref, body_ref, change_ref):
    width = body_ref.shape[1]
    rows = jnp.concatenate([block_ref[...], side_ref[...]], axis=0)
    cut = rows.shape[0]
    front, forcing = halves(left_ref[:ROWS, :cut]), halves(left_ref[ROWS:, :cut])
    for at in range(0, width, WIDTH):
        span = slice(at, at + WIDTH)
        change = dot3(front, rows[:, span])
        body_ref[:, span] = matrix_ref[:, WIDTH + at : 2 * WIDTH + at] - change
    change_ref[...] = dot3(forcing, rows[:, width:])


def second_kernel(
    at_ref, left_ref, body_ref, change_ref, far_ref, side_ref, out_ref, out_change_ref
):
    width = body_ref.shape[1]
    rows = jnp.concatenate([far_ref[...], side_ref[...]], axis=0)
    start = 256
    span = slice(start, start + rows.shape[0])
    front, forcing = halves(left_ref[:ROWS, span]), halves(left_ref[ROWS:, span])
    for at in range(0, width, WIDTH):
        span = slice(at, at + WIDTH)
        out_ref[:, span] = body_ref[:, span] - dot3(front, rows[:, span])
    out_change_ref[...] = change_ref[...] + dot3(forcing, rows[:, width:])


def final_kernel(
    at_ref, left_ref, head_ref, panel_ref, body_ref, change_ref, forcing_ref, far_ref,
    front_ref, solved_ref, block_ref, sems
):
    holder, blk = at_ref[0], at_ref[1]
    width = body_ref.shape[1]
    cut = left_ref.shape[1] - far_ref.shape[0]
    front, forcing = halves(left_ref[:ROWS, cut:]), halves(left_ref[ROWS:, cut:])
    copies = []

    def leave(at, value):
        span = pl.ds(at, WIDTH)
        block_ref[:, span] = value
        copies.append(
            pltpu.make_async_copy(
                block_ref.at[:, span], front_ref.at[:, span], sems.at[len(copies)]
            )
        )
        copies[-1].start()

    leave(0, head_ref[...])
    for at in range(0, width, WIDTH):
        span = slice(at, at + WIDTH)
        value = body_ref[:, span] - dot3(front, far_ref[:, span])
        if at == 0:
            value = jnp.where(blk == 0, panel_ref[:, WIDTH:], value)
        leave(WIDTH + at, value)
    change = change_ref[...] + dot3(forcing, far_ref[:, width:])
    kept = jnp.where(holder > 0, 0.0, forcing_ref[...])
    solved_ref[...] = kept - change.T[: kept.shape[0]]
    for copy in copies:
        copy.wait()


def from_first(value):
    got = {
        d: lax.ppermute(value, "blk", [(0, d)]) for d in Y_ORDER
    }
    return [got[d] for d in Y_ORDER]


def shards(front_entries, child_blocks, child_map, pivot_inverse, rhs_index, rhs_values):
    rank, x, z, c = place()
    blk = lax.axis_index("blk")
    holder = jnp.where(rank < 2, 1, jnp.where(rank < 4, 2, 0))
    start = (rank & 1) * ROWS
    matrix = assemble(front_entries, child_blocks, child_map)

    corner_first = (blk == 0) & ((z == 0) | (z > 4))
    sent = scatter_x(matrix)
    across_x = forcing_x(forcing_core(rhs_index, rhs_values))
    sent, across_x = lax.optimization_barrier((sent, across_x))

    quarter = jnp.where(x == 0, matrix[:32], sent[0] + sent[1] + sent[2])
    sent = scatter_z(quarter)
    kept, came = forcing_rows(*across_x)
    sent, quarter, kept, came = lax.optimization_barrier((sent, quarter, kept, came))

    share = jnp.where(z < 2, quarter[:8], sent[0] + sent[1] + sent[2])
    head, mine, ours, back = gather_z(share, kept, came, corner_first)

    head = [head] + [cube_send(head, lambda i, j, k: (i + d, j, k)) for d in (1, -1, 2)]
    count, width = mine.shape
    excites = ours.shape[1]
    block, forcing = local(
        tail_kernel,
        (c,),
        (mine, swap_core(mine), ours, back, group_order()),
        ((2 * count, width + ROWS), ours.shape[1:]),
    )
    side = cube_send(block, lambda i, j, k: (i + sign(k), j, k))

    ids, ids_of_head = tail_ids(), head_ids()
    other = swap_core(jnp.concatenate(head))
    panel, factors, head = local(
        factors_kernel,
        (holder, start, blk),
        (matrix[:, : 2 * WIDTH], pivot_inverse, ids_of_head, *head, other),
        ((ROWS, 2 * WIDTH), (ROWS, 2 * WIDTH), (2 * WIDTH, WIDTH)),
        flops=4 * 10**9,
    )
    side, panel = lax.optimization_barrier((side, panel))
    far = cube_send(side[:count], lambda i, j, k: (i + sign(k), j, k))
    turned_left, head_out = local(
        left_kernel,
        (holder, start, blk),
        (factors, *from_first(factors), pivot_inverse, ids, ids_of_head, head)
        + (matrix[:, :WIDTH], panel[:, :WIDTH]),
        ((2 * ROWS, 2 * WIDTH), (ROWS, WIDTH)),
        flops=5 * 10**9,
    )
    shapes = ((ROWS, width), (ROWS, ROWS))
    body, change = local(
        first_kernel, (0,), (turned_left, matrix, block, side), shapes, flops=10**10
    )
    body, change = local(
        second_kernel, (0,), (turned_left, body, change, far, swap_core(side)), shapes, flops=10**9
    )
    vmem = pl.BlockSpec(memory_space=pltpu.VMEM)
    arrays = (turned_left, head_out, panel, body, change, forcing, swap_core(far))
    front, solved = pl.pallas_call(
        final_kernel,
        out_shape=[
            jax.ShapeDtypeStruct(matrix.shape, jnp.float32),
            jax.ShapeDtypeStruct(forcing.shape, jnp.float32),
        ],
        in_specs=[pl.BlockSpec(memory_space=pltpu.SMEM)] + [vmem] * len(arrays),
        out_specs=[pl.BlockSpec(memory_space=pl.ANY), vmem],
        scratch_shapes=[
            pltpu.VMEM(matrix.shape, jnp.float32),
            pltpu.SemaphoreType.DMA((matrix.shape[1] // WIDTH,)),
        ],
        compiler_params=pltpu.CompilerParams(vmem_limit_bytes=40 * 2**20),
        cost_estimate=pl.CostEstimate(flops=10**9, bytes_accessed=2**21, transcendentals=0),
    )(jnp.stack([jnp.asarray(holder, jnp.int32), jnp.asarray(blk, jnp.int32)]), *arrays)
    return front, solved


def solution(mesh):
    in_specs = (P("cube", "blk"), P("cube", "blk"), P(), P(), P("cube"), P("blk", "cube"))
    out_specs = (P("cube", "blk"), P("blk", "cube"))
    return jax.shard_map(shards, mesh=mesh, in_specs=in_specs, out_specs=out_specs, check_vma=False)
```

```python
import jax
import jax.numpy as jnp
import numpy as np
from jax import lax
from jax.experimental import pallas as pl
from jax.experimental.pallas import tpu as pltpu
from jax.sharding import PartitionSpec as P

NX, NZ, NC, NY = 4, 8, 2, 4
ROWS = 128
WIDTH = 256
X_ORDER = (3, 1, 2)
Z_ORDER = (3, 2, 1)
Y_ORDER = (3, 1, 2)
HIGH = lax.Precision.HIGHEST


def dot(left, right):
    return jnp.dot(left, right, precision=HIGH, preferred_element_type=jnp.float32)


def after(value, *others):
    return lax.optimization_barrier((value, others))[0]


def cube_send(value, target):
    pairs = []
    for x in range(NX):
        for z in range(NZ):
            for c in range(NC):
                to = target(x, z, c)
                if to is not None:
                    tx, tz, tc = to
                    pairs.append(
                        ((x * NZ + z) * NC + c, ((tx % NX) * NZ + tz % NZ) * NC + tc % NC)
                    )
    return lax.ppermute(value, "cube", pairs)


def swap_core(value):
    return cube_send(value, lambda x, z, c: (x, z, 1 - c))


def place():
    rank = lax.axis_index("cube")
    return rank, rank >> 4, rank >> 1 & 7, rank & 1


def sign(core):
    return 1 - 2 * core


def local(kernel, place_scalars, arrays, shapes, flops=10**6):
    size = sum(4 * int(np.prod(shape)) for shape in shapes)
    return pl.pallas_call(
        kernel,
        out_shape=[jax.ShapeDtypeStruct(shape, jnp.float32) for shape in shapes],
        in_specs=[pl.BlockSpec(memory_space=pltpu.SMEM)]
        + [pl.BlockSpec(memory_space=pltpu.VMEM)] * len(arrays),
        out_specs=[pl.BlockSpec(memory_space=pltpu.VMEM)] * len(shapes),
        compiler_params=pltpu.CompilerParams(vmem_limit_bytes=40 * 2**20),
        cost_estimate=pl.CostEstimate(flops=flops, bytes_accessed=2 * size, transcendentals=0),
    )(jnp.stack([jnp.asarray(v, jnp.int32) for v in place_scalars]), *arrays)


def split(values):
    high = values.astype(jnp.bfloat16)
    rest = values - high.astype(jnp.float32)
    middle = rest.astype(jnp.bfloat16)
    return high, middle, (rest - middle.astype(jnp.float32)).astype(jnp.bfloat16)


def add_children(at_ref, front_ref, child_ref, came_ref, rows_ref, cols_ref, out_ref):
    parity, row_base, col_base = at_ref[0], at_ref[1], at_ref[2]
    count, width = came_ref.shape
    kept = child_ref[pl.ds(pl.multiple_of(parity * count, count), count), :]
    came = came_ref[...]
    even = parity == 0
    children = [jnp.where(even, kept, came), jnp.where(even, came, kept)]
    children = [jnp.concatenate(split(child), axis=0) for child in children]
    spots = lax.broadcasted_iota(jnp.int32, (ROWS, ROWS), 0) + row_base
    row_table = jnp.where(spots == rows_ref[...], 1.0, 0.0).astype(jnp.bfloat16)
    targets = lax.broadcasted_iota(jnp.int32, (2 * ROWS, ROWS), 0) + col_base
    for b in range(width // ROWS):
        span = slice(b * ROWS, (b + 1) * ROWS)
        out_span = slice(2 * b * ROWS, 2 * (b + 1) * ROWS)
        placed = []
        for k, child in enumerate(children):
            table = jnp.where(targets + 2 * b * ROWS == cols_ref[k : k + 1, span], 1.0, 0.0)
            parts = lax.dot_general(
                child[:, span],
                table.astype(jnp.bfloat16),
                (((1,), (1,)), ((), ())),
                preferred_element_type=jnp.float32,
            )
            placed.append(parts[:count] + (parts[count : 2 * count] + parts[2 * count :]))
        parts = jnp.concatenate(split(jnp.concatenate(placed, axis=0)), axis=1)
        sums = jnp.dot(row_table, parts, preferred_element_type=jnp.float32)
        size = 2 * ROWS
        sums = sums[:, :size] + (sums[:, size : 2 * size] + sums[:, 2 * size :])
        out_ref[:, out_span] = front_ref[:, out_span] + sums


def assemble_kernel(at_ref, *refs):
    @pl.when(at_ref[1] < NC * NC * ROWS)
    def _():
        add_children(at_ref, *refs)


def assemble_rest_kernel(at_ref, *refs):
    *given, first_ref, out_ref = refs
    holder = at_ref[1] < NC * NC * ROWS

    @pl.when(holder)
    def _():
        out_ref[...] = first_ref[...]

    @pl.when(jnp.logical_not(holder))
    def _():
        add_children(at_ref, *given, out_ref)


def assemble(front_entries, child_blocks, child_map):
    rows_dev, front_cols = front_entries.shape
    child_cols = child_blocks.shape[1]
    half_rows = rows_dev // 2
    rank, _, _, parity = place()
    blk = lax.axis_index("blk")
    sent_rows = lax.dynamic_slice_in_dim(child_blocks, (1 - parity) * half_rows, half_rows)
    child_start = (rank >> 1) * rows_dev + parity * half_rows
    rows = lax.dynamic_slice(child_map, (0, child_start), (2, half_rows)).reshape(1, rows_dev)
    cols = lax.dynamic_slice(child_map, (0, blk * child_cols), (2, child_cols))
    scalars = (parity, rank * rows_dev, blk * front_cols)
    given = (front_entries, child_blocks, swap_core(sent_rows), rows, cols)
    shapes = (front_entries.shape,)
    first = local(assemble_kernel, scalars, given, shapes, flops=10**9)[0]

    def rest(event):
        *arrays, late_rows, late_cols = given
        late = after((late_rows, late_cols), event)
        return local(
            assemble_rest_kernel, scalars, (*arrays, *late, first), shapes, flops=10**9
        )[0]

    return first, rest


def dense_kernel(at_ref, index_ref, values_ref, kept_ref, sent_ref):
    x, c = at_ref[0], at_ref[1]
    s = sign(c)
    index = index_ref[...]
    values = values_ref[...]
    excites, entries = values.shape
    parts = jnp.concatenate(split(values), axis=0)
    chip = index >> 8

    def table(at, size):
        rows = lax.broadcasted_iota(jnp.int32, (size, entries), 0)
        return jnp.where(rows == at, 1.0, 0.0).astype(jnp.bfloat16)

    def summed(masks, place_table):
        rows = [parts * mask.astype(jnp.bfloat16) for mask in masks]
        placed = lax.dot_general(
            jnp.concatenate(rows, axis=0),
            place_table,
            (((1,), (1,)), ((), ())),
            preferred_element_type=jnp.float32,
        )
        placed = placed.reshape(len(masks), 3, excites, place_table.shape[0])
        return placed[:, 0] + (placed[:, 1] + placed[:, 2])

    def mask_of(condition):
        return jnp.broadcast_to(jnp.where(condition, 1.0, 0.0), (3 * excites, entries))

    near = table(index & 255, NC * ROWS)
    pivot = table((index >> 7 & 1) * 64 + (index >> 8) * 32 + (index & 31), ROWS)

    def blocks(at):
        sums = summed([mask_of(chip == at * NZ + z) for z in range(NZ)], near)
        held = (index < 2 * WIDTH) & (index >> 5 & 3 == at)
        return sums, summed([mask_of(held)], pivot)[0]

    for ref, at in ((kept_ref, x + s & 3), (sent_ref, x - s & 3)):
        sums, group = blocks(at)
        for z in range(NZ):
            ref[2 * z] = sums[z, :, :ROWS]
            ref[2 * z + 1] = sums[z, :, ROWS:]
        ref[2 * NZ] = group
    for start, at in ((17, x + 2 & 3), (26, x)):
        sums, group = blocks(at)
        for z in range(NZ):
            first, second = sums[z, :, :ROWS], sums[z, :, ROWS:]
            kept_ref[start + z] = jnp.where(c == 0, first, second)
            sent_ref[start + z] = jnp.where(c == 0, second, first)
        kept_ref[start + NZ] = jnp.where(c == 0, group, 0.0)
        sent_ref[start + NZ] = jnp.where(c == 0, 0.0, group)


def forcing_core(rhs_index, rhs_values):
    _, x, _, c = place()
    entries = rhs_values.shape[1]
    shape = (35, rhs_values.shape[0], ROWS)
    kept, sent = local(
        dense_kernel,
        (x, c),
        (rhs_index.reshape(1, entries), rhs_values),
        (shape, shape),
        flops=10**9,
    )
    return kept + swap_core(sent)


def forcing_x(summed):
    side = cube_send(summed[:17], lambda i, j, k: (i + sign(k), j, k))
    across = cube_send(summed[17:26], lambda i, j, k: (i + 2, j, k))
    return side, across, summed[26:]


def rows_kernel(at_ref, side_ref, across_ref, own_ref, kept_ref, sent_ref):
    z, c = at_ref[0], at_ref[1]
    s = sign(c)
    for ref, sgn in ((kept_ref, s), (sent_ref, -s)):
        for n in (1, 2, 3):
            i = z + n * sgn & 7
            for k in range(NC):
                mine = own_ref[i] + across_ref[i]
                ref[2 * n - 2 + k] = side_ref[2 * i + k] + jnp.where(c == k, mine, 0.0)
    for slot, i in ((6, z + 4 & 7), (7, z)):
        kept_ref[slot] = side_ref[2 * i + c] + (own_ref[i] + across_ref[i])
        sent_ref[slot] = side_ref[2 * i + 1 - c]
    pivot = side_ref[16] + (own_ref[8] + across_ref[8])
    kept_ref[8] = pivot
    sent_ref[8] = pivot


def forcing_rows(side, across, own):
    _, _, z, c = place()
    kept, sent = local(rows_kernel, (z, c), (side, across, own), (own.shape, own.shape))
    return kept, swap_core(sent)


def scatter_x(block):
    return [
        cube_send(
            block[32 * d : 32 * d + 32],
            lambda i, j, k: (d, j, k) if i == 0 and j < 2 else None,
        )
        for d in X_ORDER
    ]


def scatter_z(quarter):
    return [
        cube_send(
            quarter[8 * d : 8 * d + 8],
            lambda i, j, k: (i, (-d if j == 0 else 1 + d), k) if j < 2 else None,
        )
        for d in range(1, NZ // 2)
    ]


def message_kernel(at_ref, share_ref, other_ref, kept_ref, came_ref, *out_refs):
    c, turn = at_ref[0], at_ref[1]
    low = c == 0
    width = share_ref.shape[1]

    def columns(ref):
        left, right = ref[:, :WIDTH], ref[:, WIDTH : 2 * WIDTH]
        yield 0, jnp.where(turn == 1, right, left)
        yield WIDTH, jnp.where(turn == 1, left, right)
        yield 2 * WIDTH, ref[:, 2 * WIDTH :]

    summed = [kept_ref[i] + came_ref[i] for i in range(9)]
    for (at, mine), (_, other) in zip(columns(share_ref), columns(other_ref)):
        span = slice(at, at + mine.shape[1])
        for ref in out_refs[:3]:
            ref[:8, span] = jnp.where(low, mine, other)
            ref[8:, span] = jnp.where(low, other, mine)
        out_refs[3][:, span] = mine
    for n, ref in enumerate(out_refs[:3]):
        for i, block in enumerate((summed[2 * n], summed[2 * n + 1], summed[8])):
            ref[:, width + i * ROWS : width + (i + 1) * ROWS] = block
    first = jnp.where(low, summed[8], 0.0)
    out_refs[2][:, width + 3 * ROWS :] = summed[6]
    for i, block in enumerate((summed[6][:8], summed[6][8:], first[:8], first[8:])):
        out_refs[3][:, width + i * ROWS : width + (i + 1) * ROWS] = block
    out_refs[4][0] = summed[7]
    out_refs[4][1] = first


def unpack_kernel(
    at_ref, own_ref, up_ref, down_ref, three_ref, two_ref, one_ref, left_ref, *out_refs
):
    low = at_ref[0] == 0
    head_ref, tail_ref, mine_ref, back_ref = out_refs
    width = WIDTH + tail_ref.shape[1]
    row = 0
    far_rows = jnp.where(low, up_ref[...], down_ref[...])
    for rows in (own_ref, one_ref, two_ref, three_ref, far_rows):
        count = rows.shape[0]
        head_ref[row : row + count] = rows[:, :WIDTH]
        tail_ref[row : row + count] = rows[:, WIDTH:width]
        row += count
    spans = [slice(width + i * ROWS, width + (i + 1) * ROWS) for i in range(4)]
    sums = [one_ref[:, at] + two_ref[:, at] + three_ref[:, at] for at in spans[:3]]
    far = [far_rows[:, at] for at in spans]
    mine_ref[0] = (
        jnp.where(low, sums[0], sums[1])
        + jnp.concatenate([far[0], far[1]], axis=0)
        + left_ref[0]
    )
    pivot = sums[2] + jnp.concatenate([far[2], far[3]], axis=0) + left_ref[1]
    mine_ref[1] = pivot
    back_ref[0] = jnp.where(low, sums[1], sums[0])
    back_ref[1] = pivot


def gather_z(share, kept, came, corner_first, beside):
    c = lax.axis_index("cube") & 1
    width = share.shape[1]
    excites = kept.shape[1]
    near = (2 * excites // 2, width + 3 * ROWS)
    *messages, left = local(
        message_kernel,
        (c, corner_first),
        (share, swap_core(share), kept, came),
        (near, near, (near[0], near[1] + ROWS), (8, width + 4 * ROWS), (2, excites, ROWS)),
    )
    got = {
        n: cube_send(messages[n - 1], lambda i, j, k: (i, j + n * sign(k), k)) for n in Z_ORDER
    }
    up = cube_send(messages[3], lambda i, j, k: (i, j + 4, k) if k == 0 else None)
    extra = got[3][:, near[1] :]
    down = jnp.concatenate(
        [got[3][8:, :width], extra[:8], extra[8:], jnp.zeros((8, 2 * ROWS), jnp.float32)], axis=1
    )
    down = cube_send(down, lambda i, j, k: (i, j - 1, k) if k == 1 else None)
    up, down, got, beside = lax.optimization_barrier((up, down, got, beside))
    head, tail, mine, back = local(
        unpack_kernel,
        (c,),
        (messages[3], up, down, got[3], got[2], got[1], left),
        ((64, WIDTH), (64, width - WIDTH), (2, excites, ROWS), (2, excites, ROWS)),
    )
    return head, tail, mine, swap_core(back), beside


def tail_kernel(at_ref, mine_ref, theirs_ref, ours_ref, back_ref, order_ref, *out_refs):
    all_ref, forcing_ref = out_refs
    count, width = mine_ref.shape
    forcing_ref[...] = ours_ref[0] + back_ref[0]
    pivots = ours_ref[1] + back_ref[1]
    excites = pivots.shape[0]
    spots = lax.broadcasted_iota(jnp.int32, (ROWS, ROWS), 0)
    table = jnp.where(spots == order_ref[...], 1.0, 0.0)
    ordered = dot(pivots, table)
    filler = jnp.zeros((ROWS - excites, ROWS), jnp.float32)
    columns = jnp.concatenate([ordered, filler], axis=0).T
    all_ref[:count, :width] = mine_ref[...]
    all_ref[count:, :width] = theirs_ref[...]
    all_ref[:, width:] = columns


def rows_8(dx, dz, core):
    return [(*dx, *dz, core, r) for r in range(8)]


def rows_64(dx, flip):
    s = -1 if flip else 1
    out = rows_8(dx, (0, 0), 2 + flip)
    for n in (1, 2, 3):
        out += rows_8(dx, (-n * s, 0), 0) + rows_8(dx, (-n * s, 0), 1)
    return out + rows_8(dx, (0, 4), 2 + flip)


def rows_128(dx, flip):
    return rows_64(dx, flip) + rows_64(dx, 1 - flip)


def row_ids(rows):
    _, x, z, c = place()
    s = sign(c)
    xs, x0, zs, z0, core, r = (np.array(v, np.int32)[None] for v in zip(*rows))
    at_x = x + xs * s + x0 & 3
    at_z = z + zs * s + z0 & 7
    core = jnp.where(core > 1, c ^ (core - 2), core)
    lower = (at_z == 0) | (at_z > 4)
    pos = jnp.where(lower, 8 - at_z & 7, at_z - 1)
    return (jnp.where(lower, 0, NC) + core) * ROWS + at_x * 32 + pos * 8 + r


def head_ids():
    return row_ids(
        sum((rows_64((0, dx), flip) for flip in range(NC) for dx in (0, -1, 1, 2)), [])
    )


def tail_ids():
    return row_ids(
        rows_128((0, 0), 0)
        + rows_128((-1, 0), 0)
        + rows_64((0, 2), 0)
        + rows_128((1, 0), 1)
        + rows_64((0, 2), 1)
    )


def group_order():
    ids = row_ids(rows_128((0, 0), 0))
    return (ids >> 7 & 1) * 64 + (ids >> 8) * 32 + (ids & 31)


def spread(values, ids, first):
    count, width = values.shape
    rows = lax.broadcasted_iota(jnp.int32, (width, ids.shape[1]), 0) + first
    table = jnp.where(rows == ids, 1.0, 0.0).astype(jnp.bfloat16)
    parts = jnp.dot(
        jnp.concatenate(split(values), axis=0), table, preferred_element_type=jnp.float32
    )
    return parts[:count] + (parts[count : 2 * count] + parts[2 * count :])


def factors_kernel(
    at_ref, panel_ref, pivots_ref, ids_ref, a_ref, b_ref, c_ref, d_ref, other_ref,
    out_ref, factors_ref, head_ref
):
    holder, start = at_ref[0], at_ref[1]
    two = holder == 2
    row = 0
    for ref in (a_ref, b_ref, c_ref, d_ref, other_ref):
        head_ref[row : row + ref.shape[0]] = ref[...]
        row += ref.shape[0]

    @pl.when(at_ref[2] == 0)
    def _():
        head = head_ref[...]
        ids = ids_ref[...]
        left, right = panel_ref[:, :WIDTH], panel_ref[:, WIDTH:]
        first, second = pivots_ref[0], pivots_ref[1]
        l1 = dot(left, first)
        reduced = right - dot(spread(l1, ids, 0), head)
        l2 = dot(reduced, second)
        lead = jnp.where(two, pivots_ref[1, pl.ds(pl.multiple_of(start, ROWS), ROWS), :], l2)
        back = dot(dot(spread(lead, ids, WIDTH), head), first)
        out_ref[:, :WIDTH] = jnp.where(holder == 1, left, l1)
        out_ref[:, WIDTH:] = jnp.where(holder == 1, right, jnp.where(two, reduced, l2))
        factors_ref[:, :WIDTH] = jnp.where(two, l1, l1 - back)
        factors_ref[:, WIDTH:] = jnp.where(two, back, l2)


def left_kernel(
    at_ref, own_ref, three_ref, one_ref, two_ref, pivots_ref, ids_ref, head_ids_ref, head_ref,
    matrix_ref, panel_ref, turned_ref, out_ref
):
    holder, start, blk = at_ref[0], at_ref[1], at_ref[2]
    one, two = holder == 1, holder == 2
    factors = own_ref[...]
    for d, ref in enumerate((one_ref, two_ref, three_ref)):
        factors = jnp.where(blk == d + 1, ref[...], factors)
    first, second = factors[:, :WIDTH], factors[:, WIDTH:]
    start = pl.multiple_of(start, ROWS)
    pick_one = pivots_ref[0, pl.ds(start, ROWS), :]
    pick_two = pivots_ref[1, pl.ds(start, ROWS), :]
    front = jnp.where(one, 0.0, first), jnp.where(holder > 0, 0.0, second)
    forcing = (
        jnp.where(one, -pick_one, jnp.where(two, second, first)),
        jnp.where(one, 0.0, jnp.where(two, -pick_two, second)),
    )
    ids = ids_ref[...]
    lead = jnp.concatenate([front[0], forcing[0]], axis=0)
    rest = jnp.concatenate([front[1], forcing[1]], axis=0)
    turned_ref[...] = spread(lead, ids, 0) + spread(rest, ids, WIDTH)
    ids = head_ids_ref[...]
    turned = spread(front[0], ids, 0) + spread(front[1], ids, WIDTH)
    change = dot3(halves(turned), head_ref[...])
    out_ref[...] = jnp.where(blk == 0, panel_ref[...], matrix_ref[...] - change)


def halves(values):
    high = values.astype(jnp.bfloat16)
    return high, (values - high.astype(jnp.float32)).astype(jnp.bfloat16)


def dot3(left, rows):
    (high, low), (rows_high, rows_low) = left, halves(rows)
    count = high.shape[0]
    both = jnp.dot(
        jnp.concatenate([high, low], axis=0), rows_high, preferred_element_type=jnp.float32
    )
    rest = jnp.dot(high, rows_low, preferred_element_type=jnp.float32)
    return both[:count] + (both[count:] + rest)


def first_kernel(at_ref, left_ref, matrix_ref, block_ref, side_ref, body_ref, change_ref):
    width = body_ref.shape[1]
    rows = jnp.concatenate([block_ref[...], side_ref[...]], axis=0)
    cut = rows.shape[0]
    front, forcing = halves(left_ref[:ROWS, :cut]), halves(left_ref[ROWS:, :cut])
    for at in range(0, width, WIDTH):
        span = slice(at, at + WIDTH)
        change = dot3(front, rows[:, span])
        body_ref[:, span] = matrix_ref[:, WIDTH + at : 2 * WIDTH + at] - change
    change_ref[...] = dot3(forcing, rows[:, width:])


def second_kernel(
    at_ref, left_ref, body_ref, change_ref, far_ref, side_ref, out_ref, out_change_ref
):
    width = body_ref.shape[1]
    rows = jnp.concatenate([far_ref[...], side_ref[...]], axis=0)
    start = 256
    span = slice(start, start + rows.shape[0])
    front, forcing = halves(left_ref[:ROWS, span]), halves(left_ref[ROWS:, span])
    for at in range(0, width, WIDTH):
        span = slice(at, at + WIDTH)
        out_ref[:, span] = body_ref[:, span] - dot3(front, rows[:, span])
    out_change_ref[...] = change_ref[...] + dot3(forcing, rows[:, width:])


def final_kernel(
    at_ref, left_ref, head_ref, panel_ref, body_ref, change_ref, forcing_ref, far_ref,
    front_ref, solved_ref
):
    holder, blk = at_ref[0], at_ref[1]
    width = body_ref.shape[1]
    cut = left_ref.shape[1] - far_ref.shape[0]
    front, forcing = halves(left_ref[:ROWS, cut:]), halves(left_ref[ROWS:, cut:])
    front_ref[:, :WIDTH] = head_ref[...]
    for at in range(0, width, WIDTH):
        span = slice(at, at + WIDTH)
        value = body_ref[:, span] - dot3(front, far_ref[:, span])
        if at == 0:
            value = jnp.where(blk == 0, panel_ref[:, WIDTH:], value)
        front_ref[:, WIDTH + at : 2 * WIDTH + at] = value
    change = change_ref[...] + dot3(forcing, far_ref[:, width:])
    kept = jnp.where(holder > 0, 0.0, forcing_ref[...])
    solved_ref[...] = kept - change.T[: kept.shape[0]]


def from_first(value):
    got = {
        d: lax.ppermute(value, "blk", [(0, d)]) for d in Y_ORDER
    }
    return [got[d] for d in Y_ORDER]


def shards(front_entries, child_blocks, child_map, pivot_inverse, rhs_index, rhs_values):
    rank, x, z, c = place()
    blk = lax.axis_index("blk")
    holder = jnp.where(rank < 2, 1, jnp.where(rank < 4, 2, 0))
    start = (rank & 1) * ROWS
    matrix, rest = assemble(front_entries, child_blocks, child_map)

    corner_first = (blk == 0) & ((z == 0) | (z > 4))
    sent = scatter_x(matrix)
    across_x = forcing_x(forcing_core(rhs_index, rhs_values))
    sent, across_x = lax.optimization_barrier((sent, across_x))

    quarter = jnp.where(x == 0, matrix[:32], sent[0] + sent[1] + sent[2])
    sent = scatter_z(quarter)
    kept, came = forcing_rows(*across_x)
    sent, quarter, kept, came = lax.optimization_barrier((sent, quarter, kept, came))

    share = jnp.where(z < 2, quarter[:8], sent[0] + sent[1] + sent[2])
    head, mine, ours, back, matrix = gather_z(share, kept, came, corner_first, rest(share))

    count, width = mine.shape
    excites = ours.shape[1]
    block, forcing = local(
        tail_kernel,
        (c,),
        (mine, swap_core(mine), ours, back, group_order()),
        ((2 * count, width + ROWS), ours.shape[1:]),
    )
    late, block = lax.optimization_barrier((head, block))
    head = [
        head,
        *(cube_send(late, lambda i, j, k: (i + d, j, k)) for d in (1, -1)),
        cube_send(head, lambda i, j, k: (i + 2, j, k)),
    ]
    side = cube_send(block, lambda i, j, k: (i + sign(k), j, k))

    ids, ids_of_head = tail_ids(), head_ids()
    other = swap_core(jnp.concatenate(head))
    panel, factors, head = local(
        factors_kernel,
        (holder, start, blk),
        (matrix[:, : 2 * WIDTH], pivot_inverse, ids_of_head, *head, other),
        ((ROWS, 2 * WIDTH), (ROWS, 2 * WIDTH), (2 * WIDTH, WIDTH)),
        flops=4 * 10**9,
    )
    side, panel = lax.optimization_barrier((side, panel))
    far = cube_send(side[:count], lambda i, j, k: (i + sign(k), j, k))
    turned_left, head_out = local(
        left_kernel,
        (holder, start, blk),
        (factors, *from_first(factors), pivot_inverse, ids, ids_of_head, head)
        + (matrix[:, :WIDTH], panel[:, :WIDTH]),
        ((2 * ROWS, 2 * WIDTH), (ROWS, WIDTH)),
        flops=5 * 10**9,
    )
    shapes = ((ROWS, width), (ROWS, ROWS))
    body, change = local(
        first_kernel, (0,), (turned_left, matrix, block, side), shapes, flops=10**10
    )
    body, change = local(
        second_kernel, (0,), (turned_left, body, change, far, swap_core(side)), shapes, flops=10**9
    )
    front, solved = local(
        final_kernel,
        (holder, blk),
        (turned_left, head_out, panel, body, change, forcing, swap_core(far)),
        (matrix.shape, forcing.shape),
        flops=10**9,
    )
    return front, solved


def solution(mesh):
    in_specs = (P("cube", "blk"), P("cube", "blk"), P(), P(), P("cube"), P("blk", "cube"))
    out_specs = (P("cube", "blk"), P("blk", "cube"))
    return jax.shard_map(shards, mesh=mesh, in_specs=in_specs, out_specs=out_specs, check_vma=False)
```

```python
import jax
import jax.numpy as jnp
import numpy as np
from jax import lax
from jax.experimental import pallas as pl
from jax.experimental.pallas import tpu as pltpu
from jax.sharding import PartitionSpec as P

NX, NZ, NC, NY = 4, 8, 2, 4
ROWS = 128
WIDTH = 256
X_ORDER = (3, 1, 2)
Z_ORDER = (3, 2, 1)
Y_ORDER = (3, 1, 2)
HIGH = lax.Precision.HIGHEST


def dot(left, right):
    return jnp.dot(left, right, precision=HIGH, preferred_element_type=jnp.float32)


def after(value, *others):
    return lax.optimization_barrier((value, others))[0]


def cube_send(value, target):
    pairs = []
    for x in range(NX):
        for z in range(NZ):
            for c in range(NC):
                to = target(x, z, c)
                if to is not None:
                    tx, tz, tc = to
                    pairs.append(
                        ((x * NZ + z) * NC + c, ((tx % NX) * NZ + tz % NZ) * NC + tc % NC)
                    )
    return lax.ppermute(value, "cube", pairs)


def swap_core(value):
    return cube_send(value, lambda x, z, c: (x, z, 1 - c))


def place():
    rank = lax.axis_index("cube")
    return rank, rank >> 4, rank >> 1 & 7, rank & 1


def sign(core):
    return 1 - 2 * core


def local(kernel, place_scalars, arrays, shapes, flops=10**6):
    size = sum(4 * int(np.prod(shape)) for shape in shapes)
    return pl.pallas_call(
        kernel,
        out_shape=[jax.ShapeDtypeStruct(shape, jnp.float32) for shape in shapes],
        in_specs=[pl.BlockSpec(memory_space=pltpu.SMEM)]
        + [pl.BlockSpec(memory_space=pltpu.VMEM)] * len(arrays),
        out_specs=[pl.BlockSpec(memory_space=pltpu.VMEM)] * len(shapes),
        compiler_params=pltpu.CompilerParams(vmem_limit_bytes=40 * 2**20),
        cost_estimate=pl.CostEstimate(flops=flops, bytes_accessed=2 * size, transcendentals=0),
    )(jnp.stack([jnp.asarray(v, jnp.int32) for v in place_scalars]), *arrays)


def split(values):
    high = values.astype(jnp.bfloat16)
    rest = values - high.astype(jnp.float32)
    middle = rest.astype(jnp.bfloat16)
    return high, middle, (rest - middle.astype(jnp.float32)).astype(jnp.bfloat16)


def add_children(at_ref, front_ref, child_ref, came_ref, rows_ref, cols_ref, out_ref):
    parity, row_base, col_base = at_ref[0], at_ref[1], at_ref[2]
    count, width = came_ref.shape
    kept = child_ref[pl.ds(pl.multiple_of(parity * count, count), count), :]
    came = came_ref[...]
    even = parity == 0
    children = [jnp.where(even, kept, came), jnp.where(even, came, kept)]
    children = [jnp.concatenate(split(child), axis=0) for child in children]
    spots = lax.broadcasted_iota(jnp.int32, (ROWS, ROWS), 0) + row_base
    row_table = jnp.where(spots == rows_ref[...], 1.0, 0.0).astype(jnp.bfloat16)
    targets = lax.broadcasted_iota(jnp.int32, (2 * ROWS, ROWS), 0) + col_base
    for b in range(width // ROWS):
        span = slice(b * ROWS, (b + 1) * ROWS)
        out_span = slice(2 * b * ROWS, 2 * (b + 1) * ROWS)
        placed = []
        for k, child in enumerate(children):
            table = jnp.where(targets + 2 * b * ROWS == cols_ref[k : k + 1, span], 1.0, 0.0)
            parts = lax.dot_general(
                child[:, span],
                table.astype(jnp.bfloat16),
                (((1,), (1,)), ((), ())),
                preferred_element_type=jnp.float32,
            )
            placed.append(parts[:count] + (parts[count : 2 * count] + parts[2 * count :]))
        parts = jnp.concatenate(split(jnp.concatenate(placed, axis=0)), axis=1)
        sums = jnp.dot(row_table, parts, preferred_element_type=jnp.float32)
        size = 2 * ROWS
        sums = sums[:, :size] + (sums[:, size : 2 * size] + sums[:, 2 * size :])
        out_ref[:, out_span] = front_ref[:, out_span] + sums


def assemble_kernel(at_ref, *refs):
    *given, out_ref, kept_ref = refs

    @pl.when(at_ref[1] < NC * NC * ROWS)
    def _():
        add_children(at_ref, *given, out_ref)
        kept_ref[...] = out_ref[: kept_ref.shape[0]]


def assemble_rest_kernel(at_ref, *refs):
    *given, first_ref, out_ref = refs
    holder = at_ref[1] < NC * NC * ROWS

    @pl.when(holder)
    def _():
        out_ref[...] = first_ref[...]

    @pl.when(jnp.logical_not(holder))
    def _():
        add_children(at_ref, *given, out_ref)


def assemble(front_entries, child_blocks, child_map):
    rows_dev, front_cols = front_entries.shape
    child_cols = child_blocks.shape[1]
    half_rows = rows_dev // 2
    rank, _, _, parity = place()
    blk = lax.axis_index("blk")
    sent_rows = lax.dynamic_slice_in_dim(child_blocks, (1 - parity) * half_rows, half_rows)
    child_start = (rank >> 1) * rows_dev + parity * half_rows
    rows = lax.dynamic_slice(child_map, (0, child_start), (2, half_rows)).reshape(1, rows_dev)
    cols = lax.dynamic_slice(child_map, (0, blk * child_cols), (2, child_cols))
    scalars = (parity, rank * rows_dev, blk * front_cols)
    given = (front_entries, child_blocks, swap_core(sent_rows), rows, cols)
    shapes = (front_entries.shape,)
    quarter = (rows_dev // NX, front_cols)
    first, kept = local(assemble_kernel, scalars, given, (*shapes, quarter), flops=10**9)

    def rest(event):
        *arrays, late_rows, late_cols = given
        late = after((late_rows, late_cols), event)
        return local(
            assemble_rest_kernel, scalars, (*arrays, *late, first), shapes, flops=10**9
        )[0]

    return first, kept, rest


def dense_kernel(at_ref, index_ref, values_ref, kept_ref, sent_ref):
    x, c = at_ref[0], at_ref[1]
    s = sign(c)
    index = index_ref[...]
    values = values_ref[...]
    excites, entries = values.shape
    parts = jnp.concatenate(split(values), axis=0)
    chip = index >> 8

    def table(at, size):
        rows = lax.broadcasted_iota(jnp.int32, (size, entries), 0)
        return jnp.where(rows == at, 1.0, 0.0).astype(jnp.bfloat16)

    def summed(masks, place_table):
        rows = [parts * mask.astype(jnp.bfloat16) for mask in masks]
        placed = lax.dot_general(
            jnp.concatenate(rows, axis=0),
            place_table,
            (((1,), (1,)), ((), ())),
            preferred_element_type=jnp.float32,
        )
        placed = placed.reshape(len(masks), 3, excites, place_table.shape[0])
        return placed[:, 0] + (placed[:, 1] + placed[:, 2])

    def mask_of(condition):
        return jnp.broadcast_to(jnp.where(condition, 1.0, 0.0), (3 * excites, entries))

    near = table(index & 255, NC * ROWS)
    pivot = table((index >> 7 & 1) * 64 + (index >> 8) * 32 + (index & 31), ROWS)

    def blocks(at):
        sums = summed([mask_of(chip == at * NZ + z) for z in range(NZ)], near)
        held = (index < 2 * WIDTH) & (index >> 5 & 3 == at)
        return sums, summed([mask_of(held)], pivot)[0]

    for ref, at in ((kept_ref, x + s & 3), (sent_ref, x - s & 3)):
        sums, group = blocks(at)
        for z in range(NZ):
            ref[2 * z] = sums[z, :, :ROWS]
            ref[2 * z + 1] = sums[z, :, ROWS:]
        ref[2 * NZ] = group
    for start, at in ((17, x + 2 & 3), (26, x)):
        sums, group = blocks(at)
        for z in range(NZ):
            first, second = sums[z, :, :ROWS], sums[z, :, ROWS:]
            kept_ref[start + z] = jnp.where(c == 0, first, second)
            sent_ref[start + z] = jnp.where(c == 0, second, first)
        kept_ref[start + NZ] = jnp.where(c == 0, group, 0.0)
        sent_ref[start + NZ] = jnp.where(c == 0, 0.0, group)


def forcing_core(rhs_index, rhs_values):
    _, x, _, c = place()
    entries = rhs_values.shape[1]
    shape = (35, rhs_values.shape[0], ROWS)
    kept, sent = local(
        dense_kernel,
        (x, c),
        (rhs_index.reshape(1, entries), rhs_values),
        (shape, shape),
        flops=10**9,
    )
    return kept + swap_core(sent)


def forcing_x(summed):
    side = cube_send(summed[:17], lambda i, j, k: (i + sign(k), j, k))
    across = cube_send(summed[17:26], lambda i, j, k: (i + 2, j, k))
    return side, across, summed[26:]


def rows_kernel(at_ref, side_ref, across_ref, own_ref, kept_ref, sent_ref):
    z, c = at_ref[0], at_ref[1]
    s = sign(c)
    for ref, sgn in ((kept_ref, s), (sent_ref, -s)):
        for n in (1, 2, 3):
            i = z + n * sgn & 7
            for k in range(NC):
                mine = own_ref[i] + across_ref[i]
                ref[2 * n - 2 + k] = side_ref[2 * i + k] + jnp.where(c == k, mine, 0.0)
    for slot, i in ((6, z + 4 & 7), (7, z)):
        kept_ref[slot] = side_ref[2 * i + c] + (own_ref[i] + across_ref[i])
        sent_ref[slot] = side_ref[2 * i + 1 - c]
    pivot = side_ref[16] + (own_ref[8] + across_ref[8])
    kept_ref[8] = pivot
    sent_ref[8] = pivot


def forcing_rows(side, across, own):
    _, _, z, c = place()
    kept, sent = local(rows_kernel, (z, c), (side, across, own), (own.shape, own.shape))
    return kept, swap_core(sent)


def scatter_x(block):
    return [
        cube_send(
            block[32 * d : 32 * d + 32],
            lambda i, j, k: (d, j, k) if i == 0 and j < 2 else None,
        )
        for d in X_ORDER
    ]


def scatter_z(quarter):
    return [
        cube_send(
            quarter[8 * d : 8 * d + 8],
            lambda i, j, k: (i, (-d if j == 0 else 1 + d), k) if j < 2 else None,
        )
        for d in range(1, NZ // 2)
    ]


def message_kernel(at_ref, share_ref, other_ref, kept_ref, came_ref, *out_refs):
    c, turn = at_ref[0], at_ref[1]
    low = c == 0
    width = share_ref.shape[1]

    def columns(ref):
        left, right = ref[:, :WIDTH], ref[:, WIDTH : 2 * WIDTH]
        yield 0, jnp.where(turn == 1, right, left)
        yield WIDTH, jnp.where(turn == 1, left, right)
        yield 2 * WIDTH, ref[:, 2 * WIDTH :]

    summed = [kept_ref[i] + came_ref[i] for i in range(9)]
    for (at, mine), (_, other) in zip(columns(share_ref), columns(other_ref)):
        span = slice(at, at + mine.shape[1])
        for ref in out_refs[:3]:
            ref[:8, span] = jnp.where(low, mine, other)
            ref[8:, span] = jnp.where(low, other, mine)
        out_refs[3][:, span] = mine
    for n, ref in enumerate(out_refs[:3]):
        for i, block in enumerate((summed[2 * n], summed[2 * n + 1], summed[8])):
            ref[:, width + i * ROWS : width + (i + 1) * ROWS] = block
    first = jnp.where(low, summed[8], 0.0)
    out_refs[2][:, width + 3 * ROWS :] = summed[6]
    for i, block in enumerate((summed[6][:8], summed[6][8:], first[:8], first[8:])):
        out_refs[3][:, width + i * ROWS : width + (i + 1) * ROWS] = block
    out_refs[4][0] = summed[7]
    out_refs[4][1] = first


def unpack_kernel(
    at_ref, own_ref, up_ref, down_ref, three_ref, two_ref, one_ref, left_ref, *out_refs
):
    low = at_ref[0] == 0
    head_ref, tail_ref, mine_ref, back_ref = out_refs
    width = WIDTH + tail_ref.shape[1]
    row = 0
    far_rows = jnp.where(low, up_ref[...], down_ref[...])
    for rows in (own_ref, one_ref, two_ref, three_ref, far_rows):
        count = rows.shape[0]
        head_ref[row : row + count] = rows[:, :WIDTH]
        tail_ref[row : row + count] = rows[:, WIDTH:width]
        row += count
    spans = [slice(width + i * ROWS, width + (i + 1) * ROWS) for i in range(4)]
    sums = [one_ref[:, at] + two_ref[:, at] + three_ref[:, at] for at in spans[:3]]
    far = [far_rows[:, at] for at in spans]
    mine_ref[0] = (
        jnp.where(low, sums[0], sums[1])
        + jnp.concatenate([far[0], far[1]], axis=0)
        + left_ref[0]
    )
    pivot = sums[2] + jnp.concatenate([far[2], far[3]], axis=0) + left_ref[1]
    mine_ref[1] = pivot
    back_ref[0] = jnp.where(low, sums[1], sums[0])
    back_ref[1] = pivot


def gather_z(share, kept, came, corner_first, beside):
    c = lax.axis_index("cube") & 1
    width = share.shape[1]
    excites = kept.shape[1]
    near = (2 * excites // 2, width + 3 * ROWS)
    *messages, left = local(
        message_kernel,
        (c, corner_first),
        (share, swap_core(share), kept, came),
        (near, near, (near[0], near[1] + ROWS), (8, width + 4 * ROWS), (2, excites, ROWS)),
    )
    got = {
        n: cube_send(messages[n - 1], lambda i, j, k: (i, j + n * sign(k), k)) for n in Z_ORDER
    }
    up = cube_send(messages[3], lambda i, j, k: (i, j + 4, k) if k == 0 else None)
    extra = got[3][:, near[1] :]
    down = jnp.concatenate(
        [got[3][8:, :width], extra[:8], extra[8:], jnp.zeros((8, 2 * ROWS), jnp.float32)], axis=1
    )
    down = cube_send(down, lambda i, j, k: (i, j - 1, k) if k == 1 else None)
    up, down, got, beside = lax.optimization_barrier((up, down, got, beside))
    head, tail, mine, back = local(
        unpack_kernel,
        (c,),
        (messages[3], up, down, got[3], got[2], got[1], left),
        ((64, WIDTH), (64, width - WIDTH), (2, excites, ROWS), (2, excites, ROWS)),
    )
    return head, tail, mine, swap_core(back), beside


def tail_kernel(at_ref, mine_ref, theirs_ref, ours_ref, back_ref, order_ref, *out_refs):
    all_ref, forcing_ref = out_refs
    count, width = mine_ref.shape
    forcing_ref[...] = ours_ref[0] + back_ref[0]
    pivots = ours_ref[1] + back_ref[1]
    excites = pivots.shape[0]
    spots = lax.broadcasted_iota(jnp.int32, (ROWS, ROWS), 0)
    table = jnp.where(spots == order_ref[...], 1.0, 0.0)
    ordered = dot(pivots, table)
    filler = jnp.zeros((ROWS - excites, ROWS), jnp.float32)
    columns = jnp.concatenate([ordered, filler], axis=0).T
    all_ref[:count, :width] = mine_ref[...]
    all_ref[count:, :width] = theirs_ref[...]
    all_ref[:, width:] = columns


def rows_8(dx, dz, core):
    return [(*dx, *dz, core, r) for r in range(8)]


def rows_64(dx, flip):
    s = -1 if flip else 1
    out = rows_8(dx, (0, 0), 2 + flip)
    for n in (1, 2, 3):
        out += rows_8(dx, (-n * s, 0), 0) + rows_8(dx, (-n * s, 0), 1)
    return out + rows_8(dx, (0, 4), 2 + flip)


def rows_128(dx, flip):
    return rows_64(dx, flip) + rows_64(dx, 1 - flip)


def row_ids(rows):
    _, x, z, c = place()
    s = sign(c)
    xs, x0, zs, z0, core, r = (np.array(v, np.int32)[None] for v in zip(*rows))
    at_x = x + xs * s + x0 & 3
    at_z = z + zs * s + z0 & 7
    core = jnp.where(core > 1, c ^ (core - 2), core)
    lower = (at_z == 0) | (at_z > 4)
    pos = jnp.where(lower, 8 - at_z & 7, at_z - 1)
    return (jnp.where(lower, 0, NC) + core) * ROWS + at_x * 32 + pos * 8 + r


def head_ids():
    return row_ids(
        sum((rows_64((0, dx), flip) for flip in range(NC) for dx in (0, -1, 1, 2)), [])
    )


def tail_ids():
    return row_ids(
        rows_128((0, 0), 0)
        + rows_128((-1, 0), 0)
        + rows_64((0, 2), 0)
        + rows_128((1, 0), 1)
        + rows_64((0, 2), 1)
    )


def group_order():
    ids = row_ids(rows_128((0, 0), 0))
    return (ids >> 7 & 1) * 64 + (ids >> 8) * 32 + (ids & 31)


def spread(values, ids, first):
    count, width = values.shape
    rows = lax.broadcasted_iota(jnp.int32, (width, ids.shape[1]), 0) + first
    table = jnp.where(rows == ids, 1.0, 0.0).astype(jnp.bfloat16)
    parts = jnp.dot(
        jnp.concatenate(split(values), axis=0), table, preferred_element_type=jnp.float32
    )
    return parts[:count] + (parts[count : 2 * count] + parts[2 * count :])


def factors_kernel(
    at_ref, panel_ref, pivots_ref, ids_ref, a_ref, b_ref, c_ref, d_ref, other_ref,
    out_ref, factors_ref, head_ref
):
    holder, start = at_ref[0], at_ref[1]
    two = holder == 2
    row = 0
    for ref in (a_ref, b_ref, c_ref, d_ref, other_ref):
        head_ref[row : row + ref.shape[0]] = ref[...]
        row += ref.shape[0]

    @pl.when(at_ref[2] == 0)
    def _():
        head = head_ref[...]
        ids = ids_ref[...]
        left, right = panel_ref[:, :WIDTH], panel_ref[:, WIDTH:]
        first, second = pivots_ref[0], pivots_ref[1]
        l1 = dot(left, first)
        reduced = right - dot(spread(l1, ids, 0), head)
        l2 = dot(reduced, second)
        lead = jnp.where(two, pivots_ref[1, pl.ds(pl.multiple_of(start, ROWS), ROWS), :], l2)
        back = dot(dot(spread(lead, ids, WIDTH), head), first)
        out_ref[:, :WIDTH] = jnp.where(holder == 1, left, l1)
        out_ref[:, WIDTH:] = jnp.where(holder == 1, right, jnp.where(two, reduced, l2))
        factors_ref[:, :WIDTH] = jnp.where(two, l1, l1 - back)
        factors_ref[:, WIDTH:] = jnp.where(two, back, l2)


def left_kernel(
    at_ref, own_ref, three_ref, one_ref, two_ref, pivots_ref, ids_ref, head_ids_ref, head_ref,
    matrix_ref, panel_ref, turned_ref, out_ref
):
    holder, start, blk = at_ref[0], at_ref[1], at_ref[2]
    one, two = holder == 1, holder == 2
    factors = own_ref[...]
    for d, ref in enumerate((one_ref, two_ref, three_ref)):
        factors = jnp.where(blk == d + 1, ref[...], factors)
    first, second = factors[:, :WIDTH], factors[:, WIDTH:]
    start = pl.multiple_of(start, ROWS)
    pick_one = pivots_ref[0, pl.ds(start, ROWS), :]
    pick_two = pivots_ref[1, pl.ds(start, ROWS), :]
    front = jnp.where(one, 0.0, first), jnp.where(holder > 0, 0.0, second)
    forcing = (
        jnp.where(one, -pick_one, jnp.where(two, second, first)),
        jnp.where(one, 0.0, jnp.where(two, -pick_two, second)),
    )
    ids = ids_ref[...]
    lead = jnp.concatenate([front[0], forcing[0]], axis=0)
    rest = jnp.concatenate([front[1], forcing[1]], axis=0)
    turned_ref[...] = spread(lead, ids, 0) + spread(rest, ids, WIDTH)
    ids = head_ids_ref[...]
    turned = spread(front[0], ids, 0) + spread(front[1], ids, WIDTH)
    change = dot3(halves(turned), head_ref[...])
    out_ref[...] = jnp.where(blk == 0, panel_ref[...], matrix_ref[...] - change)


def halves(values):
    high = values.astype(jnp.bfloat16)
    return high, (values - high.astype(jnp.float32)).astype(jnp.bfloat16)


def dot3(left, rows):
    (high, low), (rows_high, rows_low) = left, halves(rows)
    count = high.shape[0]
    both = jnp.dot(
        jnp.concatenate([high, low], axis=0), rows_high, preferred_element_type=jnp.float32
    )
    rest = jnp.dot(high, rows_low, preferred_element_type=jnp.float32)
    return both[:count] + (both[count:] + rest)


def first_kernel(at_ref, left_ref, matrix_ref, block_ref, side_ref, body_ref, change_ref):
    width = body_ref.shape[1]
    rows = jnp.concatenate([block_ref[...], side_ref[...]], axis=0)
    cut = rows.shape[0]
    front, forcing = halves(left_ref[:ROWS, :cut]), halves(left_ref[ROWS:, :cut])
    for at in range(0, width, WIDTH):
        span = slice(at, at + WIDTH)
        change = dot3(front, rows[:, span])
        body_ref[:, span] = matrix_ref[:, WIDTH + at : 2 * WIDTH + at] - change
    change_ref[...] = dot3(forcing, rows[:, width:])


def second_kernel(
    at_ref, left_ref, body_ref, change_ref, far_ref, side_ref, out_ref, out_change_ref
):
    width = body_ref.shape[1]
    rows = jnp.concatenate([far_ref[...], side_ref[...]], axis=0)
    start = 256
    span = slice(start, start + rows.shape[0])
    front, forcing = halves(left_ref[:ROWS, span]), halves(left_ref[ROWS:, span])
    for at in range(0, width, WIDTH):
        span = slice(at, at + WIDTH)
        out_ref[:, span] = body_ref[:, span] - dot3(front, rows[:, span])
    out_change_ref[...] = change_ref[...] + dot3(forcing, rows[:, width:])


def final_kernel(
    at_ref, left_ref, head_ref, panel_ref, body_ref, change_ref, forcing_ref, far_ref,
    front_ref, solved_ref
):
    holder, blk = at_ref[0], at_ref[1]
    width = body_ref.shape[1]
    cut = left_ref.shape[1] - far_ref.shape[0]
    front, forcing = halves(left_ref[:ROWS, cut:]), halves(left_ref[ROWS:, cut:])
    front_ref[:, :WIDTH] = head_ref[...]
    for at in range(0, width, WIDTH):
        span = slice(at, at + WIDTH)
        value = body_ref[:, span] - dot3(front, far_ref[:, span])
        if at == 0:
            value = jnp.where(blk == 0, panel_ref[:, WIDTH:], value)
        front_ref[:, WIDTH + at : 2 * WIDTH + at] = value
    change = change_ref[...] + dot3(forcing, far_ref[:, width:])
    kept = jnp.where(holder > 0, 0.0, forcing_ref[...])
    solved_ref[...] = kept - change.T[: kept.shape[0]]


def from_first(value):
    got = {
        d: lax.ppermute(value, "blk", [(0, d)]) for d in Y_ORDER
    }
    return [got[d] for d in Y_ORDER]


def shards(front_entries, child_blocks, child_map, pivot_inverse, rhs_index, rhs_values):
    rank, x, z, c = place()
    blk = lax.axis_index("blk")
    holder = jnp.where(rank < 2, 1, jnp.where(rank < 4, 2, 0))
    start = (rank & 1) * ROWS
    matrix, kept_rows, rest = assemble(front_entries, child_blocks, child_map)

    corner_first = (blk == 0) & ((z == 0) | (z > 4))
    sent = scatter_x(matrix)
    across_x = forcing_x(forcing_core(rhs_index, rhs_values))

    quarter = jnp.where(x == 0, kept_rows, sent[0] + sent[1] + sent[2])
    sent = scatter_z(quarter)
    kept, came = forcing_rows(*across_x)
    sent, quarter, kept, came = lax.optimization_barrier((sent, quarter, kept, came))

    share = jnp.where(z < 2, quarter[:8], sent[0] + sent[1] + sent[2])
    head, mine, ours, back, matrix = gather_z(share, kept, came, corner_first, rest(share))

    count, width = mine.shape
    excites = ours.shape[1]
    block, forcing = local(
        tail_kernel,
        (c,),
        (mine, swap_core(mine), ours, back, group_order()),
        ((2 * count, width + ROWS), ours.shape[1:]),
    )
    late, block = lax.optimization_barrier((head, block))
    head = [
        head,
        *(cube_send(late, lambda i, j, k: (i + d, j, k)) for d in (1, -1)),
        cube_send(head, lambda i, j, k: (i + 2, j, k)),
    ]
    side = cube_send(block, lambda i, j, k: (i + sign(k), j, k))

    ids, ids_of_head = tail_ids(), head_ids()
    other = swap_core(jnp.concatenate(head))
    panel, factors, head = local(
        factors_kernel,
        (holder, start, blk),
        (matrix[:, : 2 * WIDTH], pivot_inverse, ids_of_head, *head, other),
        ((ROWS, 2 * WIDTH), (ROWS, 2 * WIDTH), (2 * WIDTH, WIDTH)),
        flops=4 * 10**9,
    )
    side, panel = lax.optimization_barrier((side, panel))
    far = cube_send(side[:count], lambda i, j, k: (i + sign(k), j, k))
    turned_left, head_out = local(
        left_kernel,
        (holder, start, blk),
        (factors, *from_first(factors), pivot_inverse, ids, ids_of_head, head)
        + (matrix[:, :WIDTH], panel[:, :WIDTH]),
        ((2 * ROWS, 2 * WIDTH), (ROWS, WIDTH)),
        flops=5 * 10**9,
    )
    shapes = ((ROWS, width), (ROWS, ROWS))
    body, change = local(
        first_kernel, (0,), (turned_left, matrix, block, side), shapes, flops=10**10
    )
    body, change = local(
        second_kernel, (0,), (turned_left, body, change, far, swap_core(side)), shapes, flops=10**9
    )
    front, solved = local(
        final_kernel,
        (holder, blk),
        (turned_left, head_out, panel, body, change, forcing, swap_core(far)),
        (matrix.shape, forcing.shape),
        flops=10**9,
    )
    return front, solved


def solution(mesh):
    in_specs = (P("cube", "blk"), P("cube", "blk"), P(), P(), P("cube"), P("blk", "cube"))
    out_specs = (P("cube", "blk"), P("blk", "cube"))
    return jax.shard_map(shards, mesh=mesh, in_specs=in_specs, out_specs=out_specs, check_vma=False)
```

```python
import jax
import jax.numpy as jnp
import numpy as np
from jax import lax
from jax.experimental import pallas as pl
from jax.experimental.pallas import tpu as pltpu
from jax.sharding import PartitionSpec as P

NX, NZ, NC, NY = 4, 8, 2, 4
ROWS = 128
WIDTH = 256
X_ORDER = (3, 2, 1)
Z_ORDER = (3, 2, 1)
Y_ORDER = (3, 1, 2)
HIGH = lax.Precision.HIGHEST


def dot(left, right):
    return jnp.dot(left, right, precision=HIGH, preferred_element_type=jnp.float32)


def after(value, *others):
    return lax.optimization_barrier((value, others))[0]


def cube_send(value, target):
    pairs = []
    for x in range(NX):
        for z in range(NZ):
            for c in range(NC):
                to = target(x, z, c)
                if to is not None:
                    tx, tz, tc = to
                    pairs.append(
                        ((x * NZ + z) * NC + c, ((tx % NX) * NZ + tz % NZ) * NC + tc % NC)
                    )
    return lax.ppermute(value, "cube", pairs)


def swap_core(value):
    return cube_send(value, lambda x, z, c: (x, z, 1 - c))


def place():
    rank = lax.axis_index("cube")
    return rank, rank >> 4, rank >> 1 & 7, rank & 1


def sign(core):
    return 1 - 2 * core


def local(kernel, place_scalars, arrays, shapes, flops=10**6):
    size = sum(4 * int(np.prod(shape)) for shape in shapes)
    return pl.pallas_call(
        kernel,
        out_shape=[jax.ShapeDtypeStruct(shape, jnp.float32) for shape in shapes],
        in_specs=[pl.BlockSpec(memory_space=pltpu.SMEM)]
        + [pl.BlockSpec(memory_space=pltpu.VMEM)] * len(arrays),
        out_specs=[pl.BlockSpec(memory_space=pltpu.VMEM)] * len(shapes),
        compiler_params=pltpu.CompilerParams(vmem_limit_bytes=40 * 2**20),
        cost_estimate=pl.CostEstimate(flops=flops, bytes_accessed=2 * size, transcendentals=0),
    )(jnp.stack([jnp.asarray(v, jnp.int32) for v in place_scalars]), *arrays)


def split(values):
    high = values.astype(jnp.bfloat16)
    rest = values - high.astype(jnp.float32)
    middle = rest.astype(jnp.bfloat16)
    return high, middle, (rest - middle.astype(jnp.float32)).astype(jnp.bfloat16)


def add_children(at_ref, front_ref, child_ref, came_ref, rows_ref, cols_ref, out_ref):
    parity, row_base, col_base = at_ref[0], at_ref[1], at_ref[2]
    count, width = came_ref.shape
    kept = child_ref[pl.ds(pl.multiple_of(parity * count, count), count), :]
    came = came_ref[...]
    even = parity == 0
    children = [jnp.where(even, kept, came), jnp.where(even, came, kept)]
    children = [jnp.concatenate(split(child), axis=0) for child in children]
    spots = lax.broadcasted_iota(jnp.int32, (ROWS, ROWS), 0) + row_base
    row_table = jnp.where(spots == rows_ref[...], 1.0, 0.0).astype(jnp.bfloat16)
    targets = lax.broadcasted_iota(jnp.int32, (2 * ROWS, ROWS), 0) + col_base
    for b in range(width // ROWS):
        span = slice(b * ROWS, (b + 1) * ROWS)
        out_span = slice(2 * b * ROWS, 2 * (b + 1) * ROWS)
        placed = []
        for k, child in enumerate(children):
            table = jnp.where(targets + 2 * b * ROWS == cols_ref[k : k + 1, span], 1.0, 0.0)
            parts = lax.dot_general(
                child[:, span],
                table.astype(jnp.bfloat16),
                (((1,), (1,)), ((), ())),
                preferred_element_type=jnp.float32,
            )
            placed.append(parts[:count] + (parts[count : 2 * count] + parts[2 * count :]))
        parts = jnp.concatenate(split(jnp.concatenate(placed, axis=0)), axis=1)
        sums = jnp.dot(row_table, parts, preferred_element_type=jnp.float32)
        size = 2 * ROWS
        sums = sums[:, :size] + (sums[:, size : 2 * size] + sums[:, 2 * size :])
        out_ref[:, out_span] = front_ref[:, out_span] + sums


def assemble_kernel(at_ref, *refs):
    *given, out_ref, kept_ref = refs

    @pl.when(at_ref[1] < NC * NC * ROWS)
    def _():
        add_children(at_ref, *given, out_ref)
        kept_ref[...] = out_ref[: kept_ref.shape[0]]


def assemble_rest_kernel(at_ref, *refs):
    *given, first_ref, out_ref = refs
    holder = at_ref[1] < NC * NC * ROWS

    @pl.when(holder)
    def _():
        out_ref[...] = first_ref[...]

    @pl.when(jnp.logical_not(holder))
    def _():
        add_children(at_ref, *given, out_ref)


def assemble(front_entries, child_blocks, child_map):
    rows_dev, front_cols = front_entries.shape
    child_cols = child_blocks.shape[1]
    half_rows = rows_dev // 2
    rank, _, _, parity = place()
    blk = lax.axis_index("blk")
    sent_rows = lax.dynamic_slice_in_dim(child_blocks, (1 - parity) * half_rows, half_rows)
    child_start = (rank >> 1) * rows_dev + parity * half_rows
    rows = lax.dynamic_slice(child_map, (0, child_start), (2, half_rows)).reshape(1, rows_dev)
    cols = lax.dynamic_slice(child_map, (0, blk * child_cols), (2, child_cols))
    scalars = (parity, rank * rows_dev, blk * front_cols)
    given = (front_entries, child_blocks, swap_core(sent_rows), rows, cols)
    shapes = (front_entries.shape,)
    quarter = (rows_dev // NX, front_cols)
    first, kept = local(assemble_kernel, scalars, given, (*shapes, quarter), flops=10**9)

    def rest(event):
        *arrays, late_rows, late_cols = given
        late = after((late_rows, late_cols), event)
        return local(
            assemble_rest_kernel, scalars, (*arrays, *late, first), shapes, flops=10**9
        )[0]

    return first, kept, rest


def dense_kernel(at_ref, index_ref, values_ref, kept_ref, sent_ref):
    x, c = at_ref[0], at_ref[1]
    s = sign(c)
    index = index_ref[...]
    values = values_ref[...]
    excites, entries = values.shape
    parts = jnp.concatenate(split(values), axis=0)
    chip = index >> 8

    def table(at, size):
        rows = lax.broadcasted_iota(jnp.int32, (size, entries), 0)
        return jnp.where(rows == at, 1.0, 0.0).astype(jnp.bfloat16)

    def summed(masks, place_table):
        rows = [parts * mask.astype(jnp.bfloat16) for mask in masks]
        placed = lax.dot_general(
            jnp.concatenate(rows, axis=0),
            place_table,
            (((1,), (1,)), ((), ())),
            preferred_element_type=jnp.float32,
        )
        placed = placed.reshape(len(masks), 3, excites, place_table.shape[0])
        return placed[:, 0] + (placed[:, 1] + placed[:, 2])

    def mask_of(condition):
        return jnp.broadcast_to(jnp.where(condition, 1.0, 0.0), (3 * excites, entries))

    near = table(index & 255, NC * ROWS)
    pivot = table((index >> 7 & 1) * 64 + (index >> 8) * 32 + (index & 31), ROWS)

    def blocks(at):
        sums = summed([mask_of(chip == at * NZ + z) for z in range(NZ)], near)
        held = (index < 2 * WIDTH) & (index >> 5 & 3 == at)
        return sums, summed([mask_of(held)], pivot)[0]

    for ref, at in ((kept_ref, x + s & 3), (sent_ref, x - s & 3)):
        sums, group = blocks(at)
        for z in range(NZ):
            ref[2 * z] = sums[z, :, :ROWS]
            ref[2 * z + 1] = sums[z, :, ROWS:]
        ref[2 * NZ] = group
    for start, at in ((17, x + 2 & 3), (26, x)):
        sums, group = blocks(at)
        for z in range(NZ):
            first, second = sums[z, :, :ROWS], sums[z, :, ROWS:]
            kept_ref[start + z] = jnp.where(c == 0, first, second)
            sent_ref[start + z] = jnp.where(c == 0, second, first)
        kept_ref[start + NZ] = jnp.where(c == 0, group, 0.0)
        sent_ref[start + NZ] = jnp.where(c == 0, 0.0, group)


def forcing_core(rhs_index, rhs_values):
    _, x, _, c = place()
    entries = rhs_values.shape[1]
    shape = (35, rhs_values.shape[0], ROWS)
    kept, sent = local(
        dense_kernel,
        (x, c),
        (rhs_index.reshape(1, entries), rhs_values),
        (shape, shape),
        flops=10**9,
    )
    return kept + swap_core(sent)


def forcing_x(summed):
    side = cube_send(summed[:17], lambda i, j, k: (i + sign(k), j, k))
    across = cube_send(summed[17:26], lambda i, j, k: (i + 2, j, k))
    return side, across, summed[26:]


def rows_kernel(at_ref, side_ref, across_ref, own_ref, kept_ref, sent_ref):
    z, c = at_ref[0], at_ref[1]
    s = sign(c)
    for ref, sgn in ((kept_ref, s), (sent_ref, -s)):
        for n in (1, 2, 3):
            i = z + n * sgn & 7
            for k in range(NC):
                mine = own_ref[i] + across_ref[i]
                ref[2 * n - 2 + k] = side_ref[2 * i + k] + jnp.where(c == k, mine, 0.0)
    for slot, i in ((6, z + 4 & 7), (7, z)):
        kept_ref[slot] = side_ref[2 * i + c] + (own_ref[i] + across_ref[i])
        sent_ref[slot] = side_ref[2 * i + 1 - c]
    pivot = side_ref[16] + (own_ref[8] + across_ref[8])
    kept_ref[8] = pivot
    sent_ref[8] = pivot


def forcing_rows(side, across, own):
    _, _, z, c = place()
    kept, sent = local(rows_kernel, (z, c), (side, across, own), (own.shape, own.shape))
    return kept, swap_core(sent)


def scatter_x(block):
    return [
        cube_send(
            block[32 * d : 32 * d + 32],
            lambda i, j, k: (d, j, k) if i == 0 and j < 2 else None,
        )
        for d in X_ORDER
    ]


def scatter_z(quarter):
    return [
        cube_send(
            quarter[8 * d : 8 * d + 8],
            lambda i, j, k: (i, (-d if j == 0 else 1 + d), k) if j < 2 else None,
        )
        for d in range(1, NZ // 2)
    ]


def message_kernel(at_ref, share_ref, other_ref, kept_ref, came_ref, *out_refs):
    c, turn = at_ref[0], at_ref[1]
    low = c == 0
    width = share_ref.shape[1]

    def columns(ref):
        left, right = ref[:, :WIDTH], ref[:, WIDTH : 2 * WIDTH]
        yield 0, jnp.where(turn == 1, right, left)
        yield WIDTH, jnp.where(turn == 1, left, right)
        yield 2 * WIDTH, ref[:, 2 * WIDTH :]

    summed = [kept_ref[i] + came_ref[i] for i in range(9)]
    for (at, mine), (_, other) in zip(columns(share_ref), columns(other_ref)):
        span = slice(at, at + mine.shape[1])
        for ref in out_refs[:3]:
            ref[:8, span] = jnp.where(low, mine, other)
            ref[8:, span] = jnp.where(low, other, mine)
        out_refs[3][:, span] = mine
    for n, ref in enumerate(out_refs[:3]):
        for i, block in enumerate((summed[2 * n], summed[2 * n + 1], summed[8])):
            ref[:, width + i * ROWS : width + (i + 1) * ROWS] = block
    first = jnp.where(low, summed[8], 0.0)
    out_refs[2][:, width + 3 * ROWS :] = summed[6]
    for i, block in enumerate((summed[6][:8], summed[6][8:], first[:8], first[8:])):
        out_refs[3][:, width + i * ROWS : width + (i + 1) * ROWS] = block
    out_refs[4][0] = summed[7]
    out_refs[4][1] = first


def unpack_kernel(
    at_ref, own_ref, up_ref, down_ref, three_ref, two_ref, one_ref, left_ref, *out_refs
):
    low = at_ref[0] == 0
    head_ref, tail_ref, mine_ref, back_ref = out_refs
    width = WIDTH + tail_ref.shape[1]
    row = 0
    far_rows = jnp.where(low, up_ref[...], down_ref[...])
    for rows in (own_ref, one_ref, two_ref, three_ref, far_rows):
        count = rows.shape[0]
        head_ref[row : row + count] = rows[:, :WIDTH]
        tail_ref[row : row + count] = rows[:, WIDTH:width]
        row += count
    spans = [slice(width + i * ROWS, width + (i + 1) * ROWS) for i in range(4)]
    sums = [one_ref[:, at] + two_ref[:, at] + three_ref[:, at] for at in spans[:3]]
    far = [far_rows[:, at] for at in spans]
    mine_ref[0] = (
        jnp.where(low, sums[0], sums[1])
        + jnp.concatenate([far[0], far[1]], axis=0)
        + left_ref[0]
    )
    pivot = sums[2] + jnp.concatenate([far[2], far[3]], axis=0) + left_ref[1]
    mine_ref[1] = pivot
    back_ref[0] = jnp.where(low, sums[1], sums[0])
    back_ref[1] = pivot


def gather_z(share, kept, came, corner_first, beside):
    c = lax.axis_index("cube") & 1
    width = share.shape[1]
    excites = kept.shape[1]
    near = (2 * excites // 2, width + 3 * ROWS)
    *messages, left = local(
        message_kernel,
        (c, corner_first),
        (share, swap_core(share), kept, came),
        (near, near, (near[0], near[1] + ROWS), (8, width + 4 * ROWS), (2, excites, ROWS)),
    )
    got = {
        n: cube_send(messages[n - 1], lambda i, j, k: (i, j + n * sign(k), k)) for n in Z_ORDER
    }
    up = cube_send(messages[3], lambda i, j, k: (i, j + 4, k) if k == 0 else None)
    extra = got[3][:, near[1] :]
    down = jnp.concatenate(
        [got[3][8:, :width], extra[:8], extra[8:], jnp.zeros((8, 2 * ROWS), jnp.float32)], axis=1
    )
    down = cube_send(down, lambda i, j, k: (i, j - 1, k) if k == 1 else None)
    up, down, got, beside = lax.optimization_barrier((up, down, got, beside))
    head, tail, mine, back = local(
        unpack_kernel,
        (c,),
        (messages[3], up, down, got[3], got[2], got[1], left),
        ((64, WIDTH), (64, width - WIDTH), (2, excites, ROWS), (2, excites, ROWS)),
    )
    return head, tail, mine, swap_core(back), beside


def tail_kernel(at_ref, mine_ref, theirs_ref, ours_ref, back_ref, order_ref, *out_refs):
    all_ref, forcing_ref = out_refs
    count, width = mine_ref.shape
    forcing_ref[...] = ours_ref[0] + back_ref[0]
    pivots = ours_ref[1] + back_ref[1]
    excites = pivots.shape[0]
    spots = lax.broadcasted_iota(jnp.int32, (ROWS, ROWS), 0)
    table = jnp.where(spots == order_ref[...], 1.0, 0.0)
    ordered = dot(pivots, table)
    filler = jnp.zeros((ROWS - excites, ROWS), jnp.float32)
    columns = jnp.concatenate([ordered, filler], axis=0).T
    all_ref[:count, :width] = mine_ref[...]
    all_ref[count:, :width] = theirs_ref[...]
    all_ref[:, width:] = columns


def rows_8(dx, dz, core):
    return [(*dx, *dz, core, r) for r in range(8)]


def rows_64(dx, flip):
    s = -1 if flip else 1
    out = rows_8(dx, (0, 0), 2 + flip)
    for n in (1, 2, 3):
        out += rows_8(dx, (-n * s, 0), 0) + rows_8(dx, (-n * s, 0), 1)
    return out + rows_8(dx, (0, 4), 2 + flip)


def rows_128(dx, flip):
    return rows_64(dx, flip) + rows_64(dx, 1 - flip)


def row_ids(rows):
    _, x, z, c = place()
    s = sign(c)
    xs, x0, zs, z0, core, r = (np.array(v, np.int32)[None] for v in zip(*rows))
    at_x = x + xs * s + x0 & 3
    at_z = z + zs * s + z0 & 7
    core = jnp.where(core > 1, c ^ (core - 2), core)
    lower = (at_z == 0) | (at_z > 4)
    pos = jnp.where(lower, 8 - at_z & 7, at_z - 1)
    return (jnp.where(lower, 0, NC) + core) * ROWS + at_x * 32 + pos * 8 + r


def head_ids():
    return row_ids(
        sum((rows_64((0, dx), flip) for flip in range(NC) for dx in (0, -1, 1, 2)), [])
    )


def tail_ids():
    return row_ids(
        rows_128((0, 0), 0)
        + rows_128((-1, 0), 0)
        + rows_64((0, 2), 0)
        + rows_128((1, 0), 1)
        + rows_64((0, 2), 1)
    )


def group_order():
    ids = row_ids(rows_128((0, 0), 0))
    return (ids >> 7 & 1) * 64 + (ids >> 8) * 32 + (ids & 31)


def spread(values, ids, first):
    count, width = values.shape
    rows = lax.broadcasted_iota(jnp.int32, (width, ids.shape[1]), 0) + first
    table = jnp.where(rows == ids, 1.0, 0.0).astype(jnp.bfloat16)
    parts = jnp.dot(
        jnp.concatenate(split(values), axis=0), table, preferred_element_type=jnp.float32
    )
    return parts[:count] + (parts[count : 2 * count] + parts[2 * count :])


def factors_kernel(
    at_ref, panel_ref, pivots_ref, ids_ref, a_ref, b_ref, c_ref, d_ref, other_ref,
    out_ref, factors_ref, head_ref
):
    holder, start = at_ref[0], at_ref[1]
    two = holder == 2
    row = 0
    for ref in (a_ref, b_ref, c_ref, d_ref, other_ref):
        head_ref[row : row + ref.shape[0]] = ref[...]
        row += ref.shape[0]

    @pl.when(at_ref[2] == 0)
    def _():
        head = head_ref[...]
        ids = ids_ref[...]
        left, right = panel_ref[:, :WIDTH], panel_ref[:, WIDTH:]
        first, second = pivots_ref[0], pivots_ref[1]
        l1 = dot(left, first)
        reduced = right - dot(spread(l1, ids, 0), head)
        l2 = dot(reduced, second)
        lead = jnp.where(two, pivots_ref[1, pl.ds(pl.multiple_of(start, ROWS), ROWS), :], l2)
        back = dot(dot(spread(lead, ids, WIDTH), head), first)
        out_ref[:, :WIDTH] = jnp.where(holder == 1, left, l1)
        out_ref[:, WIDTH:] = jnp.where(holder == 1, right, jnp.where(two, reduced, l2))
        factors_ref[:, :WIDTH] = jnp.where(two, l1, l1 - back)
        factors_ref[:, WIDTH:] = jnp.where(two, back, l2)


def left_kernel(
    at_ref, own_ref, three_ref, one_ref, two_ref, pivots_ref, ids_ref, head_ids_ref, head_ref,
    matrix_ref, panel_ref, turned_ref, out_ref
):
    holder, start, blk = at_ref[0], at_ref[1], at_ref[2]
    one, two = holder == 1, holder == 2
    factors = own_ref[...]
    for d, ref in enumerate((one_ref, two_ref, three_ref)):
        factors = jnp.where(blk == d + 1, ref[...], factors)
    first, second = factors[:, :WIDTH], factors[:, WIDTH:]
    start = pl.multiple_of(start, ROWS)
    pick_one = pivots_ref[0, pl.ds(start, ROWS), :]
    pick_two = pivots_ref[1, pl.ds(start, ROWS), :]
    front = jnp.where(one, 0.0, first), jnp.where(holder > 0, 0.0, second)
    forcing = (
        jnp.where(one, -pick_one, jnp.where(two, second, first)),
        jnp.where(one, 0.0, jnp.where(two, -pick_two, second)),
    )
    ids = ids_ref[...]
    lead = jnp.concatenate([front[0], forcing[0]], axis=0)
    rest = jnp.concatenate([front[1], forcing[1]], axis=0)
    turned_ref[...] = spread(lead, ids, 0) + spread(rest, ids, WIDTH)
    ids = head_ids_ref[...]
    turned = spread(front[0], ids, 0) + spread(front[1], ids, WIDTH)
    change = dot3(halves(turned), head_ref[...])
    out_ref[...] = jnp.where(blk == 0, panel_ref[...], matrix_ref[...] - change)


def halves(values):
    high = values.astype(jnp.bfloat16)
    return high, (values - high.astype(jnp.float32)).astype(jnp.bfloat16)


def dot3(left, rows):
    (high, low), (rows_high, rows_low) = left, halves(rows)
    count = high.shape[0]
    both = jnp.dot(
        jnp.concatenate([high, low], axis=0), rows_high, preferred_element_type=jnp.float32
    )
    rest = jnp.dot(high, rows_low, preferred_element_type=jnp.float32)
    return both[:count] + (both[count:] + rest)


def first_kernel(at_ref, left_ref, matrix_ref, block_ref, side_ref, body_ref, change_ref):
    width = body_ref.shape[1]
    rows = jnp.concatenate([block_ref[...], side_ref[...]], axis=0)
    cut = rows.shape[0]
    front, forcing = halves(left_ref[:ROWS, :cut]), halves(left_ref[ROWS:, :cut])
    for at in range(0, width, WIDTH):
        span = slice(at, at + WIDTH)
        change = dot3(front, rows[:, span])
        body_ref[:, span] = matrix_ref[:, WIDTH + at : 2 * WIDTH + at] - change
    change_ref[...] = dot3(forcing, rows[:, width:])


def second_kernel(
    at_ref, left_ref, body_ref, change_ref, far_ref, side_ref, out_ref, out_change_ref
):
    width = body_ref.shape[1]
    rows = jnp.concatenate([far_ref[...], side_ref[...]], axis=0)
    start = 256
    span = slice(start, start + rows.shape[0])
    front, forcing = halves(left_ref[:ROWS, span]), halves(left_ref[ROWS:, span])
    for at in range(0, width, WIDTH):
        span = slice(at, at + WIDTH)
        out_ref[:, span] = body_ref[:, span] - dot3(front, rows[:, span])
    out_change_ref[...] = change_ref[...] + dot3(forcing, rows[:, width:])


def final_kernel(
    at_ref, left_ref, head_ref, panel_ref, body_ref, change_ref, forcing_ref, far_ref,
    front_ref, solved_ref
):
    holder, blk = at_ref[0], at_ref[1]
    width = body_ref.shape[1]
    cut = left_ref.shape[1] - far_ref.shape[0]
    front, forcing = halves(left_ref[:ROWS, cut:]), halves(left_ref[ROWS:, cut:])
    front_ref[:, :WIDTH] = head_ref[...]
    for at in range(0, width, WIDTH):
        span = slice(at, at + WIDTH)
        value = body_ref[:, span] - dot3(front, far_ref[:, span])
        if at == 0:
            value = jnp.where(blk == 0, panel_ref[:, WIDTH:], value)
        front_ref[:, WIDTH + at : 2 * WIDTH + at] = value
    change = change_ref[...] + dot3(forcing, far_ref[:, width:])
    kept = jnp.where(holder > 0, 0.0, forcing_ref[...])
    solved_ref[...] = kept - change.T[: kept.shape[0]]


def from_first(value):
    got = {
        d: lax.ppermute(value, "blk", [(0, d)]) for d in Y_ORDER
    }
    return [got[d] for d in Y_ORDER]


def shards(front_entries, child_blocks, child_map, pivot_inverse, rhs_index, rhs_values):
    rank, x, z, c = place()
    blk = lax.axis_index("blk")
    holder = jnp.where(rank < 2, 1, jnp.where(rank < 4, 2, 0))
    start = (rank & 1) * ROWS
    matrix, kept_rows, rest = assemble(front_entries, child_blocks, child_map)

    corner_first = (blk == 0) & ((z == 0) | (z > 4))
    sent = scatter_x(matrix)
    across_x = forcing_x(forcing_core(rhs_index, rhs_values))

    quarter = jnp.where(x == 0, kept_rows, sent[0] + sent[1] + sent[2])
    sent = scatter_z(quarter)
    kept, came = forcing_rows(*across_x)
    sent, quarter, kept, came = lax.optimization_barrier((sent, quarter, kept, came))

    share = jnp.where(z < 2, quarter[:8], sent[0] + sent[1] + sent[2])
    head, mine, ours, back, matrix = gather_z(share, kept, came, corner_first, rest(share))

    count, width = mine.shape
    excites = ours.shape[1]
    block, forcing = local(
        tail_kernel,
        (c,),
        (mine, swap_core(mine), ours, back, group_order()),
        ((2 * count, width + ROWS), ours.shape[1:]),
    )
    late, block = lax.optimization_barrier((head, block))
    head = [
        head,
        *(cube_send(late, lambda i, j, k: (i + d, j, k)) for d in (1, -1)),
        cube_send(head, lambda i, j, k: (i + 2, j, k)),
    ]
    side = cube_send(block, lambda i, j, k: (i + sign(k), j, k))

    ids, ids_of_head = tail_ids(), head_ids()
    other = swap_core(jnp.concatenate(head))
    panel, factors, head = local(
        factors_kernel,
        (holder, start, blk),
        (matrix[:, : 2 * WIDTH], pivot_inverse, ids_of_head, *head, other),
        ((ROWS, 2 * WIDTH), (ROWS, 2 * WIDTH), (2 * WIDTH, WIDTH)),
        flops=4 * 10**9,
    )
    side, panel = lax.optimization_barrier((side, panel))
    far = cube_send(side[:count], lambda i, j, k: (i + sign(k), j, k))
    turned_left, head_out = local(
        left_kernel,
        (holder, start, blk),
        (factors, *from_first(factors), pivot_inverse, ids, ids_of_head, head)
        + (matrix[:, :WIDTH], panel[:, :WIDTH]),
        ((2 * ROWS, 2 * WIDTH), (ROWS, WIDTH)),
        flops=5 * 10**9,
    )
    shapes = ((ROWS, width), (ROWS, ROWS))
    body, change = local(
        first_kernel, (0,), (turned_left, matrix, block, side), shapes, flops=10**10
    )
    body, change = local(
        second_kernel, (0,), (turned_left, body, change, far, swap_core(side)), shapes, flops=10**9
    )
    front, solved = local(
        final_kernel,
        (holder, blk),
        (turned_left, head_out, panel, body, change, forcing, swap_core(far)),
        (matrix.shape, forcing.shape),
        flops=10**9,
    )
    return front, solved


def solution(mesh):
    in_specs = (P("cube", "blk"), P("cube", "blk"), P(), P(), P("cube"), P("blk", "cube"))
    out_specs = (P("cube", "blk"), P("blk", "cube"))
    return jax.shard_map(shards, mesh=mesh, in_specs=in_specs, out_specs=out_specs, check_vma=False)
```
